256 devices in a mesh: dp: 8 (over z), mp: 16 (over x, y), section: 2 (over core).
Axes of the slice: x: 4, y: 4, z: 8, core: 2. Of those that a mesh axis runs over, the one named last changes fastest.
Arguments:
- encoded: bfloat16 [8192, 6144], P(('dp', 'section'), 'mp'), may hold values from -6 to 6
- visible: int32 [32, 256], P(('dp', 'section')), may hold values from 0 to 1023, as said below
- owner: int32 [1024], replicated, may hold values from 0 to 15, as said below
- embed_weight: bfloat16 [6144, 1024], P('mp'), may hold values from -0.078125 to 0.078125
- mask_token: float32 [1024], replicated, may hold values from -4 to 4
- norm_gain: float32 [1024], replicated, may hold values from 0.5 to 1.5
- query_weight: bfloat16 [1024, 1024], replicated, may hold values from -0.1875 to 0.1875
- key_weight: bfloat16 [1024, 1024], replicated, may hold values from -0.1875 to 0.1875
- value_weight: bfloat16 [1024, 1024], replicated, may hold values from -0.1875 to 0.1875
- out_weight: bfloat16 [1024, 1024], replicated, may hold values from -0.1875 to 0.1875
- pixel_weight: bfloat16 [1024, 768], replicated, may hold values from -0.1875 to 0.1875
- targets: bfloat16 [32, 1024, 768], P(('dp', 'section'), 'mp'), may hold values from -6 to 6
Outputs:
- predicted: bfloat16 [32, 1024, 768], P(('dp', 'section'), 'mp')
- encoded_grad: bfloat16 [8192, 6144], P(('dp', 'section'), 'mp')
- embed_grad: float32 [6144, 1024], P('mp')
The draws below stay inside these ranges and needn't reach their ends.
Inputs may be any that keep to these rules, and one draw needn't show every extreme that they name: Every owner holds exactly 64 patches. `visible`: each image names 256 different patches; in each image at most 32 of them belong to one owner, exactly 32 to some owner and none to some other owner.
All inputs are finite; a program needn't handle non-finite values.
Results may differ from the reference program's by a relative error of at most 0.04.
Values may be sent and summed in bfloat16 or wider, within the bound.
A program may use at most 192 MiB of HBM per device.

```python
import jax
import jax.numpy as jnp
from jax import lax

D = 6144
E = 1024
HEADS = 16
PIX = 768
GRID = 32
VIS = 256
HEAD_DIM = 64
PATCHES = 1024
OWN = 64
IMAGES = 32
TOKENS = 8192
N_MP = 16


def owner_order(key):
    return jax.random.permutation(jax.random.fold_in(key, 101), PATCHES)


def draw_owner(key, part):
    shuffled = owner_order(key)
    per_owner = PATCHES // N_MP
    labels = (jnp.arange(PATCHES, dtype=jnp.int32) // per_owner).astype(jnp.int32)
    return jnp.zeros((PATCHES,), jnp.int32).at[shuffled].set(labels)


def draw_visible(key, part):
    shuffled = owner_order(key)
    key = jax.random.fold_in(key, 7)
    per_owner = PATCHES // N_MP
    base_count = VIS // N_MP
    half_owners = N_MP // 2
    flat_patches = shuffled.astype(jnp.int32)

    def one_image(image_key):
        key_amp, key_perm, key_rank, key_final = jax.random.split(image_key, 4)
        amplitude = jax.random.randint(key_amp, (half_owners,), 0, base_count).astype(jnp.int32)
        amplitude = amplitude.at[0].set(base_count)
        counts = jnp.concatenate([base_count + amplitude, base_count - amplitude])
        counts = counts[jax.random.permutation(key_perm, N_MP)]
        ranks = jax.vmap(lambda rank_key: jax.random.permutation(rank_key, per_owner))(jax.random.split(key_rank, N_MP))
        chosen = (ranks < counts[:, None]).reshape(-1)
        picked = jnp.argsort(jnp.where(chosen, 0, 1).astype(jnp.int32), stable=True)[:VIS]
        patch_list = flat_patches[picked]
        return patch_list[jax.random.permutation(key_final, VIS)].astype(jnp.int32)
    return jax.vmap(one_image)(jax.random.split(key, IMAGES))


def block_scale(stream_key, shape, shards, low, high):
    gain = 1.0
    for dim, blocks in shards:
        steps = jax.random.uniform(jax.random.fold_in(jax.random.fold_in(stream_key, 6), dim), (blocks,), jnp.float32, low / len(shards), high / len(shards))
        gain = gain * jnp.repeat(jnp.exp(steps), shape[dim] // blocks).reshape((-1,) + (1,) * (len(shape) - 1 - dim))
    return gain


def bell_draw(stream_key, shape, width, limit, shards=(), held_as=jnp.bfloat16):
    values = jax.random.normal(stream_key, shape, jnp.float32) * width
    if len(shards) > 0:
        values = block_scale(stream_key, shape, shards, -0.22, 0.18) * values
    return jnp.clip(values, min=-limit, max=limit).astype(held_as)


def setup_inputs(seed: int = 0) -> dict:
    key_list = jax.random.split(jax.random.key(seed), 13)
    encoded = bell_draw(key_list[0], (TOKENS, D), 1.0, 6.0, ((0, 16), (1, 16)))
    visible = draw_visible(jax.random.fold_in(key_list[12], 71), 0)
    owner = draw_owner(jax.random.fold_in(key_list[12], 71), 0)
    embed_weight = bell_draw(key_list[3], (D, E), D ** -0.5, 0.078125, ((0, 16),))
    mask_token = bell_draw(key_list[4], (E,), 1.0, 4.0, (), jnp.float32)
    norm_gain = jnp.clip(1.0 + 0.1 * jax.random.normal(key_list[5], (E,), jnp.float32), 0.5, 1.5)
    query_weight = bell_draw(key_list[6], (E, E), E ** -0.5, 0.1875)
    key_weight = bell_draw(key_list[7], (E, E), E ** -0.5, 0.1875)
    value_weight = bell_draw(key_list[8], (E, E), E ** -0.5, 0.1875)
    out_weight = bell_draw(key_list[9], (E, E), E ** -0.5, 0.1875)
    pixel_weight = bell_draw(key_list[10], (E, PIX), E ** -0.5, 0.1875)
    targets = bell_draw(key_list[11], (IMAGES, PATCHES, PIX), 1.0, 6.0, ((0, 16), (1, 16)))
    return {"encoded": encoded, "visible": visible, "owner": owner, "embed_weight": embed_weight, "mask_token": mask_token, "norm_gain": norm_gain, "query_weight": query_weight, "key_weight": key_weight, "value_weight": value_weight, "out_weight": out_weight, "pixel_weight": pixel_weight, "targets": targets}


def sincos_table(patch_index, dec_width):
    quarter = dec_width // 4
    freqs = 10000.0 ** (-jnp.arange(quarter, dtype=jnp.float32) / quarter)
    row_pos = (patch_index // GRID).astype(jnp.float32)[:, None] * freqs[None, :]
    col_pos = (patch_index % GRID).astype(jnp.float32)[:, None] * freqs[None, :]
    return jnp.concatenate([jnp.sin(row_pos), jnp.cos(row_pos), jnp.sin(col_pos), jnp.cos(col_pos)], axis=1)

def prior_count(labels, span):
    onehot = (labels[..., None] == jnp.arange(span, dtype=jnp.int32)).astype(jnp.int32)
    return lax.optimization_barrier(jnp.sum((jnp.cumsum(onehot, axis=-2) - onehot) * onehot, axis=-1)).astype(jnp.int32)

def reference(encoded, visible, owner, embed_weight, mask_token, norm_gain, query_weight, key_weight, value_weight, out_weight, pixel_weight, targets):
    place = (owner * OWN + prior_count(owner, N_MP)).astype(jnp.int32)
    order = jnp.zeros((PATCHES,), jnp.int32).at[place].set(jnp.arange(PATCHES, dtype=jnp.int32))
    positions = sincos_table(order, E)
    block_width = D // N_MP
    blocks = jnp.einsum('tjd,jde->tje', encoded.astype(jnp.float32).reshape(TOKENS, N_MP, block_width), embed_weight.astype(jnp.float32).reshape(N_MP, block_width, E))
    rounded = lax.optimization_barrier(blocks.astype(jnp.bfloat16))
    embedded = lax.optimization_barrier(jnp.sum(rounded.astype(jnp.float32), axis=1)).reshape(IMAGES, VIS, E)
    score_scale = HEAD_DIM ** (-0.5)

    def one_image(items):
        embedded_rows, shown_patches, target_px = items
        spot_ids = place[shown_patches]
        seen = jnp.zeros((PATCHES,), jnp.float32).at[spot_ids].set(1.0)
        inputs = jnp.broadcast_to(mask_token[None, :], (PATCHES, E)).astype(jnp.float32).at[spot_ids].set(embedded_rows) + positions
        average = lax.optimization_barrier(jnp.mean(inputs, axis=-1, keepdims=True))
        centered = inputs - average
        inv_std = lax.rsqrt(lax.optimization_barrier(jnp.mean(centered * centered, axis=-1, keepdims=True)) + 1e-06)
        standard = centered * inv_std
        normed = (standard * norm_gain).astype(jnp.bfloat16)
        queries = jnp.dot(normed, query_weight, preferred_element_type=jnp.float32).astype(jnp.bfloat16)
        keys = jnp.dot(normed, key_weight, preferred_element_type=jnp.float32).astype(jnp.bfloat16)
        values = jnp.dot(normed, value_weight, preferred_element_type=jnp.float32).astype(jnp.bfloat16)
        query_heads = queries.astype(jnp.float32).reshape(PATCHES, HEADS, HEAD_DIM)
        key_heads = keys.astype(jnp.float32).reshape(PATCHES, HEADS, HEAD_DIM)
        value_heads = values.astype(jnp.float32).reshape(PATCHES, HEADS, HEAD_DIM)
        scores = jnp.einsum('qhd,khd->hqk', query_heads, key_heads) * score_scale
        probs32 = jax.nn.softmax(scores, axis=-1)
        probs = probs32.astype(jnp.bfloat16).astype(jnp.float32)
        attended = jnp.einsum('hqk,khd->qhd', probs, value_heads).astype(jnp.bfloat16)
        attended_flat = attended.reshape(PATCHES, E)
        updated = inputs + jnp.dot(attended_flat, out_weight, preferred_element_type=jnp.float32)
        pixels = jnp.dot(updated.astype(jnp.bfloat16), pixel_weight, preferred_element_type=jnp.float32)
        predicted = pixels.astype(jnp.bfloat16)
        residual_px = ((pixels - target_px.astype(jnp.float32)) * (1.0 - seen)[:, None]).astype(jnp.bfloat16)
        grad_updated = jnp.dot(residual_px, pixel_weight.T, preferred_element_type=jnp.float32)
        grad_attended = jnp.dot(grad_updated.astype(jnp.bfloat16), out_weight.T, preferred_element_type=jnp.float32).astype(jnp.bfloat16)
        grad_heads = grad_attended.astype(jnp.float32).reshape(PATCHES, HEADS, HEAD_DIM)
        delta_sum = lax.optimization_barrier(jnp.sum(grad_heads * attended.astype(jnp.float32), axis=-1)).T
        grad_probs = jnp.einsum('qhd,khd->hqk', grad_heads, value_heads)
        grad_scores = (probs32 * (grad_probs - delta_sum[:, :, None]) * score_scale).astype(jnp.bfloat16).astype(jnp.float32)
        grad_queries = jnp.einsum('hqk,khd->qhd', grad_scores, key_heads).astype(jnp.bfloat16).reshape(PATCHES, E)
        grad_keys = jnp.einsum('hqk,qhd->khd', grad_scores, query_heads).astype(jnp.bfloat16).reshape(PATCHES, E)
        grad_values = jnp.einsum('hqk,qhd->khd', probs, grad_heads).astype(jnp.bfloat16).reshape(PATCHES, E)
        grad_normed = jnp.dot(grad_queries, query_weight.T, preferred_element_type=jnp.float32)
        grad_normed = grad_normed + jnp.dot(grad_keys, key_weight.T, preferred_element_type=jnp.float32)
        grad_normed = grad_normed + jnp.dot(grad_values, value_weight.T, preferred_element_type=jnp.float32)
        scaled = grad_normed * norm_gain
        grad_inputs = grad_updated + inv_std * (scaled - lax.optimization_barrier(jnp.mean(scaled, axis=-1, keepdims=True)) - standard * lax.optimization_barrier(jnp.mean(scaled * standard, axis=-1, keepdims=True)))
        returned_rows = grad_inputs[spot_ids].astype(jnp.bfloat16)
        return (predicted, returned_rows)
    predicted, returned = lax.map(one_image, (embedded, visible, targets))
    returned = returned.reshape(TOKENS, E)
    encoded_grad = jnp.dot(returned, embed_weight.T, preferred_element_type=jnp.float32).astype(jnp.bfloat16)
    embed_grad = jnp.dot(encoded.T, returned, preferred_element_type=jnp.float32) * TOKENS ** (-0.5)
    return (predicted, encoded_grad, embed_grad)
```

```python
import functools

import jax
import jax.numpy as jnp
from jax import lax
from jax.experimental import pallas as pl
from jax.experimental.pallas import tpu as pltpu
from jax.sharding import PartitionSpec as P

MESH = pl.DeviceIdType.MESH
F32 = jnp.float32
BF16 = jnp.bfloat16
GRID = 32
N = 16
NZ = 8
HD = 64


def nn(a, b):
    return lax.dot_general(a, b, (((1,), (0,)), ((), ())), preferred_element_type=F32)


def nt(a, b):
    return lax.dot_general(a, b, (((1,), (1,)), ((), ())), preferred_element_type=F32)


def tn(a, b):
    return lax.dot_general(a, b, (((0,), (0,)), ((), ())), preferred_element_type=F32)


def fiota(shape, dim):
    return lax.broadcasted_iota(jnp.int32, shape, dim).astype(F32)


def hot(cond):
    return jnp.where(cond, 1.0, 0.0).astype(BF16)


def norm(x):
    c = x - jnp.mean(x, axis=-1, keepdims=True)
    inv = lax.rsqrt(jnp.mean(c * c, axis=-1, keepdims=True) + 1e-06)
    return c * inv, inv


def rows(i, size):
    return pl.ds(pl.multiple_of(i * size, size), size)


def kernel(
    enc_h, we_h, own_r, vis_r, mask_r, gain_r, wq_h, wk_h, wv_h, wo_h, wp_h, tgt_h, trig_r,
    pred_o, encg_o, emb_o,
    enc, we, wq, wk, wv, wo, wp, tgt,
    part, rsbuf, emb, encT,
    placec, vprow, vpcol, viscol, ptab, pos, xvis, wh, tab, qkvv,
    qf, kf, v2, lse, attp, attb, attf, gsend, gall, dpack, dbuf, df, ret,
    loc, zin, zbuf, zown, zgat, half_in,
    lsem, ssem, rs_s, ag_s, at_s, g_s, d_s, ag2_s, zsend, z1_s, z2_s, csend, crecv,
):
    m = lax.axis_index("mp")
    z = lax.axis_index("dp")
    c = lax.axis_index("section")

    pairs = [(enc_h, enc), (we_h, we), (wq_h, wq), (wk_h, wk), (wv_h, wv), (wo_h, wo), (wp_h, wp), (tgt_h, tgt)]
    loads = [pltpu.make_async_copy(s, d, lsem.at[i]) for i, (s, d) in enumerate(pairs)]
    for load in loads:
        load.start()

    barrier = pltpu.get_barrier_semaphore()

    def greet_mp(j, _):
        pl.semaphore_signal(barrier, inc=1, device_id={"mp": lax.rem(m + j, N)}, device_id_type=MESH)
        return 0

    def greet_z(j, _):
        pl.semaphore_signal(barrier, inc=1, device_id={"dp": lax.rem(z + j, NZ)}, device_id_type=MESH)
        return 0

    lax.fori_loop(1, N, greet_mp, 0)
    lax.fori_loop(1, NZ, greet_z, 0)
    pl.semaphore_signal(barrier, inc=1, device_id={"section": 1 - c}, device_id_type=MESH)

    def copy_to(k, src, dst, recv):
        return pltpu.make_async_remote_copy(
            src_ref=src, dst_ref=dst, send_sem=ssem.at[k], recv_sem=recv,
            device_id={"mp": k}, device_id_type=MESH,
        )

    def wait_sends(src):
        def one(j, _):
            k = lax.rem(m + j, N)
            copy_to(k, src, src, ssem.at[k]).wait_send()
            return 0

        lax.fori_loop(1, N, one, 0)

    def wait_from(k, dst, sems):
        copy_to(k, dst, dst, sems.at[k]).wait_recv()

    loads[0].wait()
    loads[1].wait()

    def partial_block(g):
        part[rows(g, 128), :] = nn(enc[rows(g, 128), :], we[...]).astype(BF16)

    def send_part(k):
        copy_to(k, part.at[rows(k, 32)], rsbuf.at[m], rs_s.at[m]).start()

    my_group = m // 4
    partial_block(lax.rem(my_group + 1, 4))
    pl.semaphore_wait(barrier, N - 1 + NZ - 1 + 1)

    def send_group(jj, _):
        g = lax.rem(my_group + jj, 4)

        @pl.when(jj > 1)
        def _():
            partial_block(g)

        for i in range(4):
            send_part(4 * g + i)
        return 0

    lax.fori_loop(1, 4, send_group, 0)
    partial_block(my_group)
    for i in range(1, 4):
        send_part(4 * my_group + lax.rem(m + i, 4))

    key_row = own_r[...].astype(F32) * 1024.0 + fiota((1, 1024), 1)
    lane = fiota((256, 1024), 1)

    def places(i, place_row):
        s = fiota((256, 1024), 0) + (i * 256).astype(F32)
        key_col = jnp.sum(jnp.where(lane == s, key_row, 0.0), axis=1, keepdims=True)
        less = jnp.where(key_row < key_col, 1.0, 0.0)
        placec[rows(i, 256), :] = jnp.sum(less, axis=1, keepdims=True)
        more = jnp.where(key_col < key_row, 1.0, 0.0)
        return place_row + jnp.sum(more, axis=0, keepdims=True)

    place_row = lax.fori_loop(0, 4, places, jnp.zeros((1, 1024), F32))

    for b in range(2):
        vrow = vis_r[b : b + 1, :].astype(F32)
        vcol = jnp.sum(jnp.where(fiota((256, 256), 0) == fiota((256, 256), 1), vrow, 0.0), axis=1, keepdims=True)
        viscol[b * 256 : (b + 1) * 256, :] = vcol
        vpcol[b * 256 : (b + 1) * 256, :] = jnp.sum(
            jnp.where(lane == vcol, place_row, 0.0), axis=1, keepdims=True
        )
        vprow[b : b + 1, :] = jnp.sum(
            jnp.where(fiota((1024, 256), 0) == vrow, placec[...], 0.0), axis=0, keepdims=True
        )

    trig = trig_r[...]
    hi = trig.astype(BF16)
    rest = trig - hi.astype(F32)
    mid = rest.astype(BF16)
    low = (rest - mid.astype(F32)).astype(BF16)
    ptab[...] = jnp.zeros_like(ptab)
    for i, term in enumerate((hi, mid, low)):
        ptab[32 * i : 32 * i + 32, 0:512] = term
        ptab[96 + 32 * i : 128 + 32 * i, 512:1024] = term

    def positions(patch_col):
        patch = patch_col.astype(jnp.int32)
        which = lax.broadcasted_iota(jnp.int32, (patch.shape[0], 192), 1)
        want = jnp.where(which < 96, patch >> 5, patch & 31)
        return nn(hot((which & 31) == want), ptab[...])

    for i in (2, 3, 4):
        loads[i].wait()
    pair = pl.ds(pl.multiple_of((m // 2) * 128, 128), 128)
    odd = jnp.full((1024, HD), lax.rem(m, 2), jnp.int32) == 1
    for i, w in enumerate((wq, wk, wv)):
        two = w[:, pair].astype(F32)
        wh[:, i * HD : (i + 1) * HD] = jnp.where(odd, two[:, HD:], two[:, :HD]).astype(BF16)

    gain = gain_r[...]
    token = mask_r[...]

    def masked(i, _):
        s = fiota((256, 1024), 0) + (i * 256).astype(F32)
        order = jnp.sum(jnp.where(place_row == s, lane, 0.0), axis=1, keepdims=True)
        p = positions(order)
        pos[rows(i, 256), :] = p
        std, _ = norm(token + p)
        tab[rows(i, 256), :] = nn((std * gain).astype(BF16), wh[...])
        return 0

    lax.fori_loop(0, 4, masked, 0)
    encT[...] = jnp.transpose(enc[...])
    for b in range(2):
        xvis[b * 256 : (b + 1) * 256, :] = positions(viscol[b * 256 : (b + 1) * 256, :])

    mine = rows(m, 32)

    def add_part(j, total):
        k = lax.rem(m + j, N)
        wait_from(k, rsbuf.at[k], rs_s)
        return total + rsbuf[k].astype(F32)

    emb[mine, :] = lax.fori_loop(1, N, add_part, part[mine, :].astype(F32)).astype(BF16)
    wait_sends(part.at[rows(0, 32)])

    def send_emb(j, _):
        copy_to(lax.rem(m + j, N), emb.at[mine], emb.at[mine], ag_s.at[m]).start()
        return 0

    lax.fori_loop(1, N, send_emb, 0)

    def get_emb(j, _):
        k = lax.rem(m + j, N)
        wait_from(k, emb.at[rows(k, 32)], ag_s)
        return 0

    lax.fori_loop(1, N, get_emb, 0)
    wait_sends(emb.at[mine])

    def visible_rows(b, _):
        r = rows(b, 256)
        x = emb[r, :].astype(F32) + xvis[r, :]
        xvis[r, :] = x
        std, _ = norm(x)
        qkvv[r, :] = nn((std * gain).astype(BF16), wh[...]).astype(BF16)
        return 0

    lax.fori_loop(0, 2, visible_rows, 0)

    v2[...] = jnp.zeros_like(v2)

    for b in range(2):

        def place_rows(i, _, b=b):
            s = fiota((256, 256), 0) + (i * 256).astype(F32)
            put = jnp.where(vprow[b : b + 1, :] == s, 1.0, 0.0)
            seen = jnp.sum(put, axis=1, keepdims=True) > 0.0
            moved = nn(put.astype(BF16), qkvv[b * 256 : (b + 1) * 256, :])
            full = jnp.where(seen, moved, tab[rows(i, 256), :]).astype(BF16)
            qf[b, rows(i, 256), :] = full[:, 0:HD] * jnp.array(0.125, BF16)
            kf[b, rows(i, 256), :] = full[:, HD : 2 * HD]
            v2[b, rows(i, 256), b * HD : (b + 1) * HD] = full[:, 2 * HD :]
            return 0

        lax.fori_loop(0, 4, place_rows, 0)

    def attend(jj, _):
        g = lax.rem(my_group + jj, 4)
        r = rows(g, 256)
        total = jnp.zeros((256, 2 * HD), F32)
        for b in range(2):
            s = nt(qf[b, r, :], kf[b])
            top = jnp.max(s, axis=1, keepdims=True)
            e = jnp.exp(s - top)
            size = jnp.sum(e, axis=1, keepdims=True)
            lse[b, r, :] = top + jnp.log(size)
            total = total + nn((e * (1.0 / size)).astype(BF16), v2[b])
        attp[r, :] = total.astype(BF16)

        @pl.when(jj < 4)
        def _():
            for i in range(4):
                k = 4 * g + i
                copy_to(k, attp.at[rows(k, 64)], attb.at[m], at_s.at[m]).start()

        @pl.when(jj == 4)
        def _():
            for i in range(1, 4):
                k = 4 * g + lax.rem(m + i, 4)
                copy_to(k, attp.at[rows(k, 64)], attb.at[m], at_s.at[m]).start()

        return 0

    lax.fori_loop(1, 5, attend, 0)

    for i in (5, 6, 7):
        loads[i].wait()
    own_place = fiota((64, 256), 0) + (m * 64).astype(F32)
    own_pos = pos[rows(m, 64), :]
    seen_own, inputs = [], []
    for b in range(2):
        put = jnp.where(vprow[b : b + 1, :] == own_place, 1.0, 0.0)
        seen = jnp.sum(put, axis=1, keepdims=True) > 0.0
        moved = nn(put.astype(BF16), emb[b * 256 : (b + 1) * 256, :])
        inputs.append(jnp.where(seen, moved, token) + own_pos)
        seen_own.append(seen)
    inputs = jnp.concatenate(inputs, axis=0)

    attb[m] = attp[rows(m, 64), :]

    def get_att(j, _):
        k = lax.rem(m + j, N)
        wait_from(k, attb.at[k], at_s)
        return 0

    lax.fori_loop(1, N, get_att, 0)
    wait_sends(attp.at[rows(0, 64)])
    for h in range(N):
        for b in range(2):
            attf[b * 64 : (b + 1) * 64, h * HD : (h + 1) * HD] = attb[h, :, b * HD : (b + 1) * HD]

    updated = inputs + nn(attf[...], wo[...])
    pixels = nn(updated.astype(BF16), wp[...])
    resid = []
    for b in range(2):
        px = pixels[b * 64 : (b + 1) * 64, :]
        pred_o[b] = px.astype(BF16)
        resid.append(jnp.where(seen_own[b], 0.0, px - tgt[b].astype(F32)).astype(BF16))
    grad_up = nt(jnp.concatenate(resid, axis=0), wp[...]).astype(BF16)
    grad_att = nt(grad_up, wo[...]).astype(BF16)
    for h in range(N):
        for b in range(2):
            cut = slice(h * HD, (h + 1) * HD)
            gsend[h, :, b * HD : (b + 1) * HD] = grad_att[b * 64 : (b + 1) * 64, cut]
            gsend[h, :, (2 + b) * HD : (3 + b) * HD] = grad_up[b * 64 : (b + 1) * 64, cut]

    own64 = rows(m, 64)

    def send_grad(j, _):
        k = lax.rem(m + j, N)
        copy_to(k, gsend.at[k], gall.at[own64], g_s.at[m]).start()
        return 0

    lax.fori_loop(1, N, send_grad, 0)
    gall[own64, :] = gsend[m]

    def get_grad(j, _):
        k = lax.rem(m + j, N)
        wait_from(k, gall.at[rows(k, 64)], g_s)
        return 0

    lax.fori_loop(1, N, get_grad, 0)
    wait_sends(gsend.at[0])

    for b in range(2):
        r = slice(b * 256, (b + 1) * 256)
        cut = slice(b * HD, (b + 1) * HD)
        kv = qkvv[r, HD : 2 * HD]
        vv = qkvv[r, 2 * HD :]
        vfull = v2[b][:, cut]

        def keys_back(i, totals, b=b, cut=cut, kv=kv, vv=vv):
            q = rows(i, 256)
            g = gall[q, cut]
            delta = jnp.sum(g.astype(F32) * attp[q, cut].astype(F32), axis=1, keepdims=True)
            p = jnp.exp(nt(qf[b, q, :], kv) - lse[b, q, :])
            ds = (p * (nt(g, vv) - delta)).astype(BF16)
            return (totals[0] + tn(ds, qf[b, q, :]), totals[1] + tn(p.astype(BF16), g))

        nil = jnp.zeros((256, HD), F32)
        dk, dv = lax.fori_loop(0, 4, keys_back, (nil, nil))

        take = hot(vpcol[r, :] == lane)
        gv = nn(take, gall[...]).astype(BF16)
        av = nn(take, attp[...])[:, cut]
        s = nt(qkvv[r, 0:HD] * jnp.array(0.125, BF16), kf[b])
        e = jnp.exp(s - jnp.max(s, axis=1, keepdims=True))
        p = e * (1.0 / jnp.sum(e, axis=1, keepdims=True))
        delta = jnp.sum(gv[:, cut].astype(F32) * av, axis=1, keepdims=True)
        ds = (p * (nt(gv[:, cut], vfull) - delta)).astype(BF16)
        dq = nn(ds, kf[b]) * 0.125
        dpack[r, 0:HD] = dq.astype(BF16)
        dpack[r, HD : 2 * HD] = dk.astype(BF16)
        dpack[r, 2 * HD : 3 * HD] = dv.astype(BF16)
        dpack[r, 3 * HD :] = gv[:, (2 + b) * HD : (3 + b) * HD]

    def send_d(j, _):
        k = lax.rem(m + j, N)
        copy_to(k, dpack.at[rows(k, 32)], dbuf.at[m], d_s.at[m]).start()
        return 0

    lax.fori_loop(1, N, send_d, 0)
    dbuf[m] = dpack[mine, :]

    std, inv = norm(xvis[mine, :])

    def get_d(j, _):
        k = lax.rem(m + j, N)
        wait_from(k, dbuf.at[k], d_s)
        return 0

    lax.fori_loop(1, N, get_d, 0)
    wait_sends(dpack.at[rows(0, 32)])
    for h in range(N):
        for t in range(4):
            df[t, :, h * HD : (h + 1) * HD] = dbuf[h, :, t * HD : (t + 1) * HD]
    scaled = (nt(df[0], wq[...]) + nt(df[1], wk[...]) + nt(df[2], wv[...])) * gain
    back = df[3].astype(F32) + inv * (
        scaled
        - jnp.mean(scaled, axis=-1, keepdims=True)
        - std * jnp.mean(scaled * std, axis=-1, keepdims=True)
    )
    ret[mine, :] = back.astype(BF16)

    def send_ret(j, _):
        copy_to(lax.rem(m + j, N), ret.at[mine], ret.at[mine], ag2_s.at[m]).start()
        return 0

    lax.fori_loop(1, N, send_ret, 0)

    def get_ret(j, _):
        k = lax.rem(m + j, N)
        wait_from(k, ret.at[rows(k, 32)], ag2_s)
        return 0

    lax.fori_loop(1, N, get_ret, 0)
    wait_sends(ret.at[mine])

    def local_grad(i, _):
        both = nn(encT[...], ret[:, rows(i, 256)]).astype(BF16)
        loc[2 * i] = both[:, 0:128]
        loc[2 * i + 1] = both[:, 128:256]
        return 0

    lax.fori_loop(0, 4, local_grad, 0)
    my_half = rows(c, 192)
    other_half = rows(1 - c, 192)

    def cross(src, dst, i):
        return pltpu.make_async_remote_copy(
            src_ref=src, dst_ref=dst, send_sem=csend.at[i], recv_sem=crecv.at[i],
            device_id={"section": 1 - c}, device_id_type=MESH,
        )

    first = cross(loc.at[:, other_half], half_in, 0)
    first.start()

    def encoder_grad(i, _):
        encg_o[rows(i, 256), :] = nt(ret[rows(i, 256), :], we[...]).astype(BF16)
        return 0

    lax.fori_loop(0, 2, encoder_grad, 0)
    first.wait()

    def add_half(i, _):
        zin[i] = (loc[i, my_half, :].astype(F32) + half_in[i].astype(F32)).astype(BF16)
        return 0

    lax.fori_loop(0, NZ, add_half, 0)

    def z_copy(k, src, dst, recv):
        return pltpu.make_async_remote_copy(
            src_ref=src, dst_ref=dst, send_sem=zsend.at[k], recv_sem=recv,
            device_id={"dp": k}, device_id_type=MESH,
        )

    def send_z(j, _):
        k = lax.rem(z + j, NZ)
        z_copy(k, zin.at[k], zbuf.at[z], z1_s.at[z]).start()
        return 0

    lax.fori_loop(1, NZ, send_z, 0)

    def add_z(j, total):
        k = lax.rem(z + j, NZ)
        z_copy(k, zbuf.at[k], zbuf.at[k], z1_s.at[k]).wait_recv()
        return total + zbuf[k].astype(F32)

    zgat[z] = lax.fori_loop(1, NZ, add_z, zin[z].astype(F32)).astype(BF16)

    def wait_z(j, _):
        k = lax.rem(z + j, NZ)
        z_copy(k, zin.at[0], zin.at[0], zsend.at[k]).wait_send()
        return 0

    lax.fori_loop(1, NZ, wait_z, 0)

    def send_z2(j, _):
        k = lax.rem(z + j, NZ)
        z_copy(k, zgat.at[z], zgat.at[z], z2_s.at[z]).start()
        return 0

    lax.fori_loop(1, NZ, send_z2, 0)

    def get_z2(j, _):
        k = lax.rem(z + j, NZ)
        z_copy(k, zgat.at[k], zgat.at[k], z2_s.at[k]).wait_recv()
        return 0

    lax.fori_loop(1, NZ, get_z2, 0)
    second = cross(zgat, zown, 1)
    second.start()
    for i in range(NZ):
        emb_o[my_half, i * 128 : (i + 1) * 128] = zgat[i]
    second.wait()
    for i in range(NZ):
        emb_o[other_half, i * 128 : (i + 1) * 128] = zown[i]
    lax.fori_loop(1, NZ, wait_z, 0)


def body(
    encoded, visible, owner, embed_weight, mask_token, norm_gain,
    query_weight, key_weight, value_weight, out_weight, pixel_weight, targets,
):
    quarter = 256
    freqs = 10000.0 ** (-jnp.arange(quarter, dtype=F32) / quarter)
    angle = jnp.arange(GRID, dtype=F32)[:, None] * freqs[None, :]
    trig = jnp.concatenate([jnp.sin(angle), jnp.cos(angle)], axis=1)
    vm = pl.BlockSpec(memory_space=pltpu.VMEM)
    hbm = pl.BlockSpec(memory_space=pl.ANY)
    V = pltpu.VMEM
    dma = pltpu.SemaphoreType.DMA
    scratch = [
        V((512, 384), BF16), V((384, 1024), BF16),
        V((1024, 1024), BF16), V((1024, 1024), BF16), V((1024, 1024), BF16), V((1024, 1024), BF16),
        V((1024, 768), BF16), V((2, 64, 768), BF16),
        V((512, 1024), BF16), V((N, 32, 1024), BF16), V((512, 1024), BF16), V((384, 512), BF16),
        V((1024, 1), F32), V((2, 256), F32), V((512, 1), F32), V((512, 1), F32), V((192, 1024), BF16),
        V((1024, 1024), F32), V((512, 1024), F32), V((1024, 192), BF16), V((1024, 192), F32), V((512, 192), BF16),
        V((2, 1024, HD), BF16), V((2, 1024, HD), BF16), V((2, 1024, 2 * HD), BF16), V((2, 1024, 1), F32),
        V((1024, 128), BF16), V((N, 64, 128), BF16), V((128, 1024), BF16),
        V((N, 64, 256), BF16), V((1024, 256), BF16), V((512, 256), BF16), V((N, 32, 256), BF16),
        V((4, 32, 1024), BF16), V((512, 1024), BF16),
        V((NZ, 384, 128), BF16), V((NZ, 192, 128), BF16), V((NZ, 192, 128), BF16),
        V((NZ, 192, 128), BF16), V((NZ, 192, 128), BF16), V((NZ, 192, 128), BF16),
        dma((8,)), dma((N,)), dma((N,)), dma((N,)), dma((N,)), dma((N,)), dma((N,)), dma((N,)),
        dma((NZ,)), dma((NZ,)), dma((NZ,)), dma((2,)), dma((2,)),
    ]
    predicted, encoded_grad, summed = pl.pallas_call(
        kernel,
        out_shape=(
            jax.ShapeDtypeStruct((2, 64, 768), BF16),
            jax.ShapeDtypeStruct((512, 384), BF16),
            jax.ShapeDtypeStruct((384, 1024), BF16),
        ),
        in_specs=[hbm, hbm, vm, vm, vm, vm, hbm, hbm, hbm, hbm, hbm, hbm, vm],
        out_specs=(vm, vm, vm),
        scratch_shapes=scratch,
        compiler_params=pltpu.CompilerParams(
            collective_id=0, has_side_effects=True, vmem_limit_bytes=58 * 1024 * 1024
        ),
        cost_estimate=pl.CostEstimate(flops=8_000_000_000, bytes_accessed=16_000_000, transcendentals=4_000_000),
    )(
        encoded, embed_weight, owner.reshape(1, 1024), visible, mask_token.reshape(1, 1024), norm_gain.reshape(1, 1024),
        query_weight, key_weight, value_weight, out_weight, pixel_weight, targets, trig,
    )
    return predicted, encoded_grad, summed.astype(F32) * 8192 ** (-0.5)


def solution(mesh):
    placed = (
        P(("dp", "section"), "mp"),
        P(("dp", "section"), None),
        P(),
        P("mp", None),
        P(),
        P(),
        P(),
        P(),
        P(),
        P(),
        P(),
        P(("dp", "section"), "mp", None),
    )
    return jax.shard_map(
        body,
        mesh=mesh,
        in_specs=placed,
        out_specs=(P(("dp", "section"), "mp", None), P(("dp", "section"), "mp"), P("mp", None)),
        check_vma=False,
    )
```

```python
import functools

import jax
import jax.numpy as jnp
from jax import lax
from jax.experimental import pallas as pl
from jax.experimental.pallas import tpu as pltpu
from jax.sharding import PartitionSpec as P

MESH = pl.DeviceIdType.MESH
F32 = jnp.float32
BF16 = jnp.bfloat16
GRID = 32
N = 16
NZ = 8
HD = 64
PIECES = 2
WIDE = 1024 // PIECES
TILES = WIDE // 128
DEEP = 192 * TILES // NZ


def nn(a, b):
    return lax.dot_general(a, b, (((1,), (0,)), ((), ())), preferred_element_type=F32)


def nt(a, b):
    return lax.dot_general(a, b, (((1,), (1,)), ((), ())), preferred_element_type=F32)


def tn(a, b):
    return lax.dot_general(a, b, (((0,), (0,)), ((), ())), preferred_element_type=F32)


def fiota(shape, dim):
    return lax.broadcasted_iota(jnp.int32, shape, dim).astype(F32)


def hot(cond):
    return jnp.where(cond, 1.0, 0.0).astype(BF16)


def norm(x):
    c = x - jnp.mean(x, axis=-1, keepdims=True)
    inv = lax.rsqrt(jnp.mean(c * c, axis=-1, keepdims=True) + 1e-06)
    return c * inv, inv


def rows(i, size):
    return pl.ds(pl.multiple_of(i * size, size), size)


def kernel(
    enc_h, we_h, own_r, vis_r, mask_r, gain_r, wq_h, wk_h, wv_h, wo_h, wp_h, tgt_h, trig_r,
    pred_o, encg_o, emb_o,
    enc, we, wq, wk, wv, wo, wp, tgt,
    part, rsbuf, emb, encT,
    placec, vprow, vpcol, viscol, seenrow, seencol, put, take, ptab, pos, xvis, wh,
    qt, kt, vt, vt2, mt, lt, acc,
    qv, kv, vv, vv2, av2, p1s, p2s, ps,
    attp, attb, attf, gasend, gusend, gaall, guall, dpack, dbuf, df, ret,
    loc, half_in, zin, zbuf, zgat, zown,
    lsem, ssem, usem, rs_s, ag_s, at_s, ga_s, gu_s, d_s, ag2send, ag2_s, zsend, z1_s, z2send, z2_s,
    csend, crecv, fsend, frecv,
):
    m = lax.axis_index("mp")
    z = lax.axis_index("dp")
    c = lax.axis_index("section")

    pairs = [(enc_h, enc), (we_h, we), (wq_h, wq), (wk_h, wk), (wv_h, wv), (wo_h, wo), (wp_h, wp), (tgt_h, tgt)]
    loads = [pltpu.make_async_copy(s, d, lsem.at[i]) for i, (s, d) in enumerate(pairs)]
    for load in loads:
        load.start()

    barrier = pltpu.get_barrier_semaphore()

    def greet_mp(j, _):
        pl.semaphore_signal(barrier, inc=1, device_id={"mp": lax.rem(m + j, N)}, device_id_type=MESH)
        return 0

    def greet_z(j, _):
        pl.semaphore_signal(barrier, inc=1, device_id={"dp": lax.rem(z + j, NZ)}, device_id_type=MESH)
        return 0

    lax.fori_loop(1, N, greet_mp, 0)
    lax.fori_loop(1, NZ, greet_z, 0)
    pl.semaphore_signal(barrier, inc=1, device_id={"section": 1 - c}, device_id_type=MESH)

    def copy_to(k, src, dst, recv, send=ssem):
        return pltpu.make_async_remote_copy(
            src_ref=src, dst_ref=dst, send_sem=send.at[k], recv_sem=recv,
            device_id={"mp": k}, device_id_type=MESH,
        )

    def each_peer(f):
        def one(j, _):
            f(lax.rem(m + j, N))
            return 0

        lax.fori_loop(1, N, one, 0)

    def each_z(f):
        def one(j, _):
            f(lax.rem(z + j, NZ))
            return 0

        lax.fori_loop(1, NZ, one, 0)

    def wait_sends(src, send=ssem):
        each_peer(lambda k: copy_to(k, src, src, send.at[k], send).wait_send())

    def wait_from(k, dst, sems):
        copy_to(k, dst, dst, sems.at[k]).wait_recv()

    loads[0].wait()
    loads[1].wait()

    def partial_block(g):
        part[rows(g, 128), :] = nn(enc[rows(g, 128), :], we[...]).astype(BF16)

    def send_part(k):
        copy_to(k, part.at[rows(k, 32)], rsbuf.at[m], rs_s.at[m]).start()

    my_group = m // 4
    partial_block(lax.rem(my_group + 1, 4))
    pl.semaphore_wait(barrier, N - 1 + NZ - 1 + 1)

    def send_group(jj, _):
        g = lax.rem(my_group + jj, 4)

        @pl.when(jj > 1)
        def _():
            partial_block(g)

        for i in range(4):
            send_part(4 * g + i)
        return 0

    lax.fori_loop(1, 4, send_group, 0)
    partial_block(my_group)
    for i in range(1, 4):
        send_part(4 * my_group + lax.rem(m + i, 4))

    key_row = own_r[...].astype(F32) * 1024.0 + fiota((1, 1024), 1)
    lane = fiota((256, 1024), 1)

    def places(i, place_row):
        s = fiota((256, 1024), 0) + (i * 256).astype(F32)
        key_col = jnp.sum(jnp.where(lane == s, key_row, 0.0), axis=1, keepdims=True)
        less = jnp.where(key_row < key_col, 1.0, 0.0)
        placec[rows(i, 256), :] = jnp.sum(less, axis=1, keepdims=True)
        more = jnp.where(key_col < key_row, 1.0, 0.0)
        return place_row + jnp.sum(more, axis=0, keepdims=True)

    place_row = lax.fori_loop(0, 4, places, jnp.zeros((1, 1024), F32))

    for b in range(2):
        r = slice(b * 256, (b + 1) * 256)
        vrow = vis_r[b : b + 1, :].astype(F32)
        vcol = jnp.sum(jnp.where(fiota((256, 256), 0) == fiota((256, 256), 1), vrow, 0.0), axis=1, keepdims=True)
        viscol[r, :] = vcol
        vpcol[r, :] = jnp.sum(jnp.where(lane == vcol, place_row, 0.0), axis=1, keepdims=True)
        vprow[b : b + 1, :] = jnp.sum(
            jnp.where(fiota((1024, 256), 0) == vrow, placec[...], 0.0), axis=0, keepdims=True
        )
        gather = jnp.where(vpcol[r, :] == lane, 1.0, 0.0)
        seenrow[b : b + 1, :] = jnp.sum(gather, axis=0, keepdims=True)
        take[r, :] = gather.astype(BF16)
        spread = jnp.where(vprow[b : b + 1, :] == fiota((1024, 256), 0), 1.0, 0.0)
        seencol[b] = jnp.sum(spread, axis=1, keepdims=True)
        put[b] = spread.astype(BF16)

    trig = trig_r[...]
    hi = trig.astype(BF16)
    rest = trig - hi.astype(F32)
    mid = rest.astype(BF16)
    low = (rest - mid.astype(F32)).astype(BF16)
    ptab[...] = jnp.zeros_like(ptab)
    for i, term in enumerate((hi, mid, low)):
        ptab[32 * i : 32 * i + 32, 0:512] = term
        ptab[96 + 32 * i : 128 + 32 * i, 512:1024] = term

    def positions(patch_col):
        patch = patch_col.astype(jnp.int32)
        which = lax.broadcasted_iota(jnp.int32, (patch.shape[0], 192), 1)
        want = jnp.where(which < 96, patch >> 5, patch & 31)
        return nn(hot((which & 31) == want), ptab[...])

    for i in (2, 3, 4):
        loads[i].wait()
    pair = pl.ds(pl.multiple_of((m // 2) * 128, 128), 128)
    odd = jnp.full((1024, HD), lax.rem(m, 2), jnp.int32) == 1
    for i, w in enumerate((wq, wk, wv)):
        two = w[:, pair].astype(F32)
        wh[:, i * HD : (i + 1) * HD] = jnp.where(odd, two[:, HD:], two[:, :HD]).astype(BF16)

    gain = gain_r[...]
    token = mask_r[...]
    scale = jnp.array(0.125, BF16)

    vt2[...] = jnp.zeros_like(vt2)
    vv2[...] = jnp.zeros_like(vv2)

    def masked(i, _):
        r = rows(i, 256)
        s = fiota((256, 1024), 0) + (i * 256).astype(F32)
        order = jnp.sum(jnp.where(place_row == s, lane, 0.0), axis=1, keepdims=True)
        p = positions(order)
        pos[r, :] = p
        std, _ = norm(token + p)
        three = nn((std * gain).astype(BF16), wh[...]).astype(BF16)
        qt[r, :] = three[:, 0:HD] * scale
        kt[r, :] = three[:, HD : 2 * HD]
        vt[r, :] = three[:, 2 * HD :]
        for b in range(2):
            vt2[b, r, b * HD : (b + 1) * HD] = three[:, 2 * HD :]
        return 0

    lax.fori_loop(0, 4, masked, 0)
    for b in range(2):
        xvis[b * 256 : (b + 1) * 256, :] = positions(viscol[b * 256 : (b + 1) * 256, :])

    mine = rows(m, 32)

    def add_part(j, total):
        k = lax.rem(m + j, N)
        wait_from(k, rsbuf.at[k], rs_s)
        return total + rsbuf[k].astype(F32)

    emb[mine, :] = lax.fori_loop(1, N, add_part, part[mine, :].astype(F32)).astype(BF16)
    wait_sends(part.at[rows(0, 32)])
    each_peer(lambda k: copy_to(k, emb.at[mine], emb.at[mine], ag_s.at[m]).start())

    def table(i, _):
        r = rows(i, 256)
        s = nt(qt[r, :], kt[...])
        total = jnp.zeros((256, 2 * HD), F32)
        for b in range(2):
            held = jnp.where(seenrow[b : b + 1, :] > 0.0, -jnp.inf, s)
            top = jnp.max(held, axis=1, keepdims=True)
            e = jnp.exp(held - top)
            mt[b, r, :] = top
            lt[b, r, :] = jnp.sum(e, axis=1, keepdims=True)
            total = total + nn(e.astype(BF16), vt2[b])
        acc[r, :] = total
        return 0

    lax.fori_loop(0, 4, table, 0)
    encT[...] = jnp.transpose(enc[...])

    each_peer(lambda k: wait_from(k, emb.at[rows(k, 32)], ag_s))
    wait_sends(emb.at[mine])

    for b in range(2):
        r = slice(b * 256, (b + 1) * 256)
        x = emb[r, :].astype(F32) + xvis[r, :]
        xvis[r, :] = x
        std, _ = norm(x)
        three = nn((std * gain).astype(BF16), wh[...]).astype(BF16)
        q, k, v = three[:, 0:HD] * scale, three[:, HD : 2 * HD], three[:, 2 * HD :]
        qv[r, :] = q
        kv[r, :] = k
        vv[r, :] = v
        vv2[b, :, b * HD : (b + 1) * HD] = v
        s1 = jnp.where(seenrow[b : b + 1, :] > 0.0, -jnp.inf, nt(q, kt[...]))
        s2 = nt(q, k)
        top = jnp.maximum(jnp.max(s1, axis=1, keepdims=True), jnp.max(s2, axis=1, keepdims=True))
        e1 = jnp.exp(s1 - top)
        e2 = jnp.exp(s2 - top)
        inv = 1.0 / (jnp.sum(e1, axis=1, keepdims=True) + jnp.sum(e2, axis=1, keepdims=True))
        p1 = e1 * inv
        p2 = e2 * inv
        p1s[b] = p1
        p2s[b] = p2
        av2[b] = (nn(p1.astype(BF16), vt2[b]) + nn(p2.astype(BF16), vv2[b])).astype(BF16)

    left = lax.broadcasted_iota(jnp.int32, (256, 2 * HD), 1) < HD

    def attend(jj, _):
        g = lax.rem(my_group + jj, 4)
        r = rows(g, 256)
        added = jnp.zeros((256, 2 * HD), F32)
        placed = jnp.zeros((256, 2 * HD), F32)
        factor = []
        for b in range(2):
            s = nt(qt[r, :], kv[b * 256 : (b + 1) * 256, :])
            old = mt[b, r, :]
            top = jnp.maximum(old, jnp.max(s, axis=1, keepdims=True))
            e = jnp.exp(s - top)
            alpha = jnp.exp(old - top)
            inv = 1.0 / (alpha * lt[b, r, :] + jnp.sum(e, axis=1, keepdims=True))
            p = e * inv
            ps[b, r, :] = p
            factor.append(alpha * inv)
            added = added + nn(p.astype(BF16), vv2[b])
            placed = placed + nn(put[b, r, :], av2[b])
        att = acc[r, :] * jnp.where(left, factor[0], factor[1]) + added
        seen = jnp.where(left, seencol[0, r, :], seencol[1, r, :]) > 0.0
        attp[r, :] = jnp.where(seen, placed, att).astype(BF16)

        @pl.when(jj < 4)
        def _():
            for i in range(4):
                k = 4 * g + i
                copy_to(k, attp.at[rows(k, 64)], attb.at[m], at_s.at[m]).start()

        @pl.when(jj == 4)
        def _():
            for i in range(1, 4):
                k = 4 * g + lax.rem(m + i, 4)
                copy_to(k, attp.at[rows(k, 64)], attb.at[m], at_s.at[m]).start()

        return 0

    lax.fori_loop(1, 5, attend, 0)

    for i in (5, 6, 7):
        loads[i].wait()
    own64 = rows(m, 64)
    own_pos = pos[own64, :]
    seen_own, inputs = [], []
    for b in range(2):
        seen = seencol[b, own64, :] > 0.0
        moved = nn(put[b, own64, :], emb[b * 256 : (b + 1) * 256, :])
        inputs.append(jnp.where(seen, moved, token) + own_pos)
        seen_own.append(seen)
    inputs = jnp.concatenate(inputs, axis=0)

    attb[m] = attp[own64, :]
    each_peer(lambda k: wait_from(k, attb.at[k], at_s))
    wait_sends(attp.at[rows(0, 64)])
    for h in range(N):
        for b in range(2):
            attf[b * 64 : (b + 1) * 64, h * HD : (h + 1) * HD] = attb[h, :, b * HD : (b + 1) * HD]

    updated = inputs + nn(attf[...], wo[...])
    pixels = nn(updated.astype(BF16), wp[...])
    resid = []
    for b in range(2):
        px = pixels[b * 64 : (b + 1) * 64, :]
        pred_o[b] = px.astype(BF16)
        resid.append(jnp.where(seen_own[b], 0.0, px - tgt[b].astype(F32)).astype(BF16))
    grad_up = nt(jnp.concatenate(resid, axis=0), wp[...]).astype(BF16)
    grad_att = nt(grad_up, wo[...]).astype(BF16)
    for h in range(N):
        cut = slice(h * HD, (h + 1) * HD)
        for b in range(2):
            gasend[h, :, b * HD : (b + 1) * HD] = grad_att[b * 64 : (b + 1) * 64, cut]
    each_peer(lambda k: copy_to(k, gasend.at[k], gaall.at[own64], ga_s.at[m]).start())
    for h in range(N):
        cut = slice(h * HD, (h + 1) * HD)
        for b in range(2):
            gusend[h, :, b * HD : (b + 1) * HD] = grad_up[b * 64 : (b + 1) * 64, cut]
    each_peer(lambda k: copy_to(k, gusend.at[k], guall.at[own64], gu_s.at[m], usem).start())
    gaall[own64, :] = gasend[m]
    guall[own64, :] = gusend[m]
    each_peer(lambda k: wait_from(k, gaall.at[rows(k, 64)], ga_s))
    wait_sends(gasend.at[0])

    for b in range(2):
        r = slice(b * 256, (b + 1) * 256)
        cut = slice(b * HD, (b + 1) * HD)

        def keys_back(i, totals, b=b, r=r, cut=cut):
            q = rows(i, 256)
            wide = jnp.where(seencol[b, q, :] > 0.0, 0.0, gaall[q, cut].astype(F32))
            g = wide.astype(BF16)
            delta = jnp.sum(wide * attp[q, cut].astype(F32), axis=1, keepdims=True)
            p = ps[b, q, :]
            ds = (p * (nt(g, vv[r, :]) - delta)).astype(BF16)
            return (totals[0] + tn(ds, qt[q, :]), totals[1] + tn(p.astype(BF16), g))

        nil = jnp.zeros((256, HD), F32)
        dk, dv = lax.fori_loop(0, 4, keys_back, (nil, nil))

        gv = nn(take[r, :], gaall[...])[:, cut]
        delta = jnp.sum(gv * av2[b].astype(F32)[:, cut], axis=1, keepdims=True)
        gv = gv.astype(BF16)
        p2 = p2s[b]
        ds1 = (p1s[b] * (nt(gv, vt[...]) - delta)).astype(BF16)
        ds2 = (p2 * (nt(gv, vv[r, :]) - delta)).astype(BF16)
        dq = (nn(ds1, kt[...]) + nn(ds2, kv[r, :])) * 0.125
        dk = dk + tn(ds2, qv[r, :])
        dv = dv + tn(p2.astype(BF16), gv)
        dpack[r, 0:HD] = dq.astype(BF16)
        dpack[r, HD : 2 * HD] = dk.astype(BF16)
        dpack[r, 2 * HD : 3 * HD] = dv.astype(BF16)

    each_peer(lambda k: wait_from(k, guall.at[rows(k, 64)], gu_s))
    wait_sends(gusend.at[0], usem)
    for b in range(2):
        r = slice(b * 256, (b + 1) * 256)
        dpack[r, 3 * HD :] = nn(take[r, :], guall[...])[:, b * HD : (b + 1) * HD].astype(BF16)

    each_peer(lambda k: copy_to(k, dpack.at[rows(k, 32)], dbuf.at[m], d_s.at[m]).start())
    dbuf[m] = dpack[mine, :]

    std, inv = norm(xvis[mine, :])
    each_peer(lambda k: wait_from(k, dbuf.at[k], d_s))
    for h in range(N):
        for t in range(4):
            df[t, :, h * HD : (h + 1) * HD] = dbuf[h, :, t * HD : (t + 1) * HD]
    scaled = (nt(df[0], wq[...]) + nt(df[1], wk[...]) + nt(df[2], wv[...])) * gain
    back = df[3].astype(F32) + inv * (
        scaled
        - jnp.mean(scaled, axis=-1, keepdims=True)
        - std * jnp.mean(scaled * std, axis=-1, keepdims=True)
    )
    for q in range(PIECES):
        ret[q, mine, :] = back[:, q * WIDE : (q + 1) * WIDE].astype(BF16)

    def ret_copy(q, k, block):
        return copy_to(k, block, block, ag2_s.at[q, m], ag2send.at[q])

    for q in range(PIECES):
        each_peer(lambda k, q=q: ret_copy(q, k, ret.at[q, mine]).start())
    wait_sends(dpack.at[rows(0, 32)])

    def cross(src, dst, send, recv):
        return pltpu.make_async_remote_copy(
            src_ref=src, dst_ref=dst, send_sem=send, recv_sem=recv,
            device_id={"section": 1 - c}, device_id_type=MESH,
        )

    def z_copy(k, src, dst, send, recv):
        return pltpu.make_async_remote_copy(
            src_ref=src, dst_ref=dst, send_sem=send, recv_sem=recv,
            device_id={"dp": k}, device_id_type=MESH,
        )

    firsts = [cross(loc.at[q, :, rows(1 - c, 192)], half_in.at[q], csend.at[q], crecv.at[q]) for q in range(PIECES)]
    for q in range(PIECES):

        def get_ret(k, q=q):
            block = ret.at[q, rows(k, 32)]
            copy_to(k, block, block, ag2_s.at[q, k], ag2send.at[q]).wait_recv()

        each_peer(get_ret)
        both = nn(encT[...], ret[q]).astype(BF16)
        for t in range(TILES):
            loc[q, t] = both[:, t * 128 : (t + 1) * 128]
        firsts[q].start()

    def scatter_z(q):
        firsts[q].wait_recv()
        for d in range(NZ):
            own_part = loc[q, d % TILES, pl.ds(pl.multiple_of(c * 192 + (d // TILES) * DEEP, DEEP), DEEP), :]
            other = half_in[q, d % TILES, (d // TILES) * DEEP : (d // TILES + 1) * DEEP, :]
            zin[q, d] = (own_part.astype(F32) + other.astype(F32)).astype(BF16)
        each_z(lambda k: z_copy(k, zin.at[q, k], zbuf.at[q, z], zsend.at[q, k], z1_s.at[q, z]).start())

    for q in range(PIECES):
        scatter_z(q)
    forward = lambda q, k: cross(zgat.at[q, k], zown.at[q, k], fsend.at[q, k], frecv.at[q, k])
    for q in range(PIECES):

        def add_z(j, total, q=q):
            k = lax.rem(z + j, NZ)
            z_copy(k, zbuf.at[q, k], zbuf.at[q, k], zsend.at[q, k], z1_s.at[q, k]).wait_recv()
            return total + zbuf[q, k].astype(F32)

        zgat[q, z] = lax.fori_loop(1, NZ, add_z, zin[q, z].astype(F32)).astype(BF16)
        each_z(lambda k, q=q: z_copy(k, zgat.at[q, z], zgat.at[q, z], z2send.at[q, k], z2_s.at[q, z]).start())
        forward(q, z).start()

    def encoder_grad(i, _):
        r = rows(i, 256)
        total = nt(ret[0, r, :], we[:, 0:WIDE])
        for q in range(1, PIECES):
            total = total + nt(ret[q, r, :], we[:, q * WIDE : (q + 1) * WIDE])
        encg_o[r, :] = total.astype(BF16)
        return 0

    lax.fori_loop(0, 2, encoder_grad, 0)

    def get_z(q, k):
        z_copy(k, zgat.at[q, k], zgat.at[q, k], z2send.at[q, k], z2_s.at[q, k]).wait_recv()
        forward(q, k).start()

    shrink = 8192 ** (-0.5)

    def write(q, core, block):
        for d in range(NZ):
            at = pl.ds(pl.multiple_of(core * 192 + (d // TILES) * DEEP, DEEP), DEEP)
            lanes = q * WIDE + (d % TILES) * 128
            emb_o[at, lanes : lanes + 128] = block[q, d].astype(F32) * shrink

    for q in range(PIECES):
        each_z(lambda k, q=q: get_z(q, k))
        write(q, c, zgat)
    for q in range(PIECES):
        for k in range(NZ):
            forward(q, k).wait_recv()
        write(q, 1 - c, zown)

    for q in range(PIECES):
        each_peer(lambda k, q=q: ret_copy(q, k, ret.at[q, mine]).wait_send())
        firsts[q].wait_send()
        each_z(lambda k, q=q: z_copy(k, zin.at[q, k], zbuf.at[q, z], zsend.at[q, k], z1_s.at[q, z]).wait_send())
        each_z(lambda k, q=q: z_copy(k, zgat.at[q, z], zgat.at[q, z], z2send.at[q, k], z2_s.at[q, z]).wait_send())
        for k in range(NZ):
            forward(q, k).wait_send()


def body(
    encoded, visible, owner, embed_weight, mask_token, norm_gain,
    query_weight, key_weight, value_weight, out_weight, pixel_weight, targets,
):
    quarter = 256
    freqs = 10000.0 ** (-jnp.arange(quarter, dtype=F32) / quarter)
    angle = jnp.arange(GRID, dtype=F32)[:, None] * freqs[None, :]
    trig = jnp.concatenate([jnp.sin(angle), jnp.cos(angle)], axis=1)
    vm = pl.BlockSpec(memory_space=pltpu.VMEM)
    hbm = pl.BlockSpec(memory_space=pl.ANY)
    V = pltpu.VMEM
    dma = pltpu.SemaphoreType.DMA
    scratch = [
        V((512, 384), BF16), V((384, 1024), BF16),
        V((1024, 1024), BF16), V((1024, 1024), BF16), V((1024, 1024), BF16), V((1024, 1024), BF16),
        V((1024, 768), BF16), V((2, 64, 768), BF16),
        V((512, 1024), BF16), V((N, 32, 1024), BF16), V((512, 1024), BF16), V((384, 512), BF16),
        V((1024, 1), F32), V((2, 256), F32), V((512, 1), F32), V((512, 1), F32), V((2, 1024), F32), V((2, 1024, 1), F32),
        V((2, 1024, 256), BF16), V((512, 1024), BF16), V((192, 1024), BF16),
        V((1024, 1024), F32), V((512, 1024), F32), V((1024, 192), BF16),
        V((1024, HD), BF16), V((1024, HD), BF16), V((1024, HD), BF16), V((2, 1024, 2 * HD), BF16),
        V((2, 1024, 1), F32), V((2, 1024, 1), F32), V((1024, 2 * HD), F32),
        V((512, HD), BF16), V((512, HD), BF16), V((512, HD), BF16), V((2, 256, 2 * HD), BF16), V((2, 256, 2 * HD), BF16),
        V((2, 256, 1024), F32), V((2, 256, 256), F32), V((2, 1024, 256), F32),
        V((1024, 128), BF16), V((N, 64, 128), BF16), V((128, 1024), BF16),
        V((N, 64, 128), BF16), V((N, 64, 128), BF16), V((1024, 128), BF16), V((1024, 128), BF16),
        V((512, 256), BF16), V((N, 32, 256), BF16), V((4, 32, 1024), BF16), V((PIECES, 512, WIDE), BF16),
        V((PIECES, TILES, 384, 128), BF16), V((PIECES, TILES, 192, 128), BF16),
        V((PIECES, NZ, DEEP, 128), BF16), V((PIECES, NZ, DEEP, 128), BF16),
        V((PIECES, NZ, DEEP, 128), BF16), V((PIECES, NZ, DEEP, 128), BF16),
        dma((8,)), dma((N,)), dma((N,)), dma((N,)), dma((N,)), dma((N,)), dma((N,)), dma((N,)), dma((N,)),
        dma((PIECES, N)), dma((PIECES, N)), dma((PIECES, NZ)), dma((PIECES, NZ)), dma((PIECES, NZ)), dma((PIECES, NZ)),
        dma((PIECES,)), dma((PIECES,)), dma((PIECES, NZ)), dma((PIECES, NZ)),
    ]
    return pl.pallas_call(
        kernel,
        out_shape=(
            jax.ShapeDtypeStruct((2, 64, 768), BF16),
            jax.ShapeDtypeStruct((512, 384), BF16),
            jax.ShapeDtypeStruct((384, 1024), F32),
        ),
        in_specs=[hbm, hbm, vm, vm, vm, vm, hbm, hbm, hbm, hbm, hbm, hbm, vm],
        out_specs=(vm, vm, vm),
        scratch_shapes=scratch,
        compiler_params=pltpu.CompilerParams(
            collective_id=0, has_side_effects=True, vmem_limit_bytes=58 * 1024 * 1024
        ),
        cost_estimate=pl.CostEstimate(flops=8_000_000_000, bytes_accessed=16_000_000, transcendentals=4_000_000),
    )(
        encoded, embed_weight, owner.reshape(1, 1024), visible, mask_token.reshape(1, 1024), norm_gain.reshape(1, 1024),
        query_weight, key_weight, value_weight, out_weight, pixel_weight, targets, trig,
    )


def solution(mesh):
    placed = (
        P(("dp", "section"), "mp"),
        P(("dp", "section"), None),
        P(),
        P("mp", None),
        P(),
        P(),
        P(),
        P(),
        P(),
        P(),
        P(),
        P(("dp", "section"), "mp", None),
    )
    return jax.shard_map(
        body,
        mesh=mesh,
        in_specs=placed,
        out_specs=(P(("dp", "section"), "mp", None), P(("dp", "section"), "mp"), P("mp", None)),
        check_vma=False,
    )
```

```python
import functools

import jax
import jax.numpy as jnp
from jax import lax
from jax.experimental import pallas as pl
from jax.experimental.pallas import tpu as pltpu
from jax.sharding import PartitionSpec as P

MESH = pl.DeviceIdType.MESH
F32 = jnp.float32
BF16 = jnp.bfloat16
GRID = 32
N = 16
NZ = 8
HD = 64
PIECES = 2
WIDE = 1024 // PIECES
TILES = WIDE // 128
DEEP = 192 * TILES // NZ


def nn(a, b):
    return lax.dot_general(a, b, (((1,), (0,)), ((), ())), preferred_element_type=F32)


def nt(a, b):
    return lax.dot_general(a, b, (((1,), (1,)), ((), ())), preferred_element_type=F32)


def tn(a, b):
    return lax.dot_general(a, b, (((0,), (0,)), ((), ())), preferred_element_type=F32)


def fiota(shape, dim):
    return lax.broadcasted_iota(jnp.int32, shape, dim).astype(F32)


def hot(cond):
    return jnp.where(cond, 1.0, 0.0).astype(BF16)


def norm(x):
    c = x - jnp.mean(x, axis=-1, keepdims=True)
    inv = lax.rsqrt(jnp.mean(c * c, axis=-1, keepdims=True) + 1e-06)
    return c * inv, inv


def lanes(i, size):
    return pl.ds(pl.multiple_of(i * size, size), size)


def loop(n, f):
    def one(i, _):
        f(i)
        return 0

    lax.fori_loop(0, n, one, 0)


def rows(i, size):
    return pl.ds(pl.multiple_of(i * size, size), size)


def kernel(
    enc_h, we_h, own_r, vis_r, mask_r, gain_r, wq_h, wk_h, wv_h, wo_h, wp_h, tgt_h, trig_r,
    pred_o, encg_o, emb_o,
    enc, we, wq, wk, wv, wo, wp, tgt,
    part, rsbuf, encT,
    placec, viscol, seenrow, seencol, put, take, ptab, pos, xown, stdo, invo, wh,
    qt, kt, vt, mt, lt, acc,
    normed, fs, qsend, qall, av, ave, p1s, p2s, ps,
    attp, attb, attf, ef, updb, resid, gub, gab, gsend, gall, dpack, dbuf, df, sc, ret,
    loc, half_in, zin, zbuf, zgat, zown,
    lsem, send_s, recv_s, ag2send, ag2_s, zsend, z1_s, z2send, z2_s, csend, crecv, fsend, frecv,
):
    m = lax.axis_index("mp")
    z = lax.axis_index("dp")
    c = lax.axis_index("section")

    pairs = [(enc_h, enc), (we_h, we), (wq_h, wq), (wk_h, wk), (wv_h, wv), (wo_h, wo), (wp_h, wp), (tgt_h, tgt)]
    loads = [pltpu.make_async_copy(s, d, lsem.at[i]) for i, (s, d) in enumerate(pairs)]
    for load in loads:
        load.start()

    barrier = pltpu.get_barrier_semaphore()

    def each_peer(f):
        def one(j, _):
            f(lax.rem(m + j, N))
            return 0

        lax.fori_loop(1, N, one, 0)

    def each_z(f):
        def one(j, _):
            f(lax.rem(z + j, NZ))
            return 0

        lax.fori_loop(1, NZ, one, 0)

    each_peer(lambda k: pl.semaphore_signal(barrier, inc=1, device_id={"mp": k}, device_id_type=MESH))
    each_z(lambda k: pl.semaphore_signal(barrier, inc=1, device_id={"dp": k}, device_id_type=MESH))
    pl.semaphore_signal(barrier, inc=1, device_id={"section": 1 - c}, device_id_type=MESH)

    def to(k, src, dst, send, recv):
        return pltpu.make_async_remote_copy(
            src_ref=src, dst_ref=dst, send_sem=send, recv_sem=recv, device_id={"mp": k}, device_id_type=MESH
        )

    other = lax.rem(m + 1, N)

    def arrived(fifteen, sem):
        to(other, fifteen, fifteen, sem, sem).wait_recv()

    def left_here(fifteen, sem):
        to(other, fifteen, fifteen, sem, sem).wait_send()

    mine = rows(m, 16)
    own64 = rows(m, 64)

    loads[0].wait()
    loads[1].wait()

    def partial_block(g):
        both = jnp.concatenate(
            [enc[rows(g, 64), :], enc[pl.ds(pl.multiple_of(256 + g * 64, 64), 64), :]], axis=0
        )
        out = nn(both, we[...]).astype(BF16)
        part[0, rows(g, 64), :] = out[:64]
        part[1, rows(g, 64), :] = out[64:]

    loop(4, partial_block)
    pl.semaphore_wait(barrier, N - 1 + NZ - 1 + 1)
    each_peer(lambda k: to(k, part.at[:, rows(k, 16)], rsbuf.at[m], send_s.at[0], recv_s.at[0]).start())

    key_row = own_r[...].astype(F32) * 1024.0 + fiota((1, 1024), 1)
    lane = fiota((256, 1024), 1)

    def places(i, place_row):
        s = fiota((256, 1024), 0) + (i * 256).astype(F32)
        key_col = jnp.sum(jnp.where(lane == s, key_row, 0.0), axis=1, keepdims=True)
        less = jnp.where(key_row < key_col, 1.0, 0.0)
        placec[rows(i, 256), :] = jnp.sum(less, axis=1, keepdims=True)
        more = jnp.where(key_col < key_row, 1.0, 0.0)
        return place_row + jnp.sum(more, axis=0, keepdims=True)

    place_row = lax.fori_loop(0, 4, places, jnp.zeros((1, 1024), F32))

    def visible_places(b):
        vrow = vis_r[b].astype(F32)
        vcol = jnp.sum(jnp.where(fiota((256, 256), 0) == fiota((256, 256), 1), vrow, 0.0), axis=1, keepdims=True)
        viscol[b] = vcol
        vpc = jnp.sum(jnp.where(lane == vcol, place_row, 0.0), axis=1, keepdims=True)
        vpr = jnp.sum(jnp.where(fiota((1024, 256), 0) == vrow, placec[...], 0.0), axis=0, keepdims=True)
        gather = jnp.where(vpc == lane, 1.0, 0.0)
        seenrow[b] = jnp.sum(gather, axis=0, keepdims=True)
        take[b] = gather.astype(BF16)
        spread = jnp.where(vpr == fiota((1024, 256), 0), 1.0, 0.0)
        seencol[b] = jnp.sum(spread, axis=1, keepdims=True)
        put[b] = spread.astype(BF16)

    loop(2, visible_places)

    trig = trig_r[...]
    hi = trig.astype(BF16)
    rest = trig - hi.astype(F32)
    mid = rest.astype(BF16)
    low = (rest - mid.astype(F32)).astype(BF16)
    ptab[...] = jnp.zeros_like(ptab)
    for i, term in enumerate((hi, mid, low)):
        ptab[32 * i : 32 * i + 32, 0:512] = term
        ptab[96 + 32 * i : 128 + 32 * i, 512:1024] = term

    def positions(patch_col):
        patch = patch_col.astype(jnp.int32)
        which = lax.broadcasted_iota(jnp.int32, (patch.shape[0], 192), 1)
        want = jnp.where(which < 96, patch >> 5, patch & 31)
        return nn(hot((which & 31) == want), ptab[...])

    for i in (2, 3, 4):
        loads[i].wait()
    pair = lanes(m // 2, 128)
    odd = jnp.full((1024, HD), lax.rem(m, 2), jnp.int32) == 1
    for i, w in enumerate((wq, wk, wv)):
        two = w[:, pair].astype(F32)
        wh[:, i * HD : (i + 1) * HD] = jnp.where(odd, two[:, HD:], two[:, :HD]).astype(BF16)

    gain = gain_r[...]
    token = mask_r[...]
    scale = jnp.array(0.125, BF16)

    def masked(i):
        r = rows(i, 256)
        s = fiota((256, 1024), 0) + (i * 256).astype(F32)
        order = jnp.sum(jnp.where(place_row == s, lane, 0.0), axis=1, keepdims=True)
        p = positions(order)
        pos[r, :] = p
        std, _ = norm(token + p)
        three = nn((std * gain).astype(BF16), wh[...]).astype(BF16)
        qt[r, :] = three[:, 0:HD] * scale
        kt[r, :] = three[:, HD : 2 * HD]
        vt[r, :] = three[:, 2 * HD :]

    loop(4, masked)
    xown[...] = positions(jnp.concatenate([viscol[0, mine, :], viscol[1, mine, :]], axis=0))

    arrived(rsbuf.at[pl.ds(0, N - 1)], recv_s.at[0])
    rsbuf[m] = part[:, mine, :]
    own_rows = lax.fori_loop(
        0, N, lambda k, total: total + rsbuf[k].astype(F32), jnp.zeros((2, 16, 1024), F32)
    ).reshape(32, 1024)
    std, inv = norm(own_rows + xown[...])
    stdo[...] = std
    invo[...] = inv
    normed[...] = (std * gain).astype(BF16)
    fs[3] = own_rows.astype(BF16)

    def project(i):
        cut = lanes(i, 256)
        fs[0, :, cut] = nn(normed[...], wq[:, cut]).astype(BF16) * scale
        fs[1, :, cut] = nn(normed[...], wk[:, cut]).astype(BF16)
        fs[2, :, cut] = nn(normed[...], wv[:, cut]).astype(BF16)

    loop(4, project)

    def pack_rows(i):
        for t in range(4):
            two = fs[t, :, lanes(i, 128)].reshape(2, 16, 128)
            qsend[2 * i, :, :, t * HD : (t + 1) * HD] = two[:, :, :HD]
            qsend[2 * i + 1, :, :, t * HD : (t + 1) * HD] = two[:, :, HD:]

    loop(N // 2, pack_rows)
    each_peer(lambda k: to(k, qsend.at[k], qall.at[:, mine], send_s.at[1], recv_s.at[1]).start())
    qall[:, mine, :] = qsend[m]

    def table(i):
        r = rows(i, 256)
        s = nt(qt[r, :], kt[...])
        for b in range(2):
            held = jnp.where(seenrow[b] > 0.0, -jnp.inf, s)
            top = jnp.max(held, axis=1, keepdims=True)
            e = jnp.exp(held - top)
            mt[b, r, :] = top
            lt[b, r, :] = jnp.sum(e, axis=1, keepdims=True)
            acc[b, r, :] = nn(e.astype(BF16), vt[...])

    loop(4, table)
    encT[...] = jnp.transpose(enc[...])

    arrived(qall.at[:, pl.ds(0, 240)], recv_s.at[1])

    my_group = m // 4

    def attention(b):
        q, k, v = (qall[b, :, t * HD : (t + 1) * HD] for t in range(3))
        s1 = jnp.where(seenrow[b] > 0.0, -jnp.inf, nt(q, kt[...]))
        s2 = nt(q, k)
        top = jnp.maximum(jnp.max(s1, axis=1, keepdims=True), jnp.max(s2, axis=1, keepdims=True))
        e1 = jnp.exp(s1 - top)
        e2 = jnp.exp(s2 - top)
        inv = 1.0 / (jnp.sum(e1, axis=1, keepdims=True) + jnp.sum(e2, axis=1, keepdims=True))
        p1 = e1 * inv
        p2 = e2 * inv
        p1s[b] = p1
        p2s[b] = p2
        a = (nn(p1.astype(BF16), vt[...]) + nn(p2.astype(BF16), v)).astype(BF16)
        av[b] = a
        ave[b, :, 0:HD] = a
        ave[b, :, HD:] = qall[b, :, 3 * HD :]

        def attend(jj, _):
            g = lax.rem(my_group + jj, 4)
            r = rows(g, 256)
            s = nt(qt[r, :], qall[b, :, HD : 2 * HD])
            old = mt[b, r, :]
            top = jnp.maximum(old, jnp.max(s, axis=1, keepdims=True))
            e = jnp.exp(s - top)
            alpha = jnp.exp(old - top)
            inv = 1.0 / (alpha * lt[b, r, :] + jnp.sum(e, axis=1, keepdims=True))
            p = e * inv
            ps[b, r, :] = p
            att = acc[b, r, :] * (alpha * inv) + nn(p.astype(BF16), qall[b, :, 2 * HD : 3 * HD])
            placed = nn(put[b, r, :], ave[b])
            att = jnp.where(seencol[b, r, :] > 0.0, placed[:, 0:HD], att)
            attp[b, r, 0:HD] = att.astype(BF16)
            attp[b, r, HD:] = placed[:, HD:].astype(BF16)

            def send(i, _):
                k = 4 * g + lax.rem(m + i, 4)
                to(k, attp.at[b, rows(k, 64)], attb.at[b, m], send_s.at[2 + b], recv_s.at[2 + b]).start()
                return 0

            lax.fori_loop(jnp.where(jj == 4, 1, 0), 4, send, 0)
            return 0

        lax.fori_loop(1, 5, attend, 0)
        attb[b, m] = attp[b, own64, :]

    loop(2, attention)

    for i in (5, 6, 7):
        loads[i].wait()

    def owner_work(b):
        arrived(attb.at[b, pl.ds(0, N - 1)], recv_s.at[2 + b])

        def unpack(i):
            one, two = attb[b, 2 * i], attb[b, 2 * i + 1]
            attf[:, lanes(i, 128)] = jnp.concatenate([one[:, :HD], two[:, :HD]], axis=1)
            ef[:, lanes(i, 128)] = jnp.concatenate([one[:, HD:], two[:, HD:]], axis=1)

        loop(N // 2, unpack)
        seen = seencol[b, own64, :] > 0.0

        def update(i):
            cut = lanes(i, 256)
            inputs = jnp.where(seen, ef[:, cut].astype(F32), mask_r[:, cut]) + pos[own64, cut]
            updb[:, cut] = (inputs + nn(attf[...], wo[:, cut])).astype(BF16)

        loop(4, update)

        def predict(i):
            cut = lanes(i, 256)
            px = nn(updb[...], wp[:, cut])
            pred_o[b, :, cut] = px.astype(BF16)
            resid[:, cut] = jnp.where(seen, 0.0, px - tgt[b, :, cut].astype(F32)).astype(BF16)

        loop(3, predict)

        def grad_updated(i):
            gub[:, lanes(i, 256)] = nt(resid[...], wp[rows(i, 256), :]).astype(BF16)

        loop(4, grad_updated)

        def grad_attended(i):
            gab[:, lanes(i, 256)] = nt(gub[...], wo[rows(i, 256), :]).astype(BF16)

        loop(4, grad_attended)

        def pack(i):
            a, u = gab[:, lanes(i, 128)], gub[:, lanes(i, 128)]
            gsend[b, 2 * i] = jnp.concatenate([a[:, :HD], u[:, :HD]], axis=1)
            gsend[b, 2 * i + 1] = jnp.concatenate([a[:, HD:], u[:, HD:]], axis=1)

        loop(N // 2, pack)
        each_peer(lambda k: to(k, gsend.at[b, k], gall.at[b, own64], send_s.at[4 + b], recv_s.at[4 + b]).start())
        gall[b, own64, :] = gsend[b, m]

    loop(2, owner_work)

    def backward(b):
        arrived(gall.at[b, pl.ds(0, 960)], recv_s.at[4 + b])
        q, k, v = (qall[b, :, t * HD : (t + 1) * HD] for t in range(3))

        def keys_back(i, totals):
            r = rows(i, 256)
            wide = jnp.where(seencol[b, r, :] > 0.0, 0.0, gall[b, r, 0:HD].astype(F32))
            g = wide.astype(BF16)
            delta = jnp.sum(wide * attp[b, r, 0:HD].astype(F32), axis=1, keepdims=True)
            p = ps[b, r, :]
            ds = (p * (nt(g, qall[b, :, 2 * HD : 3 * HD]) - delta)).astype(BF16)
            return (totals[0] + tn(ds, qt[r, :]), totals[1] + tn(p.astype(BF16), g))

        nil = jnp.zeros((256, HD), F32)
        dk, dv = lax.fori_loop(0, 4, keys_back, (nil, nil))

        both = nn(take[b], gall[b])
        gv = both[:, 0:HD]
        delta = jnp.sum(gv * av[b].astype(F32), axis=1, keepdims=True)
        gv = gv.astype(BF16)
        p2 = p2s[b]
        ds1 = (p1s[b] * (nt(gv, vt[...]) - delta)).astype(BF16)
        ds2 = (p2 * (nt(gv, v) - delta)).astype(BF16)
        dq = (nn(ds1, kt[...]) + nn(ds2, k)) * 0.125
        dk = dk + tn(ds2, q)
        dv = dv + tn(p2.astype(BF16), gv)
        dpack[b, :, 0:HD] = dq.astype(BF16)
        dpack[b, :, HD : 2 * HD] = dk.astype(BF16)
        dpack[b, :, 2 * HD : 3 * HD] = dv.astype(BF16)
        dpack[b, :, 3 * HD :] = both[:, HD:].astype(BF16)
        each_peer(lambda k: to(k, dpack.at[b, rows(k, 16)], dbuf.at[b, m], send_s.at[6 + b], recv_s.at[6 + b]).start())
        dbuf[b, m] = dpack[b, mine, :]

    loop(2, backward)

    def norm_back(b):
        arrived(dbuf.at[b, pl.ds(0, N - 1)], recv_s.at[6 + b])

        def unpack(i):
            one, two = dbuf[b, 2 * i], dbuf[b, 2 * i + 1]
            for t in range(4):
                cut = slice(t * HD, (t + 1) * HD)
                df[t, :, lanes(i, 128)] = jnp.concatenate([one[:, cut], two[:, cut]], axis=1)

        loop(N // 2, unpack)

        def back_project(i):
            r = rows(i, 256)
            cut = lanes(i, 256)
            sc[:, cut] = (nt(df[0], wq[r, :]) + nt(df[1], wk[r, :]) + nt(df[2], wv[r, :])) * gain_r[:, cut]

        loop(4, back_project)
        scaled = sc[...]
        std = stdo[rows(b, 16), :]
        back = df[3].astype(F32) + invo[rows(b, 16), :] * (
            scaled
            - jnp.mean(scaled, axis=-1, keepdims=True)
            - std * jnp.mean(scaled * std, axis=-1, keepdims=True)
        )
        for q in range(PIECES):
            ret[q, b, mine, :] = back[:, q * WIDE : (q + 1) * WIDE].astype(BF16)
        for q in range(PIECES):
            block = ret.at[q, b, mine]
            each_peer(lambda k: to(k, block, block, ag2send.at[q, b], ag2_s.at[q, b]).start())

    loop(2, norm_back)

    def cross(src, dst, send, recv):
        return pltpu.make_async_remote_copy(
            src_ref=src, dst_ref=dst, send_sem=send, recv_sem=recv,
            device_id={"section": 1 - c}, device_id_type=MESH,
        )

    def z_copy(k, src, dst, send, recv):
        return pltpu.make_async_remote_copy(
            src_ref=src, dst_ref=dst, send_sem=send, recv_sem=recv,
            device_id={"dp": k}, device_id_type=MESH,
        )

    z_other = lax.rem(z + 1, NZ)
    firsts = [cross(loc.at[q, :, rows(1 - c, 192)], half_in.at[q], csend.at[q], crecv.at[q]) for q in range(PIECES)]
    for q in range(PIECES):
        for b in range(2):
            arrived(ret.at[q, b, pl.ds(0, 240)], ag2_s.at[q, b])

        def local_grad(t, q=q):
            both = nn(encT[...], ret[q, :, :, lanes(t, 256)].reshape(512, 256)).astype(BF16)
            loc[q, 2 * t] = both[:, :128]
            loc[q, 2 * t + 1] = both[:, 128:]

        loop(WIDE // 256, local_grad)
        firsts[q].start()

    for q in range(PIECES):
        firsts[q].wait_recv()

        def both_cores(d, q=q):
            t, deep = lax.rem(d, TILES), (d // TILES) * DEEP
            own_part = loc[q, t, pl.ds(pl.multiple_of(c * 192 + deep, DEEP), DEEP), :]
            their_part = half_in[q, t, pl.ds(pl.multiple_of(deep, DEEP), DEEP), :]
            zin[q, d] = (own_part.astype(F32) + their_part.astype(F32)).astype(BF16)

        loop(NZ, both_cores)
        each_z(lambda k, q=q: z_copy(k, zin.at[q, k], zbuf.at[q, z], zsend.at[q], z1_s.at[q]).start())

    forward = lambda q, k: cross(zgat.at[q, k], zown.at[q, k], fsend.at[q, k], frecv.at[q, k])
    for q in range(PIECES):
        z_copy(z_other, zbuf.at[q, pl.ds(0, NZ - 1)], zbuf.at[q, pl.ds(0, NZ - 1)], zsend.at[q], z1_s.at[q]).wait_recv()
        zbuf[q, z] = zin[q, z]
        total = zbuf[q, 0].astype(F32)
        for k in range(1, NZ):
            total = total + zbuf[q, k].astype(F32)
        zgat[q, z] = total.astype(BF16)
        each_z(lambda k, q=q: z_copy(k, zgat.at[q, z], zgat.at[q, z], z2send.at[q], z2_s.at[q, z]).start())
        forward(q, z).start()

    def encoder_grad(b):
        total = nt(ret[0, b], we[:, 0:WIDE])
        for q in range(1, PIECES):
            total = total + nt(ret[q, b], we[:, q * WIDE : (q + 1) * WIDE])
        encg_o[rows(b, 256), :] = total.astype(BF16)

    loop(2, encoder_grad)

    def get_z(q, k):
        z_copy(k, zgat.at[q, k], zgat.at[q, k], z2send.at[q], z2_s.at[q, k]).wait_recv()
        forward(q, k).start()

    def write(q, core, block):
        for d in range(NZ):
            at = pl.ds(pl.multiple_of(core * 192 + (d // TILES) * DEEP, DEEP), DEEP)
            col = q * WIDE + (d % TILES) * 128
            emb_o[at, col : col + 128] = block[q, d]

    for q in range(PIECES):
        each_z(lambda k, q=q: get_z(q, k))
        write(q, c, zgat)
    for q in range(PIECES):
        for k in range(NZ):
            forward(q, k).wait_recv()
        write(q, 1 - c, zown)

    left_here(rsbuf.at[pl.ds(0, N - 1)], send_s.at[0])
    left_here(qsend.at[pl.ds(0, N - 1)], send_s.at[1])
    for b in range(2):
        left_here(attb.at[b, pl.ds(0, N - 1)], send_s.at[2 + b])
        left_here(gsend.at[b, pl.ds(0, N - 1)], send_s.at[4 + b])
        left_here(dbuf.at[b, pl.ds(0, N - 1)], send_s.at[6 + b])
        for q in range(PIECES):
            left_here(ret.at[q, b, pl.ds(0, 240)], ag2send.at[q, b])
    for q in range(PIECES):
        firsts[q].wait_send()
        seven = zbuf.at[q, pl.ds(0, NZ - 1)]
        z_copy(z_other, seven, seven, zsend.at[q], z1_s.at[q]).wait_send()
        z_copy(z_other, seven, seven, z2send.at[q], z1_s.at[q]).wait_send()
        for k in range(NZ):
            forward(q, k).wait_send()


def finish(pred_i, encg_i, emb_i, pred_o, encg_o, emb_o):
    pred_o[...] = pred_i[...]
    encg_o[...] = encg_i[...]
    emb_o[...] = emb_i[...].astype(F32) * 8192 ** (-0.5)


def body(
    encoded, visible, owner, embed_weight, mask_token, norm_gain,
    query_weight, key_weight, value_weight, out_weight, pixel_weight, targets,
):
    quarter = 256
    freqs = 10000.0 ** (-jnp.arange(quarter, dtype=F32) / quarter)
    angle = jnp.arange(GRID, dtype=F32)[:, None] * freqs[None, :]
    trig = jnp.concatenate([jnp.sin(angle), jnp.cos(angle)], axis=1)
    vm = pl.BlockSpec(memory_space=pltpu.VMEM)
    hbm = pl.BlockSpec(memory_space=pl.ANY)
    V = pltpu.VMEM
    dma = pltpu.SemaphoreType.DMA
    scratch = [
        V((512, 384), BF16), V((384, 1024), BF16),
        V((1024, 1024), BF16), V((1024, 1024), BF16), V((1024, 1024), BF16), V((1024, 1024), BF16),
        V((1024, 768), BF16), V((2, 64, 768), BF16),
        V((2, 256, 1024), BF16), V((N, 2, 16, 1024), BF16), V((384, 512), BF16),
        V((1024, 1), F32), V((2, 256, 1), F32), V((2, 1, 1024), F32), V((2, 1024, 1), F32),
        V((2, 1024, 256), BF16), V((2, 256, 1024), BF16), V((192, 1024), BF16),
        V((1024, 1024), F32), V((32, 1024), F32), V((32, 1024), F32), V((32, 1), F32), V((1024, 192), BF16),
        V((1024, HD), BF16), V((1024, HD), BF16), V((1024, HD), BF16),
        V((2, 1024, 1), F32), V((2, 1024, 1), F32), V((2, 1024, HD), F32),
        V((32, 1024), BF16), V((4, 32, 1024), BF16), V((N, 2, 16, 256), BF16), V((2, 256, 256), BF16), V((2, 256, HD), BF16), V((2, 256, 2 * HD), BF16),
        V((2, 256, 1024), F32), V((2, 256, 256), F32), V((2, 1024, 256), F32),
        V((2, 1024, 128), BF16), V((2, N, 64, 128), BF16), V((64, 1024), BF16), V((64, 1024), BF16),
        V((64, 1024), BF16), V((64, 768), BF16), V((64, 1024), BF16), V((64, 1024), BF16),
        V((2, N, 64, 128), BF16), V((2, 1024, 128), BF16), V((2, 256, 256), BF16), V((2, N, 16, 256), BF16),
        V((4, 16, 1024), BF16), V((16, 1024), F32), V((PIECES, 2, 256, WIDE), BF16),
        V((PIECES, TILES, 384, 128), BF16), V((PIECES, TILES, 192, 128), BF16),
        V((PIECES, NZ, DEEP, 128), BF16), V((PIECES, NZ, DEEP, 128), BF16),
        V((PIECES, NZ, DEEP, 128), BF16), V((PIECES, NZ, DEEP, 128), BF16),
        dma((8,)), dma((8,)), dma((8,)), dma((PIECES, 2)), dma((PIECES, 2)),
        dma((PIECES,)), dma((PIECES,)), dma((PIECES,)), dma((PIECES, NZ)),
        dma((PIECES,)), dma((PIECES,)), dma((PIECES, NZ)), dma((PIECES, NZ)),
    ]
    predicted, encoded_grad, summed = pl.pallas_call(
        kernel,
        out_shape=(
            jax.ShapeDtypeStruct((2, 64, 768), BF16),
            jax.ShapeDtypeStruct((512, 384), BF16),
            jax.ShapeDtypeStruct((384, 1024), BF16),
        ),
        in_specs=[hbm, hbm, vm, vm, vm, vm, hbm, hbm, hbm, hbm, hbm, hbm, vm],
        out_specs=(vm, vm, vm),
        scratch_shapes=scratch,
        compiler_params=pltpu.CompilerParams(
            collective_id=0, has_side_effects=True, vmem_limit_bytes=58 * 1024 * 1024
        ),
        cost_estimate=pl.CostEstimate(flops=8_000_000_000, bytes_accessed=16_000_000, transcendentals=4_000_000),
    )(
        encoded, embed_weight, owner.reshape(1, 1024), visible.reshape(2, 1, 256), mask_token.reshape(1, 1024), norm_gain.reshape(1, 1024),
        query_weight, key_weight, value_weight, out_weight, pixel_weight, targets, trig,
    )
    return pl.pallas_call(
        finish,
        out_shape=(
            jax.ShapeDtypeStruct((2, 64, 768), BF16),
            jax.ShapeDtypeStruct((512, 384), BF16),
            jax.ShapeDtypeStruct((384, 1024), F32),
        ),
        in_specs=[vm, vm, vm],
        out_specs=(vm, vm, vm),
        cost_estimate=pl.CostEstimate(flops=400_000, bytes_accessed=3_500_000, transcendentals=0),
    )(predicted, encoded_grad, summed)


def solution(mesh):
    placed = (
        P(("dp", "section"), "mp"),
        P(("dp", "section"), None),
        P(),
        P("mp", None),
        P(),
        P(),
        P(),
        P(),
        P(),
        P(),
        P(),
        P(("dp", "section"), "mp", None),
    )
    return jax.shard_map(
        body,
        mesh=mesh,
        in_specs=placed,
        out_specs=(P(("dp", "section"), "mp", None), P(("dp", "section"), "mp"), P("mp", None)),
        check_vma=False,
    )
```

```python
import functools

import jax
import jax.numpy as jnp
from jax import lax
from jax.experimental import pallas as pl
from jax.experimental.pallas import tpu as pltpu
from jax.sharding import PartitionSpec as P

MESH = pl.DeviceIdType.MESH
F32 = jnp.float32
BF16 = jnp.bfloat16
GRID = 32
N = 16
NZ = 8
HD = 64
OWN = 64
PIECES = 2
WIDE = 1024 // PIECES
TILES = WIDE // 128
DEEP = 192 * TILES // NZ


def nn(a, b):
    return lax.dot_general(a, b, (((1,), (0,)), ((), ())), preferred_element_type=F32)


def nt(a, b):
    return lax.dot_general(a, b, (((1,), (1,)), ((), ())), preferred_element_type=F32)


def tn(a, b):
    return lax.dot_general(a, b, (((0,), (0,)), ((), ())), preferred_element_type=F32)


def fiota(shape, dim):
    return lax.broadcasted_iota(jnp.int32, shape, dim).astype(F32)


def hot(cond):
    return jnp.where(cond, 1.0, 0.0).astype(BF16)


def norm(x):
    c = x - jnp.mean(x, axis=-1, keepdims=True)
    inv = lax.rsqrt(jnp.mean(c * c, axis=-1, keepdims=True) + 1e-06)
    return c * inv, inv


def lanes(i, size):
    if isinstance(i, int):
        return slice(i * size, (i + 1) * size)
    return pl.ds(pl.multiple_of(i * size, size), size)


def unrolled(n, f):
    for i in range(n):
        f(i)


def loop(n, f):
    def one(i, _):
        f(i)
        return 0

    lax.fori_loop(0, n, one, 0)


rows = lanes


def kernel(
    enc_h, we_h, own_r, vis_r, mask_r, gain_r, wq_h, wk_h, wv_h, wo_h, wp_h, tgt_h, trig_r,
    pred_o, encg_o, emb_o,
    enc, we, wq, wk, wv, wo, wp, tgt,
    part, rsbuf, encT,
    order, seenrow, seencol, put, take, ptab, pos, xown, stdo, invo, wh,
    qt, kt, vt, mt, lt, acc,
    normed, fs, qsend, qall, av, ave, p1s, p2s, ps,
    attp, attb, attf, ef, updb, resid, gub, gab, gsend, gall, dpack, dbuf, df, sc, ret,
    loc, half_in, zin, zbuf, zgat, zown,
    lsem, send_s, recv_s, ag2send, ag2_s, zsend, z1_s, z2send, z2_s, csend, crecv, fsend, frecv,
):
    m = lax.axis_index("mp")
    z = lax.axis_index("dp")
    c = lax.axis_index("section")

    pairs = [(enc_h, enc), (we_h, we), (wq_h, wq), (wk_h, wk), (wv_h, wv), (wo_h, wo), (wp_h, wp), (tgt_h, tgt)]
    loads = [pltpu.make_async_copy(s, d, lsem.at[i]) for i, (s, d) in enumerate(pairs)]
    for load in loads:
        load.start()

    barrier = pltpu.get_barrier_semaphore()

    def each_peer(f):
        def one(j, _):
            f(lax.rem(m + j, N))
            return 0

        lax.fori_loop(1, N, one, 0)

    def each_z(f):
        def one(j, _):
            f(lax.rem(z + j, NZ))
            return 0

        lax.fori_loop(1, NZ, one, 0)

    each_peer(lambda k: pl.semaphore_signal(barrier, inc=1, device_id={"mp": k}, device_id_type=MESH))
    each_z(lambda k: pl.semaphore_signal(barrier, inc=1, device_id={"dp": k}, device_id_type=MESH))
    pl.semaphore_signal(barrier, inc=1, device_id={"section": 1 - c}, device_id_type=MESH)

    def to(k, src, dst, send, recv):
        return pltpu.make_async_remote_copy(
            src_ref=src, dst_ref=dst, send_sem=send, recv_sem=recv, device_id={"mp": k}, device_id_type=MESH
        )

    other = lax.rem(m + 1, N)

    def arrived(fifteen, sem):
        to(other, fifteen, fifteen, sem, sem).wait_recv()

    def left_here(fifteen, sem):
        to(other, fifteen, fifteen, sem, sem).wait_send()

    mine = rows(m, 16)
    own64 = rows(m, 64)

    loads[0].wait()
    loads[1].wait()

    def partial_block(g):
        both = jnp.concatenate(
            [enc[rows(g, 64), :], enc[pl.ds(pl.multiple_of(256 + g * 64, 64), 64), :]], axis=0
        )
        out = nn(both, we[...]).astype(BF16)
        part[0, rows(g, 64), :] = out[:64]
        part[1, rows(g, 64), :] = out[64:]

    loop(4, partial_block)
    pl.semaphore_wait(barrier, N - 1 + NZ - 1 + 1)
    each_peer(lambda k: to(k, part.at[:, rows(k, 16)], rsbuf.at[m], send_s.at[0], recv_s.at[0]).start())

    owner_row = own_r[...].astype(F32)
    of_owner = jnp.where(owner_row == fiota((N, 1024), 0), 1.0, 0.0)
    before = hot(fiota((128, 128), 0) < fiota((128, 128), 1))
    carry = jnp.zeros((N, 1), F32)
    ranks = []
    for a in range(8):
        block = of_owner[:, a * 128 : (a + 1) * 128]
        prior = nn(block.astype(BF16), before) + carry
        carry = carry + jnp.sum(block, axis=1, keepdims=True)
        ranks.append(jnp.sum(prior * block, axis=0, keepdims=True))
    rank_row = jnp.concatenate(ranks, axis=1)
    patch_ids = lax.broadcasted_iota(jnp.int32, (N, 1024), 1)
    halves = jnp.concatenate(
        [of_owner * (patch_ids >> 5).astype(F32), of_owner * (patch_ids & 31).astype(F32)], axis=0
    ).astype(BF16)
    order[...] = nt(hot(rank_row == fiota((OWN, 1024), 0)), halves)

    def order_col(o):
        return jnp.sum(jnp.where(fiota((OWN, 2 * N), 1) == o, order[...], 0.0), axis=1, keepdims=True)

    lookup = jnp.concatenate(
        [owner_row[:, a * 128 : (a + 1) * 128] for a in range(8)] + [ranks[a] for a in range(8)], axis=0
    ).astype(BF16)
    eye = fiota((256, 256), 0) == fiota((256, 256), 1)
    lane = lax.broadcasted_iota(jnp.int32, (256, 128), 1)
    own_patch = []
    for b in range(2):
        vrow = vis_r[b : b + 1, :]
        found = nn(lookup, hot(lax.broadcasted_iota(jnp.int32, (128, 256), 0) == (vrow & 127)))
        part_of = lax.broadcasted_iota(jnp.int32, (8, 256), 0) == (vrow >> 7)
        vis_owner = jnp.sum(jnp.where(part_of, found[0:8], 0.0), axis=0, keepdims=True)
        vis_rank = jnp.sum(jnp.where(part_of, found[8:16], 0.0), axis=0, keepdims=True)
        by_rank = hot(vis_rank == fiota((OWN, 256), 0))
        for o in range(N):
            put[b, o * OWN : (o + 1) * OWN, :] = by_rank * hot(vis_owner == float(o))
        owner_col = jnp.sum(jnp.where(eye, vis_owner, 0.0), axis=1, keepdims=True)
        rank_col = jnp.sum(jnp.where(eye, vis_rank, 0.0), axis=1, keepdims=True)
        by_rank = hot(rank_col == (lane & 63).astype(F32))
        owner_lane = (lane >> 6).astype(F32)
        for t in range(8):
            take[b, :, t * 128 : (t + 1) * 128] = by_rank * hot(owner_col - 2.0 * t == owner_lane)
        seenrow[b] = nn(jnp.ones((N, 256), BF16), take[b])[0:1]
        seencol[b] = nn(put[b], jnp.ones((256, 128), BF16))[:, 0:1]
        mine_at = fiota((16, 256), 1) == fiota((16, 256), 0) + (m * 16).astype(F32)
        own_patch.append(jnp.sum(jnp.where(mine_at, vrow.astype(F32), 0.0), axis=1, keepdims=True))

    trig = trig_r[...]
    hi = trig.astype(BF16)
    rest = trig - hi.astype(F32)
    mid = rest.astype(BF16)
    low = (rest - mid.astype(F32)).astype(BF16)
    token = mask_r[...]
    token_hi = token.astype(BF16)
    rest = token - token_hi.astype(F32)
    token_mid = rest.astype(BF16)
    token_low = (rest - token_mid.astype(F32)).astype(BF16)
    ptab[...] = jnp.zeros_like(ptab)
    for i, term in enumerate((hi, mid, low)):
        ptab[32 * i : 32 * i + 32, 0:512] = term
        ptab[96 + 32 * i : 128 + 32 * i, 512:1024] = term
    for i, term in enumerate((token_hi, token_mid, token_low)):
        ptab[192 + 16 * i : 208 + 16 * i, :] = jnp.where(
            lax.broadcasted_iota(jnp.int32, (16, 1024), 0) == 0, term.astype(F32), 0.0
        ).astype(BF16)

    def positions(row, col, with_token):
        which = lax.broadcasted_iota(jnp.int32, (row.shape[0], 256), 1)
        want = jnp.where(which < 96, row, col)
        picked = (which & 31).astype(F32) == want
        last = (which & 15 == 0) if with_token else (which < 0)
        one = jnp.where(which < 192, jnp.where(picked, 1.0, 0.0), jnp.where(last, 1.0, 0.0))
        return nn(one.astype(BF16), ptab[...])

    for i in (2, 3, 4):
        loads[i].wait()
    pair = lanes(m // 2, 128)
    odd = jnp.full((1024, HD), lax.rem(m, 2), jnp.int32) == 1
    for i, w in enumerate((wq, wk, wv)):
        two = w[:, pair].astype(F32)
        wh[:, i * HD : (i + 1) * HD] = jnp.where(odd, two[:, HD:], two[:, :HD]).astype(BF16)

    gain = gain_r[...]
    scale = jnp.array(0.125, BF16)

    def masked(i):
        r = rows(i, 256)
        owners = [(4 * i + j).astype(F32) for j in range(4)]
        row = jnp.concatenate([order_col(o) for o in owners], axis=0)
        col = jnp.concatenate([order_col(o + N) for o in owners], axis=0)
        std, _ = norm(positions(row, col, True))
        three = nn((std * gain).astype(BF16), wh[...]).astype(BF16)
        qt[r, :] = three[:, 0:HD] * scale
        kt[r, :] = three[:, HD : 2 * HD]
        vt[r, :] = three[:, 2 * HD :]

    loop(4, masked)
    def table(i):
        r = rows(i, 256)
        s = nt(qt[r, :], kt[...])
        for b in range(2):
            held = jnp.where(seenrow[b] > 0.0, -jnp.inf, s)
            top = jnp.max(held, axis=1, keepdims=True)
            e = jnp.exp(held - top)
            mt[b, r, :] = top
            lt[b, r, :] = jnp.sum(e, axis=1, keepdims=True)
            acc[b, r, :] = nn(e.astype(BF16), vt[...])

    loop(2, table)
    ids = jnp.concatenate(own_patch, axis=0).astype(jnp.int32)
    xown[...] = positions((ids >> 5).astype(F32), (ids & 31).astype(F32), False)
    own_position = positions(order_col(m.astype(F32)), order_col((m + N).astype(F32)), False)
    pos[...] = own_position

    arrived(rsbuf.at[pl.ds(0, N - 1)], recv_s.at[0])
    rsbuf[m] = part[:, mine, :]
    own_rows = lax.fori_loop(
        0, N, lambda k, total: total + rsbuf[k].astype(F32), jnp.zeros((2, 16, 1024), F32)
    ).reshape(32, 1024)
    std, inv = norm(own_rows + xown[...])
    stdo[...] = std
    invo[...] = inv
    normed[...] = (std * gain).astype(BF16)
    fs[3] = own_rows.astype(BF16)

    def project(i):
        cut = lanes(i, 256)
        fs[0, :, cut] = nn(normed[...], wq[:, cut]).astype(BF16) * scale
        fs[1, :, cut] = nn(normed[...], wk[:, cut]).astype(BF16)
        fs[2, :, cut] = nn(normed[...], wv[:, cut]).astype(BF16)

    unrolled(4, project)

    def pack_rows(i):
        for t in range(4):
            two = fs[t, :, lanes(i, 128)].reshape(2, 16, 128)
            qsend[2 * i, :, :, t * HD : (t + 1) * HD] = two[:, :, :HD]
            qsend[2 * i + 1, :, :, t * HD : (t + 1) * HD] = two[:, :, HD:]

    unrolled(N // 2, pack_rows)
    each_peer(lambda k: to(k, qsend.at[k], qall.at[:, mine], send_s.at[1], recv_s.at[1]).start())
    qall[:, mine, :] = qsend[m]

    lax.fori_loop(2, 4, lambda i, _: (table(i), 0)[1], 0)
    encT[...] = jnp.transpose(enc[...])

    arrived(qall.at[:, pl.ds(0, 240)], recv_s.at[1])

    my_group = m // 4

    def attention(b):
        q, k, v = (qall[b, :, t * HD : (t + 1) * HD] for t in range(3))
        s1 = jnp.where(seenrow[b] > 0.0, -jnp.inf, nt(q, kt[...]))
        s2 = nt(q, k)
        top = jnp.maximum(jnp.max(s1, axis=1, keepdims=True), jnp.max(s2, axis=1, keepdims=True))
        e1 = jnp.exp(s1 - top)
        e2 = jnp.exp(s2 - top)
        inv = 1.0 / (jnp.sum(e1, axis=1, keepdims=True) + jnp.sum(e2, axis=1, keepdims=True))
        p1 = e1 * inv
        p2 = e2 * inv
        p1s[b] = p1
        p2s[b] = p2
        a = (nn(p1.astype(BF16), vt[...]) + nn(p2.astype(BF16), v)).astype(BF16)
        av[b] = a
        ave[b, :, 0:HD] = a
        ave[b, :, HD:] = qall[b, :, 3 * HD :]

        def attend(jj, _):
            g = lax.rem(my_group + jj, 4)
            r = rows(g, 256)
            s = nt(qt[r, :], qall[b, :, HD : 2 * HD])
            old = mt[b, r, :]
            top = jnp.maximum(old, jnp.max(s, axis=1, keepdims=True))
            e = jnp.exp(s - top)
            alpha = jnp.exp(old - top)
            inv = 1.0 / (alpha * lt[b, r, :] + jnp.sum(e, axis=1, keepdims=True))
            p = e * inv
            ps[b, r, :] = p
            att = acc[b, r, :] * (alpha * inv) + nn(p.astype(BF16), qall[b, :, 2 * HD : 3 * HD])
            placed = nn(put[b, r, :], ave[b])
            att = jnp.where(seencol[b, r, :] > 0.0, placed[:, 0:HD], att)
            attp[b, r, 0:HD] = att.astype(BF16)
            attp[b, r, HD:] = placed[:, HD:].astype(BF16)

            def send(i, _):
                k = 4 * g + lax.rem(m + i, 4)
                to(k, attp.at[b, rows(k, 64)], attb.at[b, m], send_s.at[2 + b], recv_s.at[2 + b]).start()
                return 0

            lax.fori_loop(jnp.where(jj == 4, 1, 0), 4, send, 0)
            return 0

        lax.fori_loop(1, 5, attend, 0)
        attb[b, m] = attp[b, own64, :]

    unrolled(2, attention)

    for i in (5, 6, 7):
        loads[i].wait()

    def owner_work(b):
        arrived(attb.at[b, pl.ds(0, N - 1)], recv_s.at[2 + b])

        def unpack(i):
            one, two = attb[b, 2 * i], attb[b, 2 * i + 1]
            attf[:, lanes(i, 128)] = jnp.concatenate([one[:, :HD], two[:, :HD]], axis=1)
            ef[:, lanes(i, 128)] = jnp.concatenate([one[:, HD:], two[:, HD:]], axis=1)

        unrolled(N // 2, unpack)
        seen = seencol[b, own64, :] > 0.0

        def update(i):
            cut = lanes(i, 256)
            inputs = jnp.where(seen, ef[:, cut].astype(F32), mask_r[:, cut]) + pos[:, cut]
            updb[:, cut] = (inputs + nn(attf[...], wo[:, cut])).astype(BF16)

        unrolled(4, update)

        def predict(i):
            cut = lanes(i, 256)
            px = nn(updb[...], wp[:, cut])
            pred_o[b, :, cut] = px.astype(BF16)
            resid[:, cut] = jnp.where(seen, 0.0, px - tgt[b, :, cut].astype(F32)).astype(BF16)

        unrolled(3, predict)

        def grad_updated(i):
            gub[:, lanes(i, 256)] = nt(resid[...], wp[rows(i, 256), :]).astype(BF16)

        unrolled(4, grad_updated)

        def grad_attended(i):
            gab[:, lanes(i, 256)] = nt(gub[...], wo[rows(i, 256), :]).astype(BF16)

        unrolled(4, grad_attended)

        def pack(i):
            a, u = gab[:, lanes(i, 128)], gub[:, lanes(i, 128)]
            gsend[b, 2 * i] = jnp.concatenate([a[:, :HD], u[:, :HD]], axis=1)
            gsend[b, 2 * i + 1] = jnp.concatenate([a[:, HD:], u[:, HD:]], axis=1)

        unrolled(N // 2, pack)
        each_peer(lambda k: to(k, gsend.at[b, k], gall.at[b, own64], send_s.at[4 + b], recv_s.at[4 + b]).start())
        gall[b, own64, :] = gsend[b, m]

    unrolled(2, owner_work)

    def backward(b):
        arrived(gall.at[b, pl.ds(0, 960)], recv_s.at[4 + b])
        q, k, v = (qall[b, :, t * HD : (t + 1) * HD] for t in range(3))

        def keys_back(i, totals):
            r = rows(i, 256)
            wide = jnp.where(seencol[b, r, :] > 0.0, 0.0, gall[b, r, 0:HD].astype(F32))
            g = wide.astype(BF16)
            delta = jnp.sum(wide * attp[b, r, 0:HD].astype(F32), axis=1, keepdims=True)
            p = ps[b, r, :]
            ds = (p * (nt(g, qall[b, :, 2 * HD : 3 * HD]) - delta)).astype(BF16)
            return (totals[0] + tn(ds, qt[r, :]), totals[1] + tn(p.astype(BF16), g))

        nil = jnp.zeros((256, HD), F32)
        dk, dv = lax.fori_loop(0, 4, keys_back, (nil, nil))

        both = nn(take[b], gall[b])
        gv = both[:, 0:HD]
        delta = jnp.sum(gv * av[b].astype(F32), axis=1, keepdims=True)
        gv = gv.astype(BF16)
        p2 = p2s[b]
        ds1 = (p1s[b] * (nt(gv, vt[...]) - delta)).astype(BF16)
        ds2 = (p2 * (nt(gv, v) - delta)).astype(BF16)
        dq = (nn(ds1, kt[...]) + nn(ds2, k)) * 0.125
        dk = dk + tn(ds2, q)
        dv = dv + tn(p2.astype(BF16), gv)
        dpack[b, :, 0:HD] = dq.astype(BF16)
        dpack[b, :, HD : 2 * HD] = dk.astype(BF16)
        dpack[b, :, 2 * HD : 3 * HD] = dv.astype(BF16)
        dpack[b, :, 3 * HD :] = both[:, HD:].astype(BF16)
        each_peer(lambda k: to(k, dpack.at[b, rows(k, 16)], dbuf.at[b, m], send_s.at[6 + b], recv_s.at[6 + b]).start())
        dbuf[b, m] = dpack[b, mine, :]

    unrolled(2, backward)

    def norm_back(b):
        arrived(dbuf.at[b, pl.ds(0, N - 1)], recv_s.at[6 + b])

        def unpack(i):
            one, two = dbuf[b, 2 * i], dbuf[b, 2 * i + 1]
            for t in range(4):
                cut = slice(t * HD, (t + 1) * HD)
                df[t, :, lanes(i, 128)] = jnp.concatenate([one[:, cut], two[:, cut]], axis=1)

        unrolled(N // 2, unpack)

        def back_project(i):
            r = rows(i, 256)
            cut = lanes(i, 256)
            sc[:, cut] = (nt(df[0], wq[r, :]) + nt(df[1], wk[r, :]) + nt(df[2], wv[r, :])) * gain_r[:, cut]

        unrolled(4, back_project)
        scaled = sc[...]
        std = stdo[rows(b, 16), :]
        back = df[3].astype(F32) + invo[rows(b, 16), :] * (
            scaled
            - jnp.mean(scaled, axis=-1, keepdims=True)
            - std * jnp.mean(scaled * std, axis=-1, keepdims=True)
        )
        for q in range(PIECES):
            ret[q, b, mine, :] = back[:, q * WIDE : (q + 1) * WIDE].astype(BF16)
        for q in range(PIECES):
            block = ret.at[q, b, mine]
            each_peer(lambda k: to(k, block, block, ag2send.at[q, b], ag2_s.at[q, b]).start())

    unrolled(2, norm_back)

    def cross(src, dst, send, recv):
        return pltpu.make_async_remote_copy(
            src_ref=src, dst_ref=dst, send_sem=send, recv_sem=recv,
            device_id={"section": 1 - c}, device_id_type=MESH,
        )

    def z_copy(k, src, dst, send, recv):
        return pltpu.make_async_remote_copy(
            src_ref=src, dst_ref=dst, send_sem=send, recv_sem=recv,
            device_id={"dp": k}, device_id_type=MESH,
        )

    z_other = lax.rem(z + 1, NZ)
    firsts = [cross(loc.at[q, :, rows(1 - c, 192)], half_in.at[q], csend.at[q], crecv.at[q]) for q in range(PIECES)]
    for q in range(PIECES):
        for b in range(2):
            arrived(ret.at[q, b, pl.ds(0, 240)], ag2_s.at[q, b])

        def local_grad(t, q=q):
            both = nn(encT[...], ret[q, :, :, lanes(t, 256)].reshape(512, 256)).astype(BF16)
            loc[q, 2 * t] = both[:, :128]
            loc[q, 2 * t + 1] = both[:, 128:]

        unrolled(WIDE // 256, local_grad)
        firsts[q].start()

    for q in range(PIECES):
        firsts[q].wait_recv()

        def both_cores(d, q=q):
            t, deep = d % TILES, (d // TILES) * DEEP
            own_part = loc[q, t, pl.ds(pl.multiple_of(c * 192 + deep, DEEP), DEEP), :]
            their_part = half_in[q, t, deep : deep + DEEP, :]
            zin[q, d] = (own_part.astype(F32) + their_part.astype(F32)).astype(BF16)

        unrolled(NZ, both_cores)
        each_z(lambda k, q=q: z_copy(k, zin.at[q, k], zbuf.at[q, z], zsend.at[q], z1_s.at[q]).start())

    forward = lambda q, k: cross(zgat.at[q, k], zown.at[q, k], fsend.at[q, k], frecv.at[q, k])
    for q in range(PIECES):
        z_copy(z_other, zbuf.at[q, pl.ds(0, NZ - 1)], zbuf.at[q, pl.ds(0, NZ - 1)], zsend.at[q], z1_s.at[q]).wait_recv()
        zbuf[q, z] = zin[q, z]
        total = zbuf[q, 0].astype(F32)
        for k in range(1, NZ):
            total = total + zbuf[q, k].astype(F32)
        zgat[q, z] = total.astype(BF16)
        each_z(lambda k, q=q: z_copy(k, zgat.at[q, z], zgat.at[q, z], z2send.at[q], z2_s.at[q, z]).start())
        forward(q, z).start()

    def encoder_grad(b):
        total = nt(ret[0, b], we[:, 0:WIDE])
        for q in range(1, PIECES):
            total = total + nt(ret[q, b], we[:, q * WIDE : (q + 1) * WIDE])
        encg_o[rows(b, 256), :] = total.astype(BF16)

    unrolled(2, encoder_grad)

    def get_z(q, k):
        z_copy(k, zgat.at[q, k], zgat.at[q, k], z2send.at[q], z2_s.at[q, k]).wait_recv()
        forward(q, k).start()

    def write(q, core, block):
        for d in range(NZ):
            at = pl.ds(pl.multiple_of(core * 192 + (d // TILES) * DEEP, DEEP), DEEP)
            col = q * WIDE + (d % TILES) * 128
            emb_o[at, col : col + 128] = block[q, d]

    for q in range(PIECES):
        each_z(lambda k, q=q: get_z(q, k))
        write(q, c, zgat)
    for q in range(PIECES):
        for k in range(NZ):
            forward(q, k).wait_recv()
        write(q, 1 - c, zown)

    left_here(rsbuf.at[pl.ds(0, N - 1)], send_s.at[0])
    left_here(qsend.at[pl.ds(0, N - 1)], send_s.at[1])
    for b in range(2):
        left_here(attb.at[b, pl.ds(0, N - 1)], send_s.at[2 + b])
        left_here(gsend.at[b, pl.ds(0, N - 1)], send_s.at[4 + b])
        left_here(dbuf.at[b, pl.ds(0, N - 1)], send_s.at[6 + b])
        for q in range(PIECES):
            left_here(ret.at[q, b, pl.ds(0, 240)], ag2send.at[q, b])
    for q in range(PIECES):
        firsts[q].wait_send()
        seven = zbuf.at[q, pl.ds(0, NZ - 1)]
        z_copy(z_other, seven, seven, zsend.at[q], z1_s.at[q]).wait_send()
        z_copy(z_other, seven, seven, z2send.at[q], z1_s.at[q]).wait_send()
        for k in range(NZ):
            forward(q, k).wait_send()


def finish(pred_i, encg_i, emb_i, pred_o, encg_o, emb_o):
    pred_o[...] = pred_i[...]
    encg_o[...] = encg_i[...]
    emb_o[...] = emb_i[...].astype(F32) * 8192 ** (-0.5)


def body(
    encoded, visible, owner, embed_weight, mask_token, norm_gain,
    query_weight, key_weight, value_weight, out_weight, pixel_weight, targets,
):
    quarter = 256
    freqs = 10000.0 ** (-jnp.arange(quarter, dtype=F32) / quarter)
    angle = jnp.arange(GRID, dtype=F32)[:, None] * freqs[None, :]
    trig = jnp.concatenate([jnp.sin(angle), jnp.cos(angle)], axis=1)
    vm = pl.BlockSpec(memory_space=pltpu.VMEM)
    hbm = pl.BlockSpec(memory_space=pl.ANY)
    V = pltpu.VMEM
    dma = pltpu.SemaphoreType.DMA
    scratch = [
        V((512, 384), BF16), V((384, 1024), BF16),
        V((1024, 1024), BF16), V((1024, 1024), BF16), V((1024, 1024), BF16), V((1024, 1024), BF16),
        V((1024, 768), BF16), V((2, 64, 768), BF16),
        V((2, 256, 1024), BF16), V((N, 2, 16, 1024), BF16), V((384, 512), BF16),
        V((OWN, 2 * N), F32), V((2, 1, 1024), F32), V((2, 1024, 1), F32),
        V((2, 1024, 256), BF16), V((2, 256, 1024), BF16), V((256, 1024), BF16),
        V((OWN, 1024), F32), V((32, 1024), F32), V((32, 1024), F32), V((32, 1), F32), V((1024, 192), BF16),
        V((1024, HD), BF16), V((1024, HD), BF16), V((1024, HD), BF16),
        V((2, 1024, 1), F32), V((2, 1024, 1), F32), V((2, 1024, HD), F32),
        V((32, 1024), BF16), V((4, 32, 1024), BF16), V((N, 2, 16, 256), BF16), V((2, 256, 256), BF16), V((2, 256, HD), BF16), V((2, 256, 2 * HD), BF16),
        V((2, 256, 1024), F32), V((2, 256, 256), F32), V((2, 1024, 256), F32),
        V((2, 1024, 128), BF16), V((2, N, 64, 128), BF16), V((64, 1024), BF16), V((64, 1024), BF16),
        V((64, 1024), BF16), V((64, 768), BF16), V((64, 1024), BF16), V((64, 1024), BF16),
        V((2, N, 64, 128), BF16), V((2, 1024, 128), BF16), V((2, 256, 256), BF16), V((2, N, 16, 256), BF16),
        V((4, 16, 1024), BF16), V((16, 1024), F32), V((PIECES, 2, 256, WIDE), BF16),
        V((PIECES, TILES, 384, 128), BF16), V((PIECES, TILES, 192, 128), BF16),
        V((PIECES, NZ, DEEP, 128), BF16), V((PIECES, NZ, DEEP, 128), BF16),
        V((PIECES, NZ, DEEP, 128), BF16), V((PIECES, NZ, DEEP, 128), BF16),
        dma((8,)), dma((8,)), dma((8,)), dma((PIECES, 2)), dma((PIECES, 2)),
        dma((PIECES,)), dma((PIECES,)), dma((PIECES,)), dma((PIECES, NZ)),
        dma((PIECES,)), dma((PIECES,)), dma((PIECES, NZ)), dma((PIECES, NZ)),
    ]
    predicted, encoded_grad, summed = pl.pallas_call(
        kernel,
        out_shape=(
            jax.ShapeDtypeStruct((2, 64, 768), BF16),
            jax.ShapeDtypeStruct((512, 384), BF16),
            jax.ShapeDtypeStruct((384, 1024), BF16),
        ),
        in_specs=[hbm, hbm, vm, vm, vm, vm, hbm, hbm, hbm, hbm, hbm, hbm, vm],
        out_specs=(vm, vm, vm),
        scratch_shapes=scratch,
        compiler_params=pltpu.CompilerParams(
            collective_id=0, has_side_effects=True, vmem_limit_bytes=58 * 1024 * 1024
        ),
        cost_estimate=pl.CostEstimate(flops=8_000_000_000, bytes_accessed=16_000_000, transcendentals=4_000_000),
    )(
        encoded, embed_weight, owner.reshape(1, 1024), visible, mask_token.reshape(1, 1024), norm_gain.reshape(1, 1024),
        query_weight, key_weight, value_weight, out_weight, pixel_weight, targets, trig,
    )
    return pl.pallas_call(
        finish,
        out_shape=(
            jax.ShapeDtypeStruct((2, 64, 768), BF16),
            jax.ShapeDtypeStruct((512, 384), BF16),
            jax.ShapeDtypeStruct((384, 1024), F32),
        ),
        in_specs=[vm, vm, vm],
        out_specs=(vm, vm, vm),
        cost_estimate=pl.CostEstimate(flops=400_000, bytes_accessed=3_500_000, transcendentals=0),
    )(predicted, encoded_grad, summed)


def solution(mesh):
    placed = (
        P(("dp", "section"), "mp"),
        P(("dp", "section"), None),
        P(),
        P("mp", None),
        P(),
        P(),
        P(),
        P(),
        P(),
        P(),
        P(),
        P(("dp", "section"), "mp", None),
    )
    return jax.shard_map(
        body,
        mesh=mesh,
        in_specs=placed,
        out_specs=(P(("dp", "section"), "mp", None), P(("dp", "section"), "mp"), P("mp", None)),
        check_vma=False,
    )
```

```python
import functools

import jax
import jax.numpy as jnp
from jax import lax
from jax.experimental import pallas as pl
from jax.experimental.pallas import tpu as pltpu
from jax.sharding import PartitionSpec as P

MESH = pl.DeviceIdType.MESH
F32 = jnp.float32
BF16 = jnp.bfloat16
GRID = 32
N = 16
NZ = 8
HD = 64
OWN = 64
PIECES = 2
WIDE = 1024 // PIECES
TILES = WIDE // 128
DEEP = 192 * TILES // NZ


def nn(a, b):
    return lax.dot_general(a, b, (((1,), (0,)), ((), ())), preferred_element_type=F32)


def nt(a, b):
    return lax.dot_general(a, b, (((1,), (1,)), ((), ())), preferred_element_type=F32)


def tn(a, b):
    return lax.dot_general(a, b, (((0,), (0,)), ((), ())), preferred_element_type=F32)


def fiota(shape, dim):
    return lax.broadcasted_iota(jnp.int32, shape, dim).astype(F32)


def hot(cond):
    return jnp.where(cond, 1.0, 0.0).astype(BF16)


def norm(x):
    c = x - jnp.mean(x, axis=-1, keepdims=True)
    inv = lax.rsqrt(jnp.mean(c * c, axis=-1, keepdims=True) + 1e-06)
    return c * inv, inv


def lanes(i, size):
    if isinstance(i, int):
        return slice(i * size, (i + 1) * size)
    return pl.ds(pl.multiple_of(i * size, size), size)


def unrolled(n, f):
    for i in range(n):
        f(i)


def loop(n, f):
    def one(i, _):
        f(i)
        return 0

    lax.fori_loop(0, n, one, 0)


rows = lanes


def kernel(
    enc_h, we_h, own_r, vis_r, mask_r, gain_r, wq_h, wk_h, wv_h, wo_h, wp_h, tgt_h, trig_r,
    pred_o, encg_o, emb_o,
    enc, we, wq, wk, wv, wo, wp, tgt,
    part, rsbuf, encT,
    order, seenrow, seencol, put, take, ptab, ttab, pos, xown, stdo, invo, wh,
    qt, kt, vt, mt, lt, acc,
    normed, fs, qsend, qall, av, ave, p1s, p2s, ps,
    attp, attb, attf, ef, updb, resid, gub, gab, gsend, gall, dpack, dbuf, df, sc, ret,
    loc, half_in, zin, zbuf, zgat, zown,
    lsem, send_s, recv_s, ag2send, ag2_s, zsend, z1_s, z2send, z2_s, csend, crecv, fsend, frecv,
):
    m = lax.axis_index("mp")
    z = lax.axis_index("dp")
    c = lax.axis_index("section")

    pairs = [(enc_h, enc), (we_h, we), (wq_h, wq), (wk_h, wk), (wv_h, wv), (wo_h, wo), (wp_h, wp), (tgt_h, tgt)]
    loads = [pltpu.make_async_copy(s, d, lsem.at[i]) for i, (s, d) in enumerate(pairs)]
    for load in loads:
        load.start()

    barrier = pltpu.get_barrier_semaphore()

    def each_peer(f):
        def one(j, _):
            f(lax.rem(m + j, N))
            return 0

        lax.fori_loop(1, N, one, 0)

    def each_z(f):
        def one(j, _):
            f(lax.rem(z + j, NZ))
            return 0

        lax.fori_loop(1, NZ, one, 0)

    each_peer(lambda k: pl.semaphore_signal(barrier, inc=1, device_id={"mp": k}, device_id_type=MESH))
    each_z(lambda k: pl.semaphore_signal(barrier, inc=1, device_id={"dp": k}, device_id_type=MESH))
    pl.semaphore_signal(barrier, inc=1, device_id={"section": 1 - c}, device_id_type=MESH)

    def to(k, src, dst, send, recv):
        return pltpu.make_async_remote_copy(
            src_ref=src, dst_ref=dst, send_sem=send, recv_sem=recv, device_id={"mp": k}, device_id_type=MESH
        )

    other = lax.rem(m + 1, N)

    def arrived(fifteen, sem):
        to(other, fifteen, fifteen, sem, sem).wait_recv()

    def left_here(fifteen, sem):
        to(other, fifteen, fifteen, sem, sem).wait_send()

    mine = rows(m, 16)
    own64 = rows(m, 64)

    loads[0].wait()
    loads[1].wait()

    def partial_block(g):
        both = jnp.concatenate(
            [enc[rows(g, 64), :], enc[pl.ds(pl.multiple_of(256 + g * 64, 64), 64), :]], axis=0
        )
        out = nn(both, we[...]).astype(BF16)
        part[0, rows(g, 64), :] = out[:64]
        part[1, rows(g, 64), :] = out[64:]

    my_group = m // 4

    def send_part(k):
        to(k, part.at[:, rows(k, 16)], rsbuf.at[m], send_s.at[0], recv_s.at[0]).start()

    partial_block(lax.rem(my_group + 1, 4))
    pl.semaphore_wait(barrier, N - 1 + NZ - 1 + 1)

    def send_group(jj, _):
        g = lax.rem(my_group + jj, 4)
        for i in range(4):
            send_part(4 * g + i)
        partial_block(lax.rem(g + 1, 4))
        return 0

    lax.fori_loop(1, 4, send_group, 0)
    for i in range(1, 4):
        send_part(4 * my_group + lax.rem(m + i, 4))

    owner_row = own_r[...].astype(F32)
    of_owner = jnp.where(owner_row == fiota((N, 1024), 0), 1.0, 0.0)
    before = hot(fiota((128, 128), 0) < fiota((128, 128), 1))
    carry = jnp.zeros((N, 1), F32)
    ranks = []
    for a in range(8):
        block = of_owner[:, a * 128 : (a + 1) * 128]
        prior = nn(block.astype(BF16), before) + carry
        carry = carry + jnp.sum(block, axis=1, keepdims=True)
        ranks.append(jnp.sum(prior * block, axis=0, keepdims=True))
    rank_row = jnp.concatenate(ranks, axis=1)
    patch_ids = lax.broadcasted_iota(jnp.int32, (N, 1024), 1)
    halves = jnp.concatenate(
        [of_owner * (patch_ids >> 5).astype(F32), of_owner * (patch_ids & 31).astype(F32)], axis=0
    ).astype(BF16)
    order[...] = nt(hot(rank_row == fiota((OWN, 1024), 0)), halves)

    def order_col(o):
        return jnp.sum(jnp.where(fiota((OWN, 2 * N), 1) == o, order[...], 0.0), axis=1, keepdims=True)

    lookup = jnp.concatenate(
        [owner_row[:, a * 128 : (a + 1) * 128] for a in range(8)] + [ranks[a] for a in range(8)], axis=0
    ).astype(BF16)
    eye = fiota((256, 256), 0) == fiota((256, 256), 1)
    lane = lax.broadcasted_iota(jnp.int32, (256, 128), 1)
    own_patch = []
    for b in range(2):
        vrow = vis_r[b : b + 1, :]
        found = nn(lookup, hot(lax.broadcasted_iota(jnp.int32, (128, 256), 0) == (vrow & 127)))
        part_of = lax.broadcasted_iota(jnp.int32, (8, 256), 0) == (vrow >> 7)
        vis_owner = jnp.sum(jnp.where(part_of, found[0:8], 0.0), axis=0, keepdims=True)
        vis_rank = jnp.sum(jnp.where(part_of, found[8:16], 0.0), axis=0, keepdims=True)
        by_rank = hot(vis_rank == fiota((OWN, 256), 0))
        for o in range(N):
            put[b, o * OWN : (o + 1) * OWN, :] = by_rank * hot(vis_owner == float(o))
        owner_col = jnp.sum(jnp.where(eye, vis_owner, 0.0), axis=1, keepdims=True)
        rank_col = jnp.sum(jnp.where(eye, vis_rank, 0.0), axis=1, keepdims=True)
        by_rank = hot(rank_col == (lane & 63).astype(F32))
        owner_lane = (lane >> 6).astype(F32)
        for t in range(8):
            take[b, :, t * 128 : (t + 1) * 128] = by_rank * hot(owner_col - 2.0 * t == owner_lane)
        seenrow[b] = nn(jnp.ones((N, 256), BF16), take[b])[0:1]
        seencol[b] = nn(put[b], jnp.ones((256, 128), BF16))[:, 0:1]
        mine_at = fiota((16, 256), 1) == fiota((16, 256), 0) + (m * 16).astype(F32)
        own_patch.append(jnp.sum(jnp.where(mine_at, vrow.astype(F32), 0.0), axis=1, keepdims=True))

    def terms(x):
        hi = x.astype(BF16)
        rest = x - hi.astype(F32)
        mid = rest.astype(BF16)
        return hi, mid, (rest - mid.astype(F32)).astype(BF16)

    trig = trig_r[...]
    ptab[...] = jnp.zeros_like(ptab)
    for i, term in enumerate(terms(trig)):
        ptab[32 * i : 32 * i + 32, 0:512] = term
        ptab[96 + 32 * i : 128 + 32 * i, 512:1024] = term

    def row_and_col(row, col):
        which = lax.broadcasted_iota(jnp.int32, (row.shape[0], 192), 1)
        return hot((which & 31).astype(F32) == jnp.where(which < 96, row, col))

    def positions(row, col):
        return nn(row_and_col(row, col), ptab[...])

    for i in (2, 3, 4):
        loads[i].wait()
    pair = lanes(m // 2, 128)
    odd = jnp.full((1024, HD), lax.rem(m, 2), jnp.int32) == 1
    for i, w in enumerate((wq, wk, wv)):
        two = w[:, pair].astype(F32)
        wh[:, i * HD : (i + 1) * HD] = jnp.where(odd, two[:, HD:], two[:, :HD]).astype(BF16)

    gain = gain_r[...]
    scale = jnp.array(0.125, BF16)

    def gained(x, gains, w):
        out = nn(jnp.concatenate(terms(x * gains), axis=0), w)
        n = x.shape[0]
        return out[0:n] + out[n : 2 * n] + out[2 * n : 3 * n]

    ones_gain = gained(jnp.ones((16, 1024), F32), gain, wh[...])[0:1]
    at_lane = lax.broadcasted_iota(jnp.int32, (GRID, 256), 1)
    for n, side in enumerate((1.0, -1.0)):
        cut = slice(512 * n, 512 * n + 512)
        x = trig + mask_r[:, cut]
        average = jnp.mean(x, axis=1, keepdims=True)
        spread = jnp.sum((x - average) * (x - average), axis=1, keepdims=True) * (1.0 / 1024)
        products = gained(x, gain[:, cut], wh[cut, :])
        full = jnp.concatenate([products, jnp.zeros((GRID, HD), F32)], axis=1)
        full = jnp.where(at_lane == 192, 0.5 * average, full)
        full = jnp.where(at_lane == 193, spread, full)
        full = jnp.where(at_lane == 194, (0.5 * side) * average, full)
        for i, term in enumerate(terms(full)):
            ttab[96 * n + 32 * i : 96 * n + 32 * i + 32, :] = term

    def masked(i):
        r = rows(i, 256)
        owners = [(4 * i + j).astype(F32) for j in range(4)]
        row = jnp.concatenate([order_col(o) for o in owners], axis=0)
        col = jnp.concatenate([order_col(o + N) for o in owners], axis=0)
        sums = nn(row_and_col(row, col), ttab[...])
        average, spread, apart = sums[:, 192:193], sums[:, 193:194], sums[:, 194:195]
        inv = lax.rsqrt(spread + apart * apart + 1e-06)
        three = ((sums[:, 0:192] - average * ones_gain) * inv).astype(BF16)
        qt[r, :] = three[:, 0:HD] * scale
        kt[r, :] = three[:, HD : 2 * HD]
        vt[r, :] = three[:, 2 * HD :]

    loop(4, masked)
    def table(i):
        r = rows(i, 256)
        s = nt(qt[r, :], kt[...])
        for b in range(2):
            held = jnp.where(seenrow[b] > 0.0, -jnp.inf, s)
            top = jnp.max(held, axis=1, keepdims=True)
            e = jnp.exp(held - top)
            mt[b, r, :] = top
            lt[b, r, :] = jnp.sum(e, axis=1, keepdims=True)
            acc[b, r, :] = nn(e.astype(BF16), vt[...])

    loop(3, table)
    ids = jnp.concatenate(own_patch, axis=0).astype(jnp.int32)
    xown[...] = positions((ids >> 5).astype(F32), (ids & 31).astype(F32))
    pos[...] = positions(order_col(m.astype(F32)), order_col((m + N).astype(F32)))
    encT[...] = jnp.transpose(enc[...])

    arrived(rsbuf.at[pl.ds(0, N - 1)], recv_s.at[0])
    rsbuf[m] = part[:, mine, :]
    own_rows = lax.fori_loop(
        0, N, lambda k, total: total + rsbuf[k].astype(F32), jnp.zeros((2, 16, 1024), F32)
    ).reshape(32, 1024)
    std, inv = norm(own_rows + xown[...])
    stdo[...] = std
    invo[...] = inv
    normed[...] = (std * gain).astype(BF16)
    fs[3] = own_rows.astype(BF16)

    def project(i):
        cut = lanes(i, 256)
        fs[0, :, cut] = nn(normed[...], wq[:, cut]).astype(BF16) * scale
        fs[1, :, cut] = nn(normed[...], wk[:, cut]).astype(BF16)
        fs[2, :, cut] = nn(normed[...], wv[:, cut]).astype(BF16)

    unrolled(4, project)

    def pack_rows(i):
        for t in range(4):
            two = fs[t, :, lanes(i, 128)].reshape(2, 16, 128)
            qsend[2 * i, :, :, t * HD : (t + 1) * HD] = two[:, :, :HD]
            qsend[2 * i + 1, :, :, t * HD : (t + 1) * HD] = two[:, :, HD:]

    unrolled(N // 2, pack_rows)
    each_peer(lambda k: to(k, qsend.at[k], qall.at[:, mine], send_s.at[1], recv_s.at[1]).start())
    qall[:, mine, :] = qsend[m]

    table(3)

    arrived(qall.at[:, pl.ds(0, 240)], recv_s.at[1])


    def attention(b):
        q, k, v = (qall[b, :, t * HD : (t + 1) * HD] for t in range(3))
        s1 = jnp.where(seenrow[b] > 0.0, -jnp.inf, nt(q, kt[...]))
        s2 = nt(q, k)
        top = jnp.maximum(jnp.max(s1, axis=1, keepdims=True), jnp.max(s2, axis=1, keepdims=True))
        e1 = jnp.exp(s1 - top)
        e2 = jnp.exp(s2 - top)
        inv = 1.0 / (jnp.sum(e1, axis=1, keepdims=True) + jnp.sum(e2, axis=1, keepdims=True))
        p1 = e1 * inv
        p2 = e2 * inv
        p1s[b] = p1
        p2s[b] = p2
        a = (nn(p1.astype(BF16), vt[...]) + nn(p2.astype(BF16), v)).astype(BF16)
        av[b] = a
        ave[b, :, 0:HD] = a
        ave[b, :, HD:] = qall[b, :, 3 * HD :]

        def attend(jj, _):
            g = lax.rem(my_group + jj, 4)
            r = rows(g, 256)
            s = nt(qt[r, :], qall[b, :, HD : 2 * HD])
            old = mt[b, r, :]
            top = jnp.maximum(old, jnp.max(s, axis=1, keepdims=True))
            e = jnp.exp(s - top)
            alpha = jnp.exp(old - top)
            inv = 1.0 / (alpha * lt[b, r, :] + jnp.sum(e, axis=1, keepdims=True))
            p = e * inv
            ps[b, r, :] = p
            att = acc[b, r, :] * (alpha * inv) + nn(p.astype(BF16), qall[b, :, 2 * HD : 3 * HD])
            placed = nn(put[b, r, :], ave[b])
            att = jnp.where(seencol[b, r, :] > 0.0, placed[:, 0:HD], att)
            attp[b, r, 0:HD] = att.astype(BF16)
            attp[b, r, HD:] = placed[:, HD:].astype(BF16)

            def send(i, _):
                k = 4 * g + lax.rem(m + i, 4)
                to(k, attp.at[b, rows(k, 64)], attb.at[b, m], send_s.at[2 + b], recv_s.at[2 + b]).start()
                return 0

            lax.fori_loop(jnp.where(jj == 4, 1, 0), 4, send, 0)
            return 0

        lax.fori_loop(1, 5, attend, 0)
        attb[b, m] = attp[b, own64, :]

    unrolled(2, attention)

    for i in (5, 6, 7):
        loads[i].wait()

    def owner_work(b):
        arrived(attb.at[b, pl.ds(0, N - 1)], recv_s.at[2 + b])

        def unpack(i):
            one, two = attb[b, 2 * i], attb[b, 2 * i + 1]
            attf[:, lanes(i, 128)] = jnp.concatenate([one[:, :HD], two[:, :HD]], axis=1)
            ef[:, lanes(i, 128)] = jnp.concatenate([one[:, HD:], two[:, HD:]], axis=1)

        unrolled(N // 2, unpack)
        seen = seencol[b, own64, :] > 0.0

        def update(i):
            cut = lanes(i, 256)
            inputs = jnp.where(seen, ef[:, cut].astype(F32), mask_r[:, cut]) + pos[:, cut]
            updb[:, cut] = (inputs + nn(attf[...], wo[:, cut])).astype(BF16)

        unrolled(4, update)

        def predict(i):
            cut = lanes(i, 256)
            px = nn(updb[...], wp[:, cut])
            pred_o[b, :, cut] = px.astype(BF16)
            resid[:, cut] = jnp.where(seen, 0.0, px - tgt[b, :, cut].astype(F32)).astype(BF16)

        unrolled(3, predict)

        def grad_updated(i):
            gub[:, lanes(i, 256)] = nt(resid[...], wp[rows(i, 256), :]).astype(BF16)

        unrolled(4, grad_updated)

        def grad_attended(i):
            gab[:, lanes(i, 256)] = nt(gub[...], wo[rows(i, 256), :]).astype(BF16)

        unrolled(4, grad_attended)

        def pack(i):
            a, u = gab[:, lanes(i, 128)], gub[:, lanes(i, 128)]
            gsend[b, 2 * i] = jnp.concatenate([a[:, :HD], u[:, :HD]], axis=1)
            gsend[b, 2 * i + 1] = jnp.concatenate([a[:, HD:], u[:, HD:]], axis=1)

        unrolled(N // 2, pack)
        each_peer(lambda k: to(k, gsend.at[b, k], gall.at[b, own64], send_s.at[4 + b], recv_s.at[4 + b]).start())
        gall[b, own64, :] = gsend[b, m]

    unrolled(2, owner_work)

    def backward(b):
        arrived(gall.at[b, pl.ds(0, 960)], recv_s.at[4 + b])
        q, k, v = (qall[b, :, t * HD : (t + 1) * HD] for t in range(3))

        def keys_back(i, totals):
            r = rows(i, 256)
            wide = jnp.where(seencol[b, r, :] > 0.0, 0.0, gall[b, r, 0:HD].astype(F32))
            g = wide.astype(BF16)
            delta = jnp.sum(wide * attp[b, r, 0:HD].astype(F32), axis=1, keepdims=True)
            p = ps[b, r, :]
            ds = (p * (nt(g, qall[b, :, 2 * HD : 3 * HD]) - delta)).astype(BF16)
            return (totals[0] + tn(ds, qt[r, :]), totals[1] + tn(p.astype(BF16), g))

        nil = jnp.zeros((256, HD), F32)
        dk, dv = lax.fori_loop(0, 4, keys_back, (nil, nil))

        both = nn(take[b], gall[b])
        gv = both[:, 0:HD]
        delta = jnp.sum(gv * av[b].astype(F32), axis=1, keepdims=True)
        gv = gv.astype(BF16)
        p2 = p2s[b]
        ds1 = (p1s[b] * (nt(gv, vt[...]) - delta)).astype(BF16)
        ds2 = (p2 * (nt(gv, v) - delta)).astype(BF16)
        dq = (nn(ds1, kt[...]) + nn(ds2, k)) * 0.125
        dk = dk + tn(ds2, q)
        dv = dv + tn(p2.astype(BF16), gv)
        dpack[b, :, 0:HD] = dq.astype(BF16)
        dpack[b, :, HD : 2 * HD] = dk.astype(BF16)
        dpack[b, :, 2 * HD : 3 * HD] = dv.astype(BF16)
        dpack[b, :, 3 * HD :] = both[:, HD:].astype(BF16)
        each_peer(lambda k: to(k, dpack.at[b, rows(k, 16)], dbuf.at[b, m], send_s.at[6 + b], recv_s.at[6 + b]).start())
        dbuf[b, m] = dpack[b, mine, :]

    unrolled(2, backward)

    def norm_back(b):
        arrived(dbuf.at[b, pl.ds(0, N - 1)], recv_s.at[6 + b])

        def unpack(i):
            one, two = dbuf[b, 2 * i], dbuf[b, 2 * i + 1]
            for t in range(4):
                cut = slice(t * HD, (t + 1) * HD)
                df[t, :, lanes(i, 128)] = jnp.concatenate([one[:, cut], two[:, cut]], axis=1)

        unrolled(N // 2, unpack)

        def back_project(i):
            r = rows(i, 256)
            cut = lanes(i, 256)
            sc[:, cut] = (nt(df[0], wq[r, :]) + nt(df[1], wk[r, :]) + nt(df[2], wv[r, :])) * gain_r[:, cut]

        unrolled(4, back_project)
        scaled = sc[...]
        std = stdo[rows(b, 16), :]
        back = df[3].astype(F32) + invo[rows(b, 16), :] * (
            scaled
            - jnp.mean(scaled, axis=-1, keepdims=True)
            - std * jnp.mean(scaled * std, axis=-1, keepdims=True)
        )
        for q in range(PIECES):
            ret[q, b, mine, :] = back[:, q * WIDE : (q + 1) * WIDE].astype(BF16)
        for block, sem in [(ret.at[:, 0, mine], (0, 0))] if b == 0 else [(ret.at[q, 1, mine], (q, 1)) for q in range(PIECES)]:
            each_peer(lambda k: to(k, block, block, ag2send.at[sem], ag2_s.at[sem]).start())

    unrolled(2, norm_back)

    def cross(src, dst, send, recv):
        return pltpu.make_async_remote_copy(
            src_ref=src, dst_ref=dst, send_sem=send, recv_sem=recv,
            device_id={"section": 1 - c}, device_id_type=MESH,
        )

    def z_copy(k, src, dst, send, recv):
        return pltpu.make_async_remote_copy(
            src_ref=src, dst_ref=dst, send_sem=send, recv_sem=recv,
            device_id={"dp": k}, device_id_type=MESH,
        )

    z_other = lax.rem(z + 1, NZ)
    firsts = [cross(loc.at[q, :, rows(1 - c, 192)], half_in.at[q], csend.at[q], crecv.at[q]) for q in range(PIECES)]
    arrived(ret.at[:, 0, pl.ds(0, 240)], ag2_s.at[0, 0])
    for q in range(PIECES):
        arrived(ret.at[q, 1, pl.ds(0, 240)], ag2_s.at[q, 1])

        def local_grad(t, q=q):
            both = nn(encT[...], ret[q, :, :, lanes(t, 256)].reshape(512, 256)).astype(BF16)
            loc[q, 2 * t] = both[:, :128]
            loc[q, 2 * t + 1] = both[:, 128:]

        unrolled(WIDE // 256, local_grad)
        firsts[q].start()

    for q in range(PIECES):
        firsts[q].wait_recv()

        def both_cores(d, q=q):
            t, deep = d % TILES, (d // TILES) * DEEP
            own_part = loc[q, t, pl.ds(pl.multiple_of(c * 192 + deep, DEEP), DEEP), :]
            their_part = half_in[q, t, deep : deep + DEEP, :]
            zin[q, d] = (own_part.astype(F32) + their_part.astype(F32)).astype(BF16)

        unrolled(NZ, both_cores)
        each_z(lambda k, q=q: z_copy(k, zin.at[q, k], zbuf.at[q, z], zsend.at[q], z1_s.at[q]).start())

    forward = lambda q, k: cross(zgat.at[q, k], zown.at[q, k], fsend.at[q, k], frecv.at[q, k])
    for q in range(PIECES):
        z_copy(z_other, zbuf.at[q, pl.ds(0, NZ - 1)], zbuf.at[q, pl.ds(0, NZ - 1)], zsend.at[q], z1_s.at[q]).wait_recv()
        zbuf[q, z] = zin[q, z]
        total = zbuf[q, 0].astype(F32)
        for k in range(1, NZ):
            total = total + zbuf[q, k].astype(F32)
        zgat[q, z] = total.astype(BF16)
        each_z(lambda k, q=q: z_copy(k, zgat.at[q, z], zgat.at[q, z], z2send.at[q], z2_s.at[q, z]).start())
        forward(q, z).start()

    def encoder_grad(b):
        total = nt(ret[0, b], we[:, 0:WIDE])
        for q in range(1, PIECES):
            total = total + nt(ret[q, b], we[:, q * WIDE : (q + 1) * WIDE])
        encg_o[rows(b, 256), :] = total.astype(BF16)

    unrolled(2, encoder_grad)

    def get_z(q, k):
        z_copy(k, zgat.at[q, k], zgat.at[q, k], z2send.at[q], z2_s.at[q, k]).wait_recv()
        forward(q, k).start()

    def write(q, core, block):
        for d in range(NZ):
            at = pl.ds(pl.multiple_of(core * 192 + (d // TILES) * DEEP, DEEP), DEEP)
            col = q * WIDE + (d % TILES) * 128
            emb_o[at, col : col + 128] = block[q, d]

    for q in range(PIECES):
        each_z(lambda k, q=q: get_z(q, k))
        write(q, c, zgat)
    for q in range(PIECES):
        for k in range(NZ):
            forward(q, k).wait_recv()
        write(q, 1 - c, zown)

    left_here(rsbuf.at[pl.ds(0, N - 1)], send_s.at[0])
    left_here(qsend.at[pl.ds(0, N - 1)], send_s.at[1])
    for b in range(2):
        left_here(attb.at[b, pl.ds(0, N - 1)], send_s.at[2 + b])
        left_here(gsend.at[b, pl.ds(0, N - 1)], send_s.at[4 + b])
        left_here(dbuf.at[b, pl.ds(0, N - 1)], send_s.at[6 + b])
    left_here(ret.at[:, 0, pl.ds(0, 240)], ag2send.at[0, 0])
    for q in range(PIECES):
        left_here(ret.at[q, 1, pl.ds(0, 240)], ag2send.at[q, 1])
    for q in range(PIECES):
        firsts[q].wait_send()
        seven = zbuf.at[q, pl.ds(0, NZ - 1)]
        z_copy(z_other, seven, seven, zsend.at[q], z1_s.at[q]).wait_send()
        z_copy(z_other, seven, seven, z2send.at[q], z1_s.at[q]).wait_send()
        for k in range(NZ):
            forward(q, k).wait_send()


def finish(pred_i, encg_i, emb_i, pred_o, encg_o, emb_o):
    pred_o[...] = pred_i[...]
    encg_o[...] = encg_i[...]
    emb_o[...] = emb_i[...].astype(F32) * 8192 ** (-0.5)


def body(
    encoded, visible, owner, embed_weight, mask_token, norm_gain,
    query_weight, key_weight, value_weight, out_weight, pixel_weight, targets,
):
    quarter = 256
    freqs = 10000.0 ** (-jnp.arange(quarter, dtype=F32) / quarter)
    angle = jnp.arange(GRID, dtype=F32)[:, None] * freqs[None, :]
    trig = jnp.concatenate([jnp.sin(angle), jnp.cos(angle)], axis=1)
    vm = pl.BlockSpec(memory_space=pltpu.VMEM)
    hbm = pl.BlockSpec(memory_space=pl.ANY)
    V = pltpu.VMEM
    dma = pltpu.SemaphoreType.DMA
    scratch = [
        V((512, 384), BF16), V((384, 1024), BF16),
        V((1024, 1024), BF16), V((1024, 1024), BF16), V((1024, 1024), BF16), V((1024, 1024), BF16),
        V((1024, 768), BF16), V((2, 64, 768), BF16),
        V((2, 256, 1024), BF16), V((N, 2, 16, 1024), BF16), V((384, 512), BF16),
        V((OWN, 2 * N), F32), V((2, 1, 1024), F32), V((2, 1024, 1), F32),
        V((2, 1024, 256), BF16), V((2, 256, 1024), BF16), V((192, 1024), BF16), V((192, 256), BF16),
        V((OWN, 1024), F32), V((32, 1024), F32), V((32, 1024), F32), V((32, 1), F32), V((1024, 192), BF16),
        V((1024, HD), BF16), V((1024, HD), BF16), V((1024, HD), BF16),
        V((2, 1024, 1), F32), V((2, 1024, 1), F32), V((2, 1024, HD), F32),
        V((32, 1024), BF16), V((4, 32, 1024), BF16), V((N, 2, 16, 256), BF16), V((2, 256, 256), BF16), V((2, 256, HD), BF16), V((2, 256, 2 * HD), BF16),
        V((2, 256, 1024), F32), V((2, 256, 256), F32), V((2, 1024, 256), F32),
        V((2, 1024, 128), BF16), V((2, N, 64, 128), BF16), V((64, 1024), BF16), V((64, 1024), BF16),
        V((64, 1024), BF16), V((64, 768), BF16), V((64, 1024), BF16), V((64, 1024), BF16),
        V((2, N, 64, 128), BF16), V((2, 1024, 128), BF16), V((2, 256, 256), BF16), V((2, N, 16, 256), BF16),
        V((4, 16, 1024), BF16), V((16, 1024), F32), V((PIECES, 2, 256, WIDE), BF16),
        V((PIECES, TILES, 384, 128), BF16), V((PIECES, TILES, 192, 128), BF16),
        V((PIECES, NZ, DEEP, 128), BF16), V((PIECES, NZ, DEEP, 128), BF16),
        V((PIECES, NZ, DEEP, 128), BF16), V((PIECES, NZ, DEEP, 128), BF16),
        dma((8,)), dma((8,)), dma((8,)), dma((PIECES, 2)), dma((PIECES, 2)),
        dma((PIECES,)), dma((PIECES,)), dma((PIECES,)), dma((PIECES, NZ)),
        dma((PIECES,)), dma((PIECES,)), dma((PIECES, NZ)), dma((PIECES, NZ)),
    ]
    predicted, encoded_grad, summed = pl.pallas_call(
        kernel,
        out_shape=(
            jax.ShapeDtypeStruct((2, 64, 768), BF16),
            jax.ShapeDtypeStruct((512, 384), BF16),
            jax.ShapeDtypeStruct((384, 1024), BF16),
        ),
        in_specs=[hbm, hbm, vm, vm, vm, vm, hbm, hbm, hbm, hbm, hbm, hbm, vm],
        out_specs=(vm, vm, vm),
        scratch_shapes=scratch,
        compiler_params=pltpu.CompilerParams(
            collective_id=0, has_side_effects=True, vmem_limit_bytes=58 * 1024 * 1024
        ),
        cost_estimate=pl.CostEstimate(flops=8_000_000_000, bytes_accessed=16_000_000, transcendentals=4_000_000),
    )(
        encoded, embed_weight, owner.reshape(1, 1024), visible, mask_token.reshape(1, 1024), norm_gain.reshape(1, 1024),
        query_weight, key_weight, value_weight, out_weight, pixel_weight, targets, trig,
    )
    return pl.pallas_call(
        finish,
        out_shape=(
            jax.ShapeDtypeStruct((2, 64, 768), BF16),
            jax.ShapeDtypeStruct((512, 384), BF16),
            jax.ShapeDtypeStruct((384, 1024), F32),
        ),
        in_specs=[vm, vm, vm],
        out_specs=(vm, vm, vm),
        cost_estimate=pl.CostEstimate(flops=400_000, bytes_accessed=3_500_000, transcendentals=0),
    )(predicted, encoded_grad, summed)


def solution(mesh):
    placed = (
        P(("dp", "section"), "mp"),
        P(("dp", "section"), None),
        P(),
        P("mp", None),
        P(),
        P(),
        P(),
        P(),
        P(),
        P(),
        P(),
        P(("dp", "section"), "mp", None),
    )
    return jax.shard_map(
        body,
        mesh=mesh,
        in_specs=placed,
        out_specs=(P(("dp", "section"), "mp", None), P(("dp", "section"), "mp"), P("mp", None)),
        check_vma=False,
    )
```

```python
import functools

import jax
import jax.numpy as jnp
from jax import lax
from jax.experimental import pallas as pl
from jax.experimental.pallas import tpu as pltpu
from jax.sharding import PartitionSpec as P

MESH = pl.DeviceIdType.MESH
F32 = jnp.float32
BF16 = jnp.bfloat16
GRID = 32
N = 16
NZ = 8
HD = 64
OWN = 64
PIECES = 2
WIDE = 1024 // PIECES
TILES = WIDE // 128
DEEP = 192 * TILES // NZ


def nn(a, b):
    return lax.dot_general(a, b, (((1,), (0,)), ((), ())), preferred_element_type=F32)


def nt(a, b):
    return lax.dot_general(a, b, (((1,), (1,)), ((), ())), preferred_element_type=F32)


def tn(a, b):
    return lax.dot_general(a, b, (((0,), (0,)), ((), ())), preferred_element_type=F32)


def fiota(shape, dim):
    return lax.broadcasted_iota(jnp.int32, shape, dim).astype(F32)


def hot(cond):
    return jnp.where(cond, 1.0, 0.0).astype(BF16)


def norm(x):
    c = x - jnp.mean(x, axis=-1, keepdims=True)
    inv = lax.rsqrt(jnp.mean(c * c, axis=-1, keepdims=True) + 1e-06)
    return c * inv, inv


def lanes(i, size):
    if isinstance(i, int):
        return slice(i * size, (i + 1) * size)
    return pl.ds(pl.multiple_of(i * size, size), size)


def unrolled(n, f):
    for i in range(n):
        f(i)


def loop(n, f):
    def one(i, _):
        f(i)
        return 0

    lax.fori_loop(0, n, one, 0)


rows = lanes


def kernel(
    enc_h, we_h, own_r, vis_r, mask_r, gain_r, wq_h, wk_h, wv_h, wo_h, wp_h, tgt_h, trig_r,
    pred_o, encg_o, emb_o,
    enc, we, wq, wk, wv, wo, wp, tgt,
    part, rsbuf, rsbuf2, line, encT,
    order, seenrow, seencol, put, take, ptab, ttab, pos, xown, stdo, invo, wh,
    qt, kt, vt, mt, lt, acc,
    normed, fs, qsend, qall, av, ave, p1s, p2s, ps,
    attp, attb, attf, ef, updb, resid, gub, gab, gsend, gall, dpack, dbuf, df, sc, ret,
    loc, half_in, zin, zbuf, zgat, zown,
    lsem, one_s, one_r, two_s, two_r, send_s, recv_s, ag2send, ag2_s, zsend, z1_s, z2send, z2_s, csend, crecv, fsend, frecv,
):
    m = lax.axis_index("mp")
    z = lax.axis_index("dp")
    c = lax.axis_index("section")

    pairs = [(enc_h, enc), (we_h, we), (wq_h, wq), (wk_h, wk), (wv_h, wv), (wo_h, wo), (wp_h, wp), (tgt_h, tgt)]
    loads = [pltpu.make_async_copy(s, d, lsem.at[i]) for i, (s, d) in enumerate(pairs)]
    for load in loads:
        load.start()

    barrier = pltpu.get_barrier_semaphore()

    def each_peer(f):
        def one(j, _):
            f(lax.rem(m + j, N))
            return 0

        lax.fori_loop(1, N, one, 0)

    def each_z(f):
        def one(j, _):
            f(lax.rem(z + j, NZ))
            return 0

        lax.fori_loop(1, NZ, one, 0)

    each_peer(lambda k: pl.semaphore_signal(barrier, inc=1, device_id={"mp": k}, device_id_type=MESH))
    each_z(lambda k: pl.semaphore_signal(barrier, inc=1, device_id={"dp": k}, device_id_type=MESH))
    pl.semaphore_signal(barrier, inc=1, device_id={"section": 1 - c}, device_id_type=MESH)

    def to(k, src, dst, send, recv):
        return pltpu.make_async_remote_copy(
            src_ref=src, dst_ref=dst, send_sem=send, recv_sem=recv, device_id={"mp": k}, device_id_type=MESH
        )

    other = lax.rem(m + 1, N)

    def arrived(fifteen, sem):
        to(other, fifteen, fifteen, sem, sem).wait_recv()

    def left_here(fifteen, sem):
        to(other, fifteen, fifteen, sem, sem).wait_send()

    mine = rows(m, 16)
    own64 = rows(m, 64)

    loads[0].wait()
    loads[1].wait()

    mx, my = m // 4, lax.rem(m, 4)
    first_at, second_at = (mx, my), (my, mx)

    def device(half, along_first, along_second):
        return 4 * along_first + along_second if half == 0 else 4 * along_second + along_first

    def partial_block(g):
        both = jnp.concatenate(
            [enc[rows(g, 64), :], enc[pl.ds(pl.multiple_of(256 + g * 64, 64), 64), :]], axis=0
        )
        out = nn(both, we[...]).astype(BF16)
        for b in range(2):
            part[0, b, rows(g, 64), :] = out[b * 64 : (b + 1) * 64, 0:512]
            for y in range(4):
                at = pl.ds(pl.multiple_of(y * 64 + g * 16, 16), 16)
                part[1, b, at, :] = out[b * 64 + y * 16 : b * 64 + (y + 1) * 16, 512:1024]

    def send_first(half, to_line):
        to(
            device(half, to_line, second_at[half]), part.at[half, :, rows(to_line, 64)],
            rsbuf.at[half, first_at[half]], one_s.at[half], one_r.at[half],
        ).start()

    partial_block(lax.rem(mx + 1, 4))
    pl.semaphore_wait(barrier, N - 1 + NZ - 1 + 1)

    def send_group(jj, _):
        g = lax.rem(mx + jj, 4)
        send_first(0, g)
        partial_block(lax.rem(g + 1, 4))
        return 0

    lax.fori_loop(1, 4, send_group, 0)
    for j in range(1, 4):
        send_first(1, lax.rem(my + j, 4))
    my_group = mx

    owner_row = own_r[...].astype(F32)
    of_owner = jnp.where(owner_row == fiota((N, 1024), 0), 1.0, 0.0)
    before = hot(fiota((128, 128), 0) < fiota((128, 128), 1))
    carry = jnp.zeros((N, 1), F32)
    ranks = []
    for a in range(8):
        block = of_owner[:, a * 128 : (a + 1) * 128]
        prior = nn(block.astype(BF16), before) + carry
        carry = carry + jnp.sum(block, axis=1, keepdims=True)
        ranks.append(jnp.sum(prior * block, axis=0, keepdims=True))
    rank_row = jnp.concatenate(ranks, axis=1)
    patch_ids = lax.broadcasted_iota(jnp.int32, (N, 1024), 1)
    halves = jnp.concatenate(
        [of_owner * (patch_ids >> 5).astype(F32), of_owner * (patch_ids & 31).astype(F32)], axis=0
    ).astype(BF16)
    order[...] = nt(hot(rank_row == fiota((OWN, 1024), 0)), halves)

    def order_col(o):
        return jnp.sum(jnp.where(fiota((OWN, 2 * N), 1) == o, order[...], 0.0), axis=1, keepdims=True)

    lookup = jnp.concatenate(
        [owner_row[:, a * 128 : (a + 1) * 128] for a in range(8)] + [ranks[a] for a in range(8)], axis=0
    ).astype(BF16)
    eye = fiota((256, 256), 0) == fiota((256, 256), 1)
    lane = lax.broadcasted_iota(jnp.int32, (256, 128), 1)
    own_patch = []
    for b in range(2):
        vrow = vis_r[b : b + 1, :]
        found = nn(lookup, hot(lax.broadcasted_iota(jnp.int32, (128, 256), 0) == (vrow & 127)))
        part_of = lax.broadcasted_iota(jnp.int32, (8, 256), 0) == (vrow >> 7)
        vis_owner = jnp.sum(jnp.where(part_of, found[0:8], 0.0), axis=0, keepdims=True)
        vis_rank = jnp.sum(jnp.where(part_of, found[8:16], 0.0), axis=0, keepdims=True)
        by_rank = hot(vis_rank == fiota((OWN, 256), 0))
        for o in range(N):
            put[b, o * OWN : (o + 1) * OWN, :] = by_rank * hot(vis_owner == float(o))
        owner_col = jnp.sum(jnp.where(eye, vis_owner, 0.0), axis=1, keepdims=True)
        rank_col = jnp.sum(jnp.where(eye, vis_rank, 0.0), axis=1, keepdims=True)
        by_rank = hot(rank_col == (lane & 63).astype(F32))
        owner_lane = (lane >> 6).astype(F32)
        for t in range(8):
            take[b, :, t * 128 : (t + 1) * 128] = by_rank * hot(owner_col - 2.0 * t == owner_lane)
        seenrow[b] = nn(jnp.ones((N, 256), BF16), take[b])[0:1]
        seencol[b] = nn(put[b], jnp.ones((256, 128), BF16))[:, 0:1]
        mine_at = fiota((16, 256), 1) == fiota((16, 256), 0) + (m * 16).astype(F32)
        own_patch.append(jnp.sum(jnp.where(mine_at, vrow.astype(F32), 0.0), axis=1, keepdims=True))

    def terms(x):
        hi = x.astype(BF16)
        rest = x - hi.astype(F32)
        mid = rest.astype(BF16)
        return hi, mid, (rest - mid.astype(F32)).astype(BF16)

    trig = trig_r[...]
    ptab[...] = jnp.zeros_like(ptab)
    for i, term in enumerate(terms(trig)):
        ptab[32 * i : 32 * i + 32, 0:512] = term
        ptab[96 + 32 * i : 128 + 32 * i, 512:1024] = term

    def row_and_col(row, col):
        which = lax.broadcasted_iota(jnp.int32, (row.shape[0], 192), 1)
        return hot((which & 31).astype(F32) == jnp.where(which < 96, row, col))

    def positions(row, col):
        return nn(row_and_col(row, col), ptab[...])

    for i in (2, 3, 4):
        loads[i].wait()
    pair = lanes(m // 2, 128)
    odd = jnp.full((1024, HD), lax.rem(m, 2), jnp.int32) == 1
    for i, w in enumerate((wq, wk, wv)):
        two = w[:, pair].astype(F32)
        wh[:, i * HD : (i + 1) * HD] = jnp.where(odd, two[:, HD:], two[:, :HD]).astype(BF16)

    gain = gain_r[...]
    scale = jnp.array(0.125, BF16)

    def gained(x, gains, w):
        out = nn(jnp.concatenate(terms(x * gains), axis=0), w)
        n = x.shape[0]
        return out[0:n] + out[n : 2 * n] + out[2 * n : 3 * n]

    ones_gain = gained(jnp.ones((16, 1024), F32), gain, wh[...])[0:1]
    at_lane = lax.broadcasted_iota(jnp.int32, (GRID, 256), 1)
    for n, side in enumerate((1.0, -1.0)):
        cut = slice(512 * n, 512 * n + 512)
        x = trig + mask_r[:, cut]
        average = jnp.mean(x, axis=1, keepdims=True)
        spread = jnp.sum((x - average) * (x - average), axis=1, keepdims=True) * (1.0 / 1024)
        products = gained(x, gain[:, cut], wh[cut, :])
        full = jnp.concatenate([products, jnp.zeros((GRID, HD), F32)], axis=1)
        full = jnp.where(at_lane == 192, 0.5 * average, full)
        full = jnp.where(at_lane == 193, spread, full)
        full = jnp.where(at_lane == 194, (0.5 * side) * average, full)
        for i, term in enumerate(terms(full)):
            ttab[96 * n + 32 * i : 96 * n + 32 * i + 32, :] = term

    def masked(i):
        r = rows(i, 256)
        owners = [(4 * i + j).astype(F32) for j in range(4)]
        row = jnp.concatenate([order_col(o) for o in owners], axis=0)
        col = jnp.concatenate([order_col(o + N) for o in owners], axis=0)
        sums = nn(row_and_col(row, col), ttab[...])
        average, spread, apart = sums[:, 192:193], sums[:, 193:194], sums[:, 194:195]
        inv = lax.rsqrt(spread + apart * apart + 1e-06)
        three = ((sums[:, 0:192] - average * ones_gain) * inv).astype(BF16)
        qt[r, :] = three[:, 0:HD] * scale
        kt[r, :] = three[:, HD : 2 * HD]
        vt[r, :] = three[:, 2 * HD :]

    loop(4, masked)
    def table(i):
        r = rows(i, 256)
        s = nt(qt[r, :], kt[...])
        for b in range(2):
            held = jnp.where(seenrow[b] > 0.0, -jnp.inf, s)
            top = jnp.max(held, axis=1, keepdims=True)
            e = jnp.exp(held - top)
            mt[b, r, :] = top
            lt[b, r, :] = jnp.sum(e, axis=1, keepdims=True)
            acc[b, r, :] = nn(e.astype(BF16), vt[...])

    table(0)

    for half in range(2):
        here = first_at[half]
        arrived(rsbuf.at[half, pl.ds(0, 3)], one_r.at[half])
        rsbuf[half, here] = part[half, :, rows(here, 64), :]
        total = rsbuf[half, 0].astype(F32)
        for a in range(1, 4):
            total = total + rsbuf[half, a].astype(F32)
        line[half] = total.astype(BF16)
        for j in range(1, 4):
            there = lax.rem(second_at[half] + j, 4)
            to(
                device(half, here, there), line.at[half, :, rows(there, 16)],
                rsbuf2.at[half, second_at[half]], two_s.at[half], two_r.at[half],
            ).start()

    lax.fori_loop(1, 3, lambda i, _: (table(i), 0)[1], 0)
    ids = jnp.concatenate(own_patch, axis=0).astype(jnp.int32)
    xown[...] = positions((ids >> 5).astype(F32), (ids & 31).astype(F32))
    pos[...] = positions(order_col(m.astype(F32)), order_col((m + N).astype(F32)))
    encT[...] = jnp.transpose(enc[...])

    own_rows = []
    for half in range(2):
        here = second_at[half]
        arrived(rsbuf2.at[half, pl.ds(0, 3)], two_r.at[half])
        rsbuf2[half, here] = line[half, :, rows(here, 16), :]
        total = rsbuf2[half, 0].astype(F32)
        for a in range(1, 4):
            total = total + rsbuf2[half, a].astype(F32)
        own_rows.append(total.reshape(32, 512))
    own_rows = jnp.concatenate(own_rows, axis=1)
    std, inv = norm(own_rows + xown[...])
    stdo[...] = std
    invo[...] = inv
    normed[...] = (std * gain).astype(BF16)
    fs[3] = own_rows.astype(BF16)

    def project(i):
        cut = lanes(i, 256)
        fs[0, :, cut] = nn(normed[...], wq[:, cut]).astype(BF16) * scale
        fs[1, :, cut] = nn(normed[...], wk[:, cut]).astype(BF16)
        fs[2, :, cut] = nn(normed[...], wv[:, cut]).astype(BF16)

    unrolled(4, project)

    def pack_rows(i):
        for t in range(4):
            two = fs[t, :, lanes(i, 128)].reshape(2, 16, 128)
            qsend[2 * i, :, :, t * HD : (t + 1) * HD] = two[:, :, :HD]
            qsend[2 * i + 1, :, :, t * HD : (t + 1) * HD] = two[:, :, HD:]

    unrolled(N // 2, pack_rows)
    each_peer(lambda k: to(k, qsend.at[k], qall.at[:, mine], send_s.at[1], recv_s.at[1]).start())
    qall[:, mine, :] = qsend[m]

    table(3)

    arrived(qall.at[:, pl.ds(0, 240)], recv_s.at[1])


    def attention(b):
        q, k, v = (qall[b, :, t * HD : (t + 1) * HD] for t in range(3))
        s1 = jnp.where(seenrow[b] > 0.0, -jnp.inf, nt(q, kt[...]))
        s2 = nt(q, k)
        top = jnp.maximum(jnp.max(s1, axis=1, keepdims=True), jnp.max(s2, axis=1, keepdims=True))
        e1 = jnp.exp(s1 - top)
        e2 = jnp.exp(s2 - top)
        inv = 1.0 / (jnp.sum(e1, axis=1, keepdims=True) + jnp.sum(e2, axis=1, keepdims=True))
        p1 = e1 * inv
        p2 = e2 * inv
        p1s[b] = p1
        p2s[b] = p2
        a = (nn(p1.astype(BF16), vt[...]) + nn(p2.astype(BF16), v)).astype(BF16)
        av[b] = a
        ave[b, :, 0:HD] = a
        ave[b, :, HD:] = qall[b, :, 3 * HD :]

        def attend(jj, _):
            g = lax.rem(my_group + jj, 4)
            r = rows(g, 256)
            s = nt(qt[r, :], qall[b, :, HD : 2 * HD])
            old = mt[b, r, :]
            top = jnp.maximum(old, jnp.max(s, axis=1, keepdims=True))
            e = jnp.exp(s - top)
            alpha = jnp.exp(old - top)
            inv = 1.0 / (alpha * lt[b, r, :] + jnp.sum(e, axis=1, keepdims=True))
            p = e * inv
            ps[b, r, :] = p
            att = acc[b, r, :] * (alpha * inv) + nn(p.astype(BF16), qall[b, :, 2 * HD : 3 * HD])
            placed = nn(put[b, r, :], ave[b])
            att = jnp.where(seencol[b, r, :] > 0.0, placed[:, 0:HD], att)
            attp[b, r, 0:HD] = att.astype(BF16)
            attp[b, r, HD:] = placed[:, HD:].astype(BF16)

            def send(i, _):
                k = 4 * g + lax.rem(m + i, 4)
                to(k, attp.at[b, rows(k, 64)], attb.at[b, m], send_s.at[2 + b], recv_s.at[2 + b]).start()
                return 0

            lax.fori_loop(jnp.where(jj == 4, 1, 0), 4, send, 0)
            return 0

        lax.fori_loop(1, 5, attend, 0)
        attb[b, m] = attp[b, own64, :]

    unrolled(2, attention)

    for i in (5, 6, 7):
        loads[i].wait()

    def owner_work(b):
        arrived(attb.at[b, pl.ds(0, N - 1)], recv_s.at[2 + b])

        def unpack(i):
            one, two = attb[b, 2 * i], attb[b, 2 * i + 1]
            attf[:, lanes(i, 128)] = jnp.concatenate([one[:, :HD], two[:, :HD]], axis=1)
            ef[:, lanes(i, 128)] = jnp.concatenate([one[:, HD:], two[:, HD:]], axis=1)

        unrolled(N // 2, unpack)
        seen = seencol[b, own64, :] > 0.0

        def update(i):
            cut = lanes(i, 256)
            inputs = jnp.where(seen, ef[:, cut].astype(F32), mask_r[:, cut]) + pos[:, cut]
            updb[:, cut] = (inputs + nn(attf[...], wo[:, cut])).astype(BF16)

        unrolled(4, update)

        def predict(i):
            cut = lanes(i, 256)
            px = nn(updb[...], wp[:, cut])
            pred_o[b, :, cut] = px.astype(BF16)
            resid[:, cut] = jnp.where(seen, 0.0, px - tgt[b, :, cut].astype(F32)).astype(BF16)

        unrolled(3, predict)

        def grad_updated(i):
            gub[:, lanes(i, 256)] = nt(resid[...], wp[rows(i, 256), :]).astype(BF16)

        unrolled(4, grad_updated)

        def grad_attended(i):
            gab[:, lanes(i, 256)] = nt(gub[...], wo[rows(i, 256), :]).astype(BF16)

        unrolled(4, grad_attended)

        def pack(i):
            a, u = gab[:, lanes(i, 128)], gub[:, lanes(i, 128)]
            gsend[b, 2 * i] = jnp.concatenate([a[:, :HD], u[:, :HD]], axis=1)
            gsend[b, 2 * i + 1] = jnp.concatenate([a[:, HD:], u[:, HD:]], axis=1)

        unrolled(N // 2, pack)
        each_peer(lambda k: to(k, gsend.at[b, k], gall.at[b, own64], send_s.at[4 + b], recv_s.at[4 + b]).start())
        gall[b, own64, :] = gsend[b, m]

    unrolled(2, owner_work)

    def backward(b):
        arrived(gall.at[b, pl.ds(0, 960)], recv_s.at[4 + b])
        q, k, v = (qall[b, :, t * HD : (t + 1) * HD] for t in range(3))

        def keys_back(i, totals):
            r = rows(i, 256)
            wide = jnp.where(seencol[b, r, :] > 0.0, 0.0, gall[b, r, 0:HD].astype(F32))
            g = wide.astype(BF16)
            delta = jnp.sum(wide * attp[b, r, 0:HD].astype(F32), axis=1, keepdims=True)
            p = ps[b, r, :]
            ds = (p * (nt(g, qall[b, :, 2 * HD : 3 * HD]) - delta)).astype(BF16)
            return (totals[0] + tn(ds, qt[r, :]), totals[1] + tn(p.astype(BF16), g))

        nil = jnp.zeros((256, HD), F32)
        dk, dv = lax.fori_loop(0, 4, keys_back, (nil, nil))

        both = nn(take[b], gall[b])
        gv = both[:, 0:HD]
        delta = jnp.sum(gv * av[b].astype(F32), axis=1, keepdims=True)
        gv = gv.astype(BF16)
        p2 = p2s[b]
        ds1 = (p1s[b] * (nt(gv, vt[...]) - delta)).astype(BF16)
        ds2 = (p2 * (nt(gv, v) - delta)).astype(BF16)
        dq = (nn(ds1, kt[...]) + nn(ds2, k)) * 0.125
        dk = dk + tn(ds2, q)
        dv = dv + tn(p2.astype(BF16), gv)
        dpack[b, :, 0:HD] = dq.astype(BF16)
        dpack[b, :, HD : 2 * HD] = dk.astype(BF16)
        dpack[b, :, 2 * HD : 3 * HD] = dv.astype(BF16)
        dpack[b, :, 3 * HD :] = both[:, HD:].astype(BF16)
        each_peer(lambda k: to(k, dpack.at[b, rows(k, 16)], dbuf.at[b, m], send_s.at[6 + b], recv_s.at[6 + b]).start())
        dbuf[b, m] = dpack[b, mine, :]

    unrolled(2, backward)

    def norm_back(b):
        arrived(dbuf.at[b, pl.ds(0, N - 1)], recv_s.at[6 + b])

        def unpack(i):
            one, two = dbuf[b, 2 * i], dbuf[b, 2 * i + 1]
            for t in range(4):
                cut = slice(t * HD, (t + 1) * HD)
                df[t, :, lanes(i, 128)] = jnp.concatenate([one[:, cut], two[:, cut]], axis=1)

        unrolled(N // 2, unpack)

        def back_project(i):
            r = rows(i, 256)
            cut = lanes(i, 256)
            sc[:, cut] = (nt(df[0], wq[r, :]) + nt(df[1], wk[r, :]) + nt(df[2], wv[r, :])) * gain_r[:, cut]

        unrolled(4, back_project)
        scaled = sc[...]
        std = stdo[rows(b, 16), :]
        back = df[3].astype(F32) + invo[rows(b, 16), :] * (
            scaled
            - jnp.mean(scaled, axis=-1, keepdims=True)
            - std * jnp.mean(scaled * std, axis=-1, keepdims=True)
        )
        for q in range(PIECES):
            ret[q, b, mine, :] = back[:, q * WIDE : (q + 1) * WIDE].astype(BF16)
        for block, sem in [(ret.at[:, 0, mine], (0, 0))] if b == 0 else [(ret.at[q, 1, mine], (q, 1)) for q in range(PIECES)]:
            each_peer(lambda k: to(k, block, block, ag2send.at[sem], ag2_s.at[sem]).start())

    unrolled(2, norm_back)

    def cross(src, dst, send, recv):
        return pltpu.make_async_remote_copy(
            src_ref=src, dst_ref=dst, send_sem=send, recv_sem=recv,
            device_id={"section": 1 - c}, device_id_type=MESH,
        )

    def z_copy(k, src, dst, send, recv):
        return pltpu.make_async_remote_copy(
            src_ref=src, dst_ref=dst, send_sem=send, recv_sem=recv,
            device_id={"dp": k}, device_id_type=MESH,
        )

    z_other = lax.rem(z + 1, NZ)
    firsts = [cross(loc.at[q, :, rows(1 - c, 192)], half_in.at[q], csend.at[q], crecv.at[q]) for q in range(PIECES)]
    arrived(ret.at[:, 0, pl.ds(0, 240)], ag2_s.at[0, 0])
    for q in range(PIECES):
        arrived(ret.at[q, 1, pl.ds(0, 240)], ag2_s.at[q, 1])

        def local_grad(t, q=q):
            both = nn(encT[...], ret[q, :, :, lanes(t, 256)].reshape(512, 256)).astype(BF16)
            loc[q, 2 * t] = both[:, :128]
            loc[q, 2 * t + 1] = both[:, 128:]

        unrolled(WIDE // 256, local_grad)
        firsts[q].start()

    for q in range(PIECES):
        firsts[q].wait_recv()

        def both_cores(d, q=q):
            t, deep = d % TILES, (d // TILES) * DEEP
            own_part = loc[q, t, pl.ds(pl.multiple_of(c * 192 + deep, DEEP), DEEP), :]
            their_part = half_in[q, t, deep : deep + DEEP, :]
            zin[q, d] = (own_part.astype(F32) + their_part.astype(F32)).astype(BF16)

        unrolled(NZ, both_cores)
        each_z(lambda k, q=q: z_copy(k, zin.at[q, k], zbuf.at[q, z], zsend.at[q], z1_s.at[q]).start())

    forward = lambda q, k: cross(zgat.at[q, k], zown.at[q, k], fsend.at[q, k], frecv.at[q, k])
    for q in range(PIECES):
        z_copy(z_other, zbuf.at[q, pl.ds(0, NZ - 1)], zbuf.at[q, pl.ds(0, NZ - 1)], zsend.at[q], z1_s.at[q]).wait_recv()
        zbuf[q, z] = zin[q, z]
        total = zbuf[q, 0].astype(F32)
        for k in range(1, NZ):
            total = total + zbuf[q, k].astype(F32)
        zgat[q, z] = total.astype(BF16)
        each_z(lambda k, q=q: z_copy(k, zgat.at[q, z], zgat.at[q, z], z2send.at[q], z2_s.at[q, z]).start())
        forward(q, z).start()

    def encoder_grad(b):
        total = nt(ret[0, b], we[:, 0:WIDE])
        for q in range(1, PIECES):
            total = total + nt(ret[q, b], we[:, q * WIDE : (q + 1) * WIDE])
        encg_o[rows(b, 256), :] = total.astype(BF16)

    unrolled(2, encoder_grad)

    def get_z(q, k):
        z_copy(k, zgat.at[q, k], zgat.at[q, k], z2send.at[q], z2_s.at[q, k]).wait_recv()
        forward(q, k).start()

    def write(q, core, block):
        for d in range(NZ):
            at = pl.ds(pl.multiple_of(core * 192 + (d // TILES) * DEEP, DEEP), DEEP)
            col = q * WIDE + (d % TILES) * 128
            emb_o[at, col : col + 128] = block[q, d]

    for q in range(PIECES):
        each_z(lambda k, q=q: get_z(q, k))
        write(q, c, zgat)
    for q in range(PIECES):
        for k in range(NZ):
            forward(q, k).wait_recv()
        write(q, 1 - c, zown)

    for half in range(2):
        left_here(rsbuf.at[half, pl.ds(0, 3)], one_s.at[half])
        left_here(rsbuf2.at[half, pl.ds(0, 3)], two_s.at[half])
    left_here(qsend.at[pl.ds(0, N - 1)], send_s.at[1])
    for b in range(2):
        left_here(attb.at[b, pl.ds(0, N - 1)], send_s.at[2 + b])
        left_here(gsend.at[b, pl.ds(0, N - 1)], send_s.at[4 + b])
        left_here(dbuf.at[b, pl.ds(0, N - 1)], send_s.at[6 + b])
    left_here(ret.at[:, 0, pl.ds(0, 240)], ag2send.at[0, 0])
    for q in range(PIECES):
        left_here(ret.at[q, 1, pl.ds(0, 240)], ag2send.at[q, 1])
    for q in range(PIECES):
        firsts[q].wait_send()
        seven = zbuf.at[q, pl.ds(0, NZ - 1)]
        z_copy(z_other, seven, seven, zsend.at[q], z1_s.at[q]).wait_send()
        z_copy(z_other, seven, seven, z2send.at[q], z1_s.at[q]).wait_send()
        for k in range(NZ):
            forward(q, k).wait_send()


def finish(pred_i, encg_i, emb_i, pred_o, encg_o, emb_o):
    pred_o[...] = pred_i[...]
    encg_o[...] = encg_i[...]
    emb_o[...] = emb_i[...].astype(F32) * 8192 ** (-0.5)


def body(
    encoded, visible, owner, embed_weight, mask_token, norm_gain,
    query_weight, key_weight, value_weight, out_weight, pixel_weight, targets,
):
    quarter = 256
    freqs = 10000.0 ** (-jnp.arange(quarter, dtype=F32) / quarter)
    angle = jnp.arange(GRID, dtype=F32)[:, None] * freqs[None, :]
    trig = jnp.concatenate([jnp.sin(angle), jnp.cos(angle)], axis=1)
    vm = pl.BlockSpec(memory_space=pltpu.VMEM)
    hbm = pl.BlockSpec(memory_space=pl.ANY)
    V = pltpu.VMEM
    dma = pltpu.SemaphoreType.DMA
    scratch = [
        V((512, 384), BF16), V((384, 1024), BF16),
        V((1024, 1024), BF16), V((1024, 1024), BF16), V((1024, 1024), BF16), V((1024, 1024), BF16),
        V((1024, 768), BF16), V((2, 64, 768), BF16),
        V((2, 2, 256, 512), BF16), V((2, 4, 2, 64, 512), BF16), V((2, 4, 2, 16, 512), BF16), V((2, 2, 64, 512), BF16), V((384, 512), BF16),
        V((OWN, 2 * N), F32), V((2, 1, 1024), F32), V((2, 1024, 1), F32),
        V((2, 1024, 256), BF16), V((2, 256, 1024), BF16), V((192, 1024), BF16), V((192, 256), BF16),
        V((OWN, 1024), F32), V((32, 1024), F32), V((32, 1024), F32), V((32, 1), F32), V((1024, 192), BF16),
        V((1024, HD), BF16), V((1024, HD), BF16), V((1024, HD), BF16),
        V((2, 1024, 1), F32), V((2, 1024, 1), F32), V((2, 1024, HD), F32),
        V((32, 1024), BF16), V((4, 32, 1024), BF16), V((N, 2, 16, 256), BF16), V((2, 256, 256), BF16), V((2, 256, HD), BF16), V((2, 256, 2 * HD), BF16),
        V((2, 256, 1024), F32), V((2, 256, 256), F32), V((2, 1024, 256), F32),
        V((2, 1024, 128), BF16), V((2, N, 64, 128), BF16), V((64, 1024), BF16), V((64, 1024), BF16),
        V((64, 1024), BF16), V((64, 768), BF16), V((64, 1024), BF16), V((64, 1024), BF16),
        V((2, N, 64, 128), BF16), V((2, 1024, 128), BF16), V((2, 256, 256), BF16), V((2, N, 16, 256), BF16),
        V((4, 16, 1024), BF16), V((16, 1024), F32), V((PIECES, 2, 256, WIDE), BF16),
        V((PIECES, TILES, 384, 128), BF16), V((PIECES, TILES, 192, 128), BF16),
        V((PIECES, NZ, DEEP, 128), BF16), V((PIECES, NZ, DEEP, 128), BF16),
        V((PIECES, NZ, DEEP, 128), BF16), V((PIECES, NZ, DEEP, 128), BF16),
        dma((8,)), dma((2,)), dma((2,)), dma((2,)), dma((2,)), dma((8,)), dma((8,)), dma((PIECES, 2)), dma((PIECES, 2)),
        dma((PIECES,)), dma((PIECES,)), dma((PIECES,)), dma((PIECES, NZ)),
        dma((PIECES,)), dma((PIECES,)), dma((PIECES, NZ)), dma((PIECES, NZ)),
    ]
    predicted, encoded_grad, summed = pl.pallas_call(
        kernel,
        out_shape=(
            jax.ShapeDtypeStruct((2, 64, 768), BF16),
            jax.ShapeDtypeStruct((512, 384), BF16),
            jax.ShapeDtypeStruct((384, 1024), BF16),
        ),
        in_specs=[hbm, hbm, vm, vm, vm, vm, hbm, hbm, hbm, hbm, hbm, hbm, vm],
        out_specs=(vm, vm, vm),
        scratch_shapes=scratch,
        compiler_params=pltpu.CompilerParams(
            collective_id=0, has_side_effects=True, vmem_limit_bytes=58 * 1024 * 1024
        ),
        cost_estimate=pl.CostEstimate(flops=8_000_000_000, bytes_accessed=16_000_000, transcendentals=4_000_000),
    )(
        encoded, embed_weight, owner.reshape(1, 1024), visible, mask_token.reshape(1, 1024), norm_gain.reshape(1, 1024),
        query_weight, key_weight, value_weight, out_weight, pixel_weight, targets, trig,
    )
    return pl.pallas_call(
        finish,
        out_shape=(
            jax.ShapeDtypeStruct((2, 64, 768), BF16),
            jax.ShapeDtypeStruct((512, 384), BF16),
            jax.ShapeDtypeStruct((384, 1024), F32),
        ),
        in_specs=[vm, vm, vm],
        out_specs=(vm, vm, vm),
        cost_estimate=pl.CostEstimate(flops=400_000, bytes_accessed=3_500_000, transcendentals=0),
    )(predicted, encoded_grad, summed)


def solution(mesh):
    placed = (
        P(("dp", "section"), "mp"),
        P(("dp", "section"), None),
        P(),
        P("mp", None),
        P(),
        P(),
        P(),
        P(),
        P(),
        P(),
        P(),
        P(("dp", "section"), "mp", None),
    )
    return jax.shard_map(
        body,
        mesh=mesh,
        in_specs=placed,
        out_specs=(P(("dp", "section"), "mp", None), P(("dp", "section"), "mp"), P("mp", None)),
        check_vma=False,
    )
```

```python
import functools

import jax
import jax.numpy as jnp
from jax import lax
from jax.experimental import pallas as pl
from jax.experimental.pallas import tpu as pltpu
from jax.sharding import PartitionSpec as P

MESH = pl.DeviceIdType.MESH
F32 = jnp.float32
BF16 = jnp.bfloat16
GRID = 32
N = 16
NZ = 8
HD = 64
OWN = 64
PIECES = 2
WIDE = 1024 // PIECES
TILES = WIDE // 128
DEEP = 192 * TILES // NZ


def nn(a, b):
    return lax.dot_general(a, b, (((1,), (0,)), ((), ())), preferred_element_type=F32)


def nt(a, b):
    return lax.dot_general(a, b, (((1,), (1,)), ((), ())), preferred_element_type=F32)


def tn(a, b):
    return lax.dot_general(a, b, (((0,), (0,)), ((), ())), preferred_element_type=F32)


def fiota(shape, dim):
    return lax.broadcasted_iota(jnp.int32, shape, dim).astype(F32)


def hot(cond):
    return jnp.where(cond, 1.0, 0.0).astype(BF16)


def norm(x):
    c = x - jnp.mean(x, axis=-1, keepdims=True)
    inv = lax.rsqrt(jnp.mean(c * c, axis=-1, keepdims=True) + 1e-06)
    return c * inv, inv


def lanes(i, size):
    if isinstance(i, int):
        return slice(i * size, (i + 1) * size)
    return pl.ds(pl.multiple_of(i * size, size), size)


def unrolled(n, f):
    for i in range(n):
        f(i)


def loop(n, f):
    def one(i, _):
        f(i)
        return 0

    lax.fori_loop(0, n, one, 0)


rows = lanes


def kernel(
    enc_h, we_h, own_r, vis_r, mask_r, gain_r, wq_h, wk_h, wv_h, wo_h, wp_h, tgt_h, sin_r, cos_r,
    pred_o, encg_o, emb_o,
    enc, we, wq, wk, wv, wo, wp, tgt,
    part, rsbuf, rsbuf2, line, encT,
    order, seenrow, seencol, put, take, ptab, ttab, pos, xown, stdo, invo, wh,
    qt, kt, vt, mt, lt, acc,
    normed, fs, qsend, qall, av, ave, p1s, p2s, ps,
    attp, attb, attf, ef, updb, resid, gub, gab, gsend, gall, dpack, dbuf, df, sc, ret,
    loc, half_in, zin, zbuf, zgat, zown,
    lsem, one_s, one_r, two_s, two_r, send_s, recv_s, ag1send, ag1_s, ag2send, ag2_s, zsend, z1_s, z2send, z2_s, csend, crecv, fsend, frecv,
):
    m = lax.axis_index("mp")
    z = lax.axis_index("dp")
    c = lax.axis_index("section")

    pairs = [(enc_h, enc), (we_h, we), (wq_h, wq), (wk_h, wk), (wv_h, wv), (wo_h, wo), (wp_h, wp), (tgt_h, tgt)]
    loads = [pltpu.make_async_copy(s, d, lsem.at[i]) for i, (s, d) in enumerate(pairs)]
    for load in loads:
        load.start()

    barrier = pltpu.get_barrier_semaphore()

    def each_peer(f):
        def one(j, _):
            f(lax.rem(m + j, N))
            return 0

        lax.fori_loop(1, N, one, 0)

    def each_z(f):
        def one(j, _):
            f(lax.rem(z + j, NZ))
            return 0

        lax.fori_loop(1, NZ, one, 0)

    each_peer(lambda k: pl.semaphore_signal(barrier, inc=1, device_id={"mp": k}, device_id_type=MESH))
    each_z(lambda k: pl.semaphore_signal(barrier, inc=1, device_id={"dp": k}, device_id_type=MESH))
    pl.semaphore_signal(barrier, inc=1, device_id={"section": 1 - c}, device_id_type=MESH)

    def to(k, src, dst, send, recv):
        return pltpu.make_async_remote_copy(
            src_ref=src, dst_ref=dst, send_sem=send, recv_sem=recv, device_id={"mp": k}, device_id_type=MESH
        )

    other = lax.rem(m + 1, N)

    def arrived(fifteen, sem):
        to(other, fifteen, fifteen, sem, sem).wait_recv()

    def left_here(fifteen, sem):
        to(other, fifteen, fifteen, sem, sem).wait_send()

    mine = rows(m, 16)
    own64 = rows(m, 64)

    loads[0].wait()
    loads[1].wait()

    mx, my = m // 4, lax.rem(m, 4)
    first_at, second_at = (mx, my), (my, mx)

    def device(half, along_first, along_second):
        return 4 * along_first + along_second if half == 0 else 4 * along_second + along_first

    def partial_block(g):
        both = jnp.concatenate(
            [enc[rows(g, 64), :], enc[pl.ds(pl.multiple_of(256 + g * 64, 64), 64), :]], axis=0
        )
        out = nn(both, we[...]).astype(BF16)
        for b in range(2):
            part[0, b, rows(g, 64), :] = out[b * 64 : (b + 1) * 64, 0:512]
            for y in range(4):
                at = pl.ds(pl.multiple_of(y * 64 + g * 16, 16), 16)
                part[1, b, at, :] = out[b * 64 + y * 16 : b * 64 + (y + 1) * 16, 512:1024]

    def send_first(half, to_line):
        to(
            device(half, to_line, second_at[half]), part.at[half, :, rows(to_line, 64)],
            rsbuf.at[half, first_at[half]], one_s.at[half], one_r.at[half],
        ).start()

    partial_block(lax.rem(mx + 1, 4))
    pl.semaphore_wait(barrier, N - 1 + NZ - 1 + 1)

    def send_group(jj, _):
        g = lax.rem(mx + jj, 4)
        send_first(0, g)
        partial_block(lax.rem(g + 1, 4))
        return 0

    lax.fori_loop(1, 4, send_group, 0)
    for j in range(1, 4):
        send_first(1, lax.rem(my + j, 4))
    my_group = mx

    owner_row = own_r[...].astype(F32)
    of_owner = jnp.where(owner_row == fiota((N, 1024), 0), 1.0, 0.0)
    before = hot(fiota((128, 128), 0) < fiota((128, 128), 1))
    carry = jnp.zeros((N, 1), F32)
    ranks = []
    for a in range(8):
        block = of_owner[:, a * 128 : (a + 1) * 128]
        prior = nn(block.astype(BF16), before) + carry
        carry = carry + jnp.sum(block, axis=1, keepdims=True)
        ranks.append(jnp.sum(prior * block, axis=0, keepdims=True))
    rank_row = jnp.concatenate(ranks, axis=1)
    patch_ids = lax.broadcasted_iota(jnp.int32, (N, 1024), 1)
    halves = jnp.concatenate(
        [of_owner * (patch_ids >> 5).astype(F32), of_owner * (patch_ids & 31).astype(F32)], axis=0
    ).astype(BF16)
    order[...] = nt(hot(rank_row == fiota((OWN, 1024), 0)), halves)

    def order_col(o):
        return jnp.sum(jnp.where(fiota((OWN, 2 * N), 1) == o, order[...], 0.0), axis=1, keepdims=True)

    lookup = jnp.concatenate(
        [owner_row[:, a * 128 : (a + 1) * 128] for a in range(8)] + [ranks[a] for a in range(8)], axis=0
    ).astype(BF16)
    eye = fiota((256, 256), 0) == fiota((256, 256), 1)
    lane = lax.broadcasted_iota(jnp.int32, (256, 128), 1)
    own_patch = []
    for b in range(2):
        vrow = vis_r[b : b + 1, :]
        found = nn(lookup, hot(lax.broadcasted_iota(jnp.int32, (128, 256), 0) == (vrow & 127)))
        part_of = lax.broadcasted_iota(jnp.int32, (8, 256), 0) == (vrow >> 7)
        vis_owner = jnp.sum(jnp.where(part_of, found[0:8], 0.0), axis=0, keepdims=True)
        vis_rank = jnp.sum(jnp.where(part_of, found[8:16], 0.0), axis=0, keepdims=True)
        by_rank = hot(vis_rank == fiota((OWN, 256), 0))
        for o in range(N):
            put[b, o * OWN : (o + 1) * OWN, :] = by_rank * hot(vis_owner == float(o))
        owner_col = jnp.sum(jnp.where(eye, vis_owner, 0.0), axis=1, keepdims=True)
        rank_col = jnp.sum(jnp.where(eye, vis_rank, 0.0), axis=1, keepdims=True)
        by_rank = hot(rank_col == (lane & 63).astype(F32))
        owner_lane = (lane >> 6).astype(F32)
        for t in range(8):
            take[b, :, t * 128 : (t + 1) * 128] = by_rank * hot(owner_col - 2.0 * t == owner_lane)
        seenrow[b] = nn(jnp.ones((N, 256), BF16), take[b])[0:1]
        seencol[b] = nn(put[b], jnp.ones((256, 128), BF16))[:, 0:1]
        mine_at = fiota((16, 256), 1) == fiota((16, 256), 0) + (m * 16).astype(F32)
        own_patch.append(jnp.sum(jnp.where(mine_at, vrow.astype(F32), 0.0), axis=1, keepdims=True))

    def terms(x):
        hi = x.astype(BF16)
        rest = x - hi.astype(F32)
        mid = rest.astype(BF16)
        return hi, mid, (rest - mid.astype(F32)).astype(BF16)

    trig = jnp.concatenate([sin_r[...], cos_r[...]], axis=1)
    ptab[...] = jnp.zeros_like(ptab)
    for i, term in enumerate(terms(trig)):
        ptab[32 * i : 32 * i + 32, 0:512] = term
        ptab[96 + 32 * i : 128 + 32 * i, 512:1024] = term

    def row_and_col(row, col):
        which = lax.broadcasted_iota(jnp.int32, (row.shape[0], 192), 1)
        return hot((which & 31).astype(F32) == jnp.where(which < 96, row, col))

    def positions(row, col):
        return nn(row_and_col(row, col), ptab[...])

    for i in (2, 3, 4):
        loads[i].wait()
    pair = lanes(m // 2, 128)
    odd = jnp.full((1024, HD), lax.rem(m, 2), jnp.int32) == 1
    for i, w in enumerate((wq, wk, wv)):
        two = w[:, pair].astype(F32)
        wh[:, i * HD : (i + 1) * HD] = jnp.where(odd, two[:, HD:], two[:, :HD]).astype(BF16)

    gain = gain_r[...]
    scale = jnp.array(0.125, BF16)

    def gained(x, gains, w):
        out = nn(jnp.concatenate(terms(x * gains), axis=0), w)
        n = x.shape[0]
        return out[0:n] + out[n : 2 * n] + out[2 * n : 3 * n]

    ones_gain = gained(jnp.ones((16, 1024), F32), gain, wh[...])[0:1]
    at_lane = lax.broadcasted_iota(jnp.int32, (GRID, 256), 1)
    for n, side in enumerate((1.0, -1.0)):
        cut = slice(512 * n, 512 * n + 512)
        x = trig + mask_r[:, cut]
        average = jnp.mean(x, axis=1, keepdims=True)
        spread = jnp.sum((x - average) * (x - average), axis=1, keepdims=True) * (1.0 / 1024)
        products = gained(x, gain[:, cut], wh[cut, :])
        full = jnp.concatenate([products, jnp.zeros((GRID, HD), F32)], axis=1)
        full = jnp.where(at_lane == 192, 0.5 * average, full)
        full = jnp.where(at_lane == 193, spread, full)
        full = jnp.where(at_lane == 194, (0.5 * side) * average, full)
        for i, term in enumerate(terms(full)):
            ttab[96 * n + 32 * i : 96 * n + 32 * i + 32, :] = term

    def masked(i):
        r = rows(i, 256)
        owners = [(4 * i + j).astype(F32) for j in range(4)]
        row = jnp.concatenate([order_col(o) for o in owners], axis=0)
        col = jnp.concatenate([order_col(o + N) for o in owners], axis=0)
        sums = nn(row_and_col(row, col), ttab[...])
        average, spread, apart = sums[:, 192:193], sums[:, 193:194], sums[:, 194:195]
        inv = lax.rsqrt(spread + apart * apart + 1e-06)
        three = ((sums[:, 0:192] - average * ones_gain) * inv).astype(BF16)
        qt[r, :] = three[:, 0:HD] * scale
        kt[r, :] = three[:, HD : 2 * HD]
        vt[r, :] = three[:, 2 * HD :]

    loop(4, masked)
    def table(i):
        r = rows(i, 256)
        s = nt(qt[r, :], kt[...])
        for b in range(2):
            held = jnp.where(seenrow[b] > 0.0, -jnp.inf, s)
            top = jnp.max(held, axis=1, keepdims=True)
            e = jnp.exp(held - top)
            mt[b, r, :] = top
            lt[b, r, :] = jnp.sum(e, axis=1, keepdims=True)
            acc[b, r, :] = nn(e.astype(BF16), vt[...])

    table(0)

    for half in range(2):
        here = first_at[half]
        arrived(rsbuf.at[half, pl.ds(0, 3)], one_r.at[half])
        rsbuf[half, here] = part[half, :, rows(here, 64), :]
        total = rsbuf[half, 0].astype(F32)
        for a in range(1, 4):
            total = total + rsbuf[half, a].astype(F32)
        line[half] = total.astype(BF16)
        for j in range(1, 4):
            there = lax.rem(second_at[half] + j, 4)
            to(
                device(half, here, there), line.at[half, :, rows(there, 16)],
                rsbuf2.at[half, second_at[half]], two_s.at[half], two_r.at[half],
            ).start()

    lax.fori_loop(1, 3, lambda i, _: (table(i), 0)[1], 0)
    ids = jnp.concatenate(own_patch, axis=0).astype(jnp.int32)
    xown[...] = positions((ids >> 5).astype(F32), (ids & 31).astype(F32))
    pos[...] = positions(order_col(m.astype(F32)), order_col((m + N).astype(F32)))
    encT[...] = jnp.transpose(enc[...])

    own_rows = []
    for half in range(2):
        here = second_at[half]
        arrived(rsbuf2.at[half, pl.ds(0, 3)], two_r.at[half])
        rsbuf2[half, here] = line[half, :, rows(here, 16), :]
        total = rsbuf2[half, 0].astype(F32)
        for a in range(1, 4):
            total = total + rsbuf2[half, a].astype(F32)
        own_rows.append(total.reshape(32, 512))
    own_rows = jnp.concatenate(own_rows, axis=1)
    std, inv = norm(own_rows + xown[...])
    stdo[...] = std
    invo[...] = inv
    normed[...] = (std * gain).astype(BF16)
    fs[3] = own_rows.astype(BF16)

    def project(i):
        cut = lanes(i, 256)
        fs[0, :, cut] = nn(normed[...], wq[:, cut]).astype(BF16) * scale
        fs[1, :, cut] = nn(normed[...], wk[:, cut]).astype(BF16)
        fs[2, :, cut] = nn(normed[...], wv[:, cut]).astype(BF16)

    unrolled(4, project)

    def pack_rows(i):
        for t in range(4):
            two = fs[t, :, lanes(i, 128)].reshape(2, 16, 128)
            qsend[2 * i, :, :, t * HD : (t + 1) * HD] = two[:, :, :HD]
            qsend[2 * i + 1, :, :, t * HD : (t + 1) * HD] = two[:, :, HD:]

    unrolled(N // 2, pack_rows)
    each_peer(lambda k: to(k, qsend.at[k], qall.at[:, mine], send_s.at[1], recv_s.at[1]).start())
    qall[:, mine, :] = qsend[m]

    table(3)

    arrived(qall.at[:, pl.ds(0, 240)], recv_s.at[1])


    def attention(b):
        q, k, v = (qall[b, :, t * HD : (t + 1) * HD] for t in range(3))
        s1 = jnp.where(seenrow[b] > 0.0, -jnp.inf, nt(q, kt[...]))
        s2 = nt(q, k)
        top = jnp.maximum(jnp.max(s1, axis=1, keepdims=True), jnp.max(s2, axis=1, keepdims=True))
        e1 = jnp.exp(s1 - top)
        e2 = jnp.exp(s2 - top)
        inv = 1.0 / (jnp.sum(e1, axis=1, keepdims=True) + jnp.sum(e2, axis=1, keepdims=True))
        p1 = e1 * inv
        p2 = e2 * inv
        p1s[b] = p1
        p2s[b] = p2
        a = (nn(p1.astype(BF16), vt[...]) + nn(p2.astype(BF16), v)).astype(BF16)
        av[b] = a
        ave[b, :, 0:HD] = a
        ave[b, :, HD:] = qall[b, :, 3 * HD :]

        def attend(jj, _):
            g = lax.rem(my_group + jj, 4)
            r = rows(g, 256)
            s = nt(qt[r, :], qall[b, :, HD : 2 * HD])
            old = mt[b, r, :]
            top = jnp.maximum(old, jnp.max(s, axis=1, keepdims=True))
            e = jnp.exp(s - top)
            alpha = jnp.exp(old - top)
            inv = 1.0 / (alpha * lt[b, r, :] + jnp.sum(e, axis=1, keepdims=True))
            p = e * inv
            ps[b, r, :] = p
            att = acc[b, r, :] * (alpha * inv) + nn(p.astype(BF16), qall[b, :, 2 * HD : 3 * HD])
            placed = nn(put[b, r, :], ave[b])
            att = jnp.where(seencol[b, r, :] > 0.0, placed[:, 0:HD], att)
            attp[b, r, 0:HD] = att.astype(BF16)
            attp[b, r, HD:] = placed[:, HD:].astype(BF16)

            def send(i, _):
                k = 4 * g + lax.rem(m + i, 4)
                to(k, attp.at[b, rows(k, 64)], attb.at[b, m], send_s.at[2 + b], recv_s.at[2 + b]).start()
                return 0

            lax.fori_loop(jnp.where(jj == 4, 1, 0), 4, send, 0)
            return 0

        lax.fori_loop(1, 5, attend, 0)
        attb[b, m] = attp[b, own64, :]

    unrolled(2, attention)

    for i in (5, 6, 7):
        loads[i].wait()

    def owner_work(b):
        arrived(attb.at[b, pl.ds(0, N - 1)], recv_s.at[2 + b])

        def unpack(i):
            one, two = attb[b, 2 * i], attb[b, 2 * i + 1]
            attf[:, lanes(i, 128)] = jnp.concatenate([one[:, :HD], two[:, :HD]], axis=1)
            ef[:, lanes(i, 128)] = jnp.concatenate([one[:, HD:], two[:, HD:]], axis=1)

        unrolled(N // 2, unpack)
        seen = seencol[b, own64, :] > 0.0

        def update(i):
            cut = lanes(i, 256)
            inputs = jnp.where(seen, ef[:, cut].astype(F32), mask_r[:, cut]) + pos[:, cut]
            updb[:, cut] = (inputs + nn(attf[...], wo[:, cut])).astype(BF16)

        unrolled(4, update)

        def predict(i):
            cut = lanes(i, 256)
            px = nn(updb[...], wp[:, cut])
            pred_o[b, :, cut] = px.astype(BF16)
            resid[:, cut] = jnp.where(seen, 0.0, px - tgt[b, :, cut].astype(F32)).astype(BF16)

        unrolled(3, predict)

        def grad_updated(i):
            gub[:, lanes(i, 256)] = nt(resid[...], wp[rows(i, 256), :]).astype(BF16)

        unrolled(4, grad_updated)

        def grad_attended(i):
            gab[:, lanes(i, 256)] = nt(gub[...], wo[rows(i, 256), :]).astype(BF16)

        unrolled(4, grad_attended)

        def pack(i):
            a, u = gab[:, lanes(i, 128)], gub[:, lanes(i, 128)]
            gsend[b, 2 * i] = jnp.concatenate([a[:, :HD], u[:, :HD]], axis=1)
            gsend[b, 2 * i + 1] = jnp.concatenate([a[:, HD:], u[:, HD:]], axis=1)

        unrolled(N // 2, pack)
        each_peer(lambda k: to(k, gsend.at[b, k], gall.at[b, own64], send_s.at[4 + b], recv_s.at[4 + b]).start())
        gall[b, own64, :] = gsend[b, m]

    unrolled(2, owner_work)

    def backward(b):
        arrived(gall.at[b, pl.ds(0, 960)], recv_s.at[4 + b])
        q, k, v = (qall[b, :, t * HD : (t + 1) * HD] for t in range(3))

        def keys_back(i, totals):
            r = rows(i, 256)
            wide = jnp.where(seencol[b, r, :] > 0.0, 0.0, gall[b, r, 0:HD].astype(F32))
            g = wide.astype(BF16)
            delta = jnp.sum(wide * attp[b, r, 0:HD].astype(F32), axis=1, keepdims=True)
            p = ps[b, r, :]
            ds = (p * (nt(g, qall[b, :, 2 * HD : 3 * HD]) - delta)).astype(BF16)
            return (totals[0] + tn(ds, qt[r, :]), totals[1] + tn(p.astype(BF16), g))

        nil = jnp.zeros((256, HD), F32)
        dk, dv = lax.fori_loop(0, 4, keys_back, (nil, nil))

        both = nn(take[b], gall[b])
        gv = both[:, 0:HD]
        delta = jnp.sum(gv * av[b].astype(F32), axis=1, keepdims=True)
        gv = gv.astype(BF16)
        p2 = p2s[b]
        ds1 = (p1s[b] * (nt(gv, vt[...]) - delta)).astype(BF16)
        ds2 = (p2 * (nt(gv, v) - delta)).astype(BF16)
        dq = (nn(ds1, kt[...]) + nn(ds2, k)) * 0.125
        dk = dk + tn(ds2, q)
        dv = dv + tn(p2.astype(BF16), gv)
        dpack[b, :, 0:HD] = dq.astype(BF16)
        dpack[b, :, HD : 2 * HD] = dk.astype(BF16)
        dpack[b, :, 2 * HD : 3 * HD] = dv.astype(BF16)
        dpack[b, :, 3 * HD :] = both[:, HD:].astype(BF16)
        each_peer(lambda k: to(k, dpack.at[b, rows(k, 16)], dbuf.at[b, m], send_s.at[6 + b], recv_s.at[6 + b]).start())
        dbuf[b, m] = dpack[b, mine, :]

    unrolled(2, backward)

    def norm_back(b):
        arrived(dbuf.at[b, pl.ds(0, N - 1)], recv_s.at[6 + b])
        if b == 1:
            pass_lines(0)

        def unpack(i):
            one, two = dbuf[b, 2 * i], dbuf[b, 2 * i + 1]
            for t in range(4):
                cut = slice(t * HD, (t + 1) * HD)
                df[t, :, lanes(i, 128)] = jnp.concatenate([one[:, cut], two[:, cut]], axis=1)

        unrolled(N // 2, unpack)

        def back_project(i):
            r = rows(i, 256)
            cut = lanes(i, 256)
            sc[:, cut] = (nt(df[0], wq[r, :]) + nt(df[1], wk[r, :]) + nt(df[2], wv[r, :])) * gain_r[:, cut]

        unrolled(4, back_project)
        scaled = sc[...]
        std = stdo[rows(b, 16), :]
        back = df[3].astype(F32) + invo[rows(b, 16), :] * (
            scaled
            - jnp.mean(scaled, axis=-1, keepdims=True)
            - std * jnp.mean(scaled * std, axis=-1, keepdims=True)
        )
        for q in range(PIECES):
            ret[q, b, mx, my] = back[:, q * WIDE : (q + 1) * WIDE].astype(BF16)
        for q in range(PIECES):
            block = ret.at[q, b, mx, my]
            for j in range(1, 4):
                there = lax.rem(first_at[q] + j, 4)
                to(device(q, there, second_at[q]), block, block, ag1send.at[q, b], ag1_s.at[q, b]).start()

    def pass_lines(b):
        for q in range(PIECES):
            arrived(ret.at[q, b, 0, pl.ds(0, 3)], ag1_s.at[q, b])
            line_of = ret.at[q, b, :, my] if q == 0 else ret.at[q, b, mx]
            for j in range(1, 4):
                there = lax.rem(second_at[q] + j, 4)
                to(device(q, first_at[q], there), line_of, line_of, ag2send.at[q, b], ag2_s.at[q, b]).start()

    unrolled(2, norm_back)
    pass_lines(1)

    def cross(src, dst, send, recv):
        return pltpu.make_async_remote_copy(
            src_ref=src, dst_ref=dst, send_sem=send, recv_sem=recv,
            device_id={"section": 1 - c}, device_id_type=MESH,
        )

    def z_copy(k, src, dst, send, recv):
        return pltpu.make_async_remote_copy(
            src_ref=src, dst_ref=dst, send_sem=send, recv_sem=recv,
            device_id={"dp": k}, device_id_type=MESH,
        )

    z_other = lax.rem(z + 1, NZ)
    firsts = [cross(loc.at[q, :, rows(1 - c, 192)], half_in.at[q], csend.at[q], crecv.at[q]) for q in range(PIECES)]
    for q in range(PIECES):
        for b in range(2):
            arrived(ret.at[q, b, pl.ds(0, 3)], ag2_s.at[q, b])

        def local_grad(t, q=q):
            both = nn(encT[...], ret[q, :, :, :, :, lanes(t, 256)].reshape(512, 256)).astype(BF16)
            loc[q, 2 * t] = both[:, :128]
            loc[q, 2 * t + 1] = both[:, 128:]

        unrolled(WIDE // 256, local_grad)
        firsts[q].start()

    for q in range(PIECES):
        firsts[q].wait_recv()

        def both_cores(d, q=q):
            t, deep = d % TILES, (d // TILES) * DEEP
            own_part = loc[q, t, pl.ds(pl.multiple_of(c * 192 + deep, DEEP), DEEP), :]
            their_part = half_in[q, t, deep : deep + DEEP, :]
            zin[q, d] = (own_part.astype(F32) + their_part.astype(F32)).astype(BF16)

        unrolled(NZ, both_cores)
        each_z(lambda k, q=q: z_copy(k, zin.at[q, k], zbuf.at[q, z], zsend.at[q], z1_s.at[q]).start())

    forward = lambda q, k: cross(zgat.at[q, k], zown.at[q, k], fsend.at[q, k], frecv.at[q, k])
    for q in range(PIECES):
        z_copy(z_other, zbuf.at[q, pl.ds(0, NZ - 1)], zbuf.at[q, pl.ds(0, NZ - 1)], zsend.at[q], z1_s.at[q]).wait_recv()
        zbuf[q, z] = zin[q, z]
        total = zbuf[q, 0].astype(F32)
        for k in range(1, NZ):
            total = total + zbuf[q, k].astype(F32)
        zgat[q, z] = total.astype(BF16)
        each_z(lambda k, q=q: z_copy(k, zgat.at[q, z], zgat.at[q, z], z2send.at[q], z2_s.at[q, z]).start())
        forward(q, z).start()

    def encoder_grad(b):
        total = nt(ret[0, b].reshape(256, WIDE), we[:, 0:WIDE])
        for q in range(1, PIECES):
            total = total + nt(ret[q, b].reshape(256, WIDE), we[:, q * WIDE : (q + 1) * WIDE])
        encg_o[rows(b, 256), :] = total.astype(BF16)

    unrolled(2, encoder_grad)

    def get_z(q, k):
        z_copy(k, zgat.at[q, k], zgat.at[q, k], z2send.at[q], z2_s.at[q, k]).wait_recv()
        forward(q, k).start()

    def write(q, core, block):
        for d in range(NZ):
            at = pl.ds(pl.multiple_of(core * 192 + (d // TILES) * DEEP, DEEP), DEEP)
            col = q * WIDE + (d % TILES) * 128
            emb_o[at, col : col + 128] = block[q, d]

    for q in range(PIECES):
        each_z(lambda k, q=q: get_z(q, k))
        write(q, c, zgat)
    for q in range(PIECES):
        for k in range(NZ):
            forward(q, k).wait_recv()
        write(q, 1 - c, zown)

    for half in range(2):
        left_here(rsbuf.at[half, pl.ds(0, 3)], one_s.at[half])
        left_here(rsbuf2.at[half, pl.ds(0, 3)], two_s.at[half])
    left_here(qsend.at[pl.ds(0, N - 1)], send_s.at[1])
    for b in range(2):
        left_here(attb.at[b, pl.ds(0, N - 1)], send_s.at[2 + b])
        left_here(gsend.at[b, pl.ds(0, N - 1)], send_s.at[4 + b])
        left_here(dbuf.at[b, pl.ds(0, N - 1)], send_s.at[6 + b])
    for q in range(PIECES):
        for b in range(2):
            left_here(ret.at[q, b, 0, pl.ds(0, 3)], ag1send.at[q, b])
            left_here(ret.at[q, b, pl.ds(0, 3)], ag2send.at[q, b])
    for q in range(PIECES):
        firsts[q].wait_send()
        seven = zbuf.at[q, pl.ds(0, NZ - 1)]
        z_copy(z_other, seven, seven, zsend.at[q], z1_s.at[q]).wait_send()
        z_copy(z_other, seven, seven, z2send.at[q], z1_s.at[q]).wait_send()
        for k in range(NZ):
            forward(q, k).wait_send()


def finish(pred_i, encg_i, emb_i, pred_o, encg_o, emb_o):
    pred_o[...] = pred_i[...]
    encg_o[...] = encg_i[...]
    emb_o[...] = emb_i[...].astype(F32) * 8192 ** (-0.5)


def body(
    encoded, visible, owner, embed_weight, mask_token, norm_gain,
    query_weight, key_weight, value_weight, out_weight, pixel_weight, targets,
):
    quarter = 256
    freqs = 10000.0 ** (-jnp.arange(quarter, dtype=F32) / quarter)
    angle = jnp.arange(GRID, dtype=F32)[:, None] * freqs[None, :]
    vm = pl.BlockSpec(memory_space=pltpu.VMEM)
    hbm = pl.BlockSpec(memory_space=pl.ANY)
    V = pltpu.VMEM
    dma = pltpu.SemaphoreType.DMA
    scratch = [
        V((512, 384), BF16), V((384, 1024), BF16),
        V((1024, 1024), BF16), V((1024, 1024), BF16), V((1024, 1024), BF16), V((1024, 1024), BF16),
        V((1024, 768), BF16), V((2, 64, 768), BF16),
        V((2, 2, 256, 512), BF16), V((2, 4, 2, 64, 512), BF16), V((2, 4, 2, 16, 512), BF16), V((2, 2, 64, 512), BF16), V((384, 512), BF16),
        V((OWN, 2 * N), F32), V((2, 1, 1024), F32), V((2, 1024, 1), F32),
        V((2, 1024, 256), BF16), V((2, 256, 1024), BF16), V((192, 1024), BF16), V((192, 256), BF16),
        V((OWN, 1024), F32), V((32, 1024), F32), V((32, 1024), F32), V((32, 1), F32), V((1024, 192), BF16),
        V((1024, HD), BF16), V((1024, HD), BF16), V((1024, HD), BF16),
        V((2, 1024, 1), F32), V((2, 1024, 1), F32), V((2, 1024, HD), F32),
        V((32, 1024), BF16), V((4, 32, 1024), BF16), V((N, 2, 16, 256), BF16), V((2, 256, 256), BF16), V((2, 256, HD), BF16), V((2, 256, 2 * HD), BF16),
        V((2, 256, 1024), F32), V((2, 256, 256), F32), V((2, 1024, 256), F32),
        V((2, 1024, 128), BF16), V((2, N, 64, 128), BF16), V((64, 1024), BF16), V((64, 1024), BF16),
        V((64, 1024), BF16), V((64, 768), BF16), V((64, 1024), BF16), V((64, 1024), BF16),
        V((2, N, 64, 128), BF16), V((2, 1024, 128), BF16), V((2, 256, 256), BF16), V((2, N, 16, 256), BF16),
        V((4, 16, 1024), BF16), V((16, 1024), F32), V((PIECES, 2, 4, 4, 16, WIDE), BF16),
        V((PIECES, TILES, 384, 128), BF16), V((PIECES, TILES, 192, 128), BF16),
        V((PIECES, NZ, DEEP, 128), BF16), V((PIECES, NZ, DEEP, 128), BF16),
        V((PIECES, NZ, DEEP, 128), BF16), V((PIECES, NZ, DEEP, 128), BF16),
        dma((8,)), dma((2,)), dma((2,)), dma((2,)), dma((2,)), dma((8,)), dma((8,)), dma((PIECES, 2)), dma((PIECES, 2)), dma((PIECES, 2)), dma((PIECES, 2)),
        dma((PIECES,)), dma((PIECES,)), dma((PIECES,)), dma((PIECES, NZ)),
        dma((PIECES,)), dma((PIECES,)), dma((PIECES, NZ)), dma((PIECES, NZ)),
    ]
    predicted, encoded_grad, summed = pl.pallas_call(
        kernel,
        out_shape=(
            jax.ShapeDtypeStruct((2, 64, 768), BF16),
            jax.ShapeDtypeStruct((512, 384), BF16),
            jax.ShapeDtypeStruct((384, 1024), BF16),
        ),
        in_specs=[hbm, hbm, vm, vm, vm, vm, hbm, hbm, hbm, hbm, hbm, hbm, vm, vm],
        out_specs=(vm, vm, vm),
        scratch_shapes=scratch,
        compiler_params=pltpu.CompilerParams(
            collective_id=0, has_side_effects=True, vmem_limit_bytes=58 * 1024 * 1024
        ),
        cost_estimate=pl.CostEstimate(flops=8_000_000_000, bytes_accessed=16_000_000, transcendentals=4_000_000),
    )(
        encoded, embed_weight, owner.reshape(1, 1024), visible, mask_token.reshape(1, 1024), norm_gain.reshape(1, 1024),
        query_weight, key_weight, value_weight, out_weight, pixel_weight, targets, jnp.sin(angle), jnp.cos(angle),
    )
    return pl.pallas_call(
        finish,
        out_shape=(
            jax.ShapeDtypeStruct((2, 64, 768), BF16),
            jax.ShapeDtypeStruct((512, 384), BF16),
            jax.ShapeDtypeStruct((384, 1024), F32),
        ),
        in_specs=[vm, vm, vm],
        out_specs=(vm, vm, vm),
        cost_estimate=pl.CostEstimate(flops=400_000, bytes_accessed=3_500_000, transcendentals=0),
    )(predicted, encoded_grad, summed)


def solution(mesh):
    placed = (
        P(("dp", "section"), "mp"),
        P(("dp", "section"), None),
        P(),
        P("mp", None),
        P(),
        P(),
        P(),
        P(),
        P(),
        P(),
        P(),
        P(("dp", "section"), "mp", None),
    )
    return jax.shard_map(
        body,
        mesh=mesh,
        in_specs=placed,
        out_specs=(P(("dp", "section"), "mp", None), P(("dp", "section"), "mp"), P("mp", None)),
        check_vma=False,
    )
```
